32 devices in a mesh: section: 2 (over core), dp: 4 (over z), mp: 4 (over y, x).
Axes of the slice: x: 2, y: 2, z: 4, core: 2. Of those that a mesh axis runs over, the one named last changes fastest.
Arguments:
- tokens: bfloat16 [512, 12288], P('mp', 'dp'), may hold values from -600 to 600
- weights: bfloat16 [2, 12288, 24576], P('section', 'dp', 'mp'), may hold values from -0.078125 to 0.078125
- gain: float32 [12288], P('dp'), may hold values from 0.1 to 1.9
- cotangent: bfloat16 [512, 12288], P('mp', 'dp'), may hold values from -6 to 6
Outputs:
- section_results: bfloat16 [2, 512, 12288], P('section', 'mp', 'dp')
- weight_grads: bfloat16 [2, 12288, 24576], P('section', 'dp', 'mp')
The draws below stay inside these ranges and needn't reach their ends.
All inputs are finite; a program needn't handle non-finite values.
Results may differ from the reference program's by a relative error of at most 0.035.
Values may be sent and summed in bfloat16 or wider, within the bound.
No kernel may reach another device: no remote copies, remote signals or barrier semaphores. Data moves between devices by JAX's collectives and lax.ppermute only.
A program may use at most 192 MiB of HBM per device.

```python
import math
import jax
import jax.numpy as jnp
from jax import lax

D = 12288
F = 24576
TOKENS = 512
N_DP = 4
N_MP = 4


def draw_tokens(key, part):
    key = jax.random.fold_in(key, 11)
    keys = jax.random.split(key, 3)
    base = jnp.clip(jax.random.normal(keys[0], (TOKENS, D), jnp.float32), -6.0, 6.0)
    row_scale = jnp.exp(jax.random.uniform(keys[1], (TOKENS, 1), jnp.float32) * math.log(10.0))
    ramp = jnp.exp(math.log(3.0) * jnp.arange(D, dtype=jnp.float32) / D)
    col_scale = ramp[None, :] * jnp.exp(jax.random.uniform(keys[2], (1, D), jnp.float32) * math.log(3.3))
    return (base * row_scale * col_scale).astype(jnp.bfloat16)


def raised(array, rng, source, target, blocks, factor):
    def block_of(position):
        return (jnp.arange(array.shape[position]) // (array.shape[position] // blocks)).reshape((-1,) + (1,) * (array.ndim - 1 - position))

    near = jax.random.permutation(rng, blocks)[block_of(target)]
    second = (block_of(target) + blocks // 2) % blocks
    return jnp.where((block_of(source) == near) | (block_of(source) == second), factor * array, array)


def block_scale(key, extent, cuts, smallest, top_value):
    factor_of, own = 1.0, jax.random.fold_in(key, 6)
    for dim, blocks in cuts:
        heights = jnp.exp(jax.random.uniform(jax.random.fold_in(own, dim), (blocks,), jnp.float32, smallest / len(cuts), top_value / len(cuts)))
        factor_of = factor_of * jnp.repeat(heights, extent[dim] // blocks).reshape([-1 if axis == dim else 1 for axis in range(len(extent))])
    return factor_of


def bell_draw(own_key, shape, deviation, bound, pieces=(), held_as=jnp.bfloat16):
    level = block_scale(own_key, shape, pieces, -0.22, 0.18) if pieces else 1.0
    values = jax.random.normal(own_key, shape, jnp.float32) * deviation * level
    return jnp.minimum(jnp.maximum(values, -bound), bound).astype(held_as)


def noise_with(rng, extent, spread, reach, cuts, heavy, kind=jnp.bfloat16):
    entries = spread * jax.random.normal(rng, extent, jnp.float32)
    if cuts:
        entries = entries * block_scale(rng, extent, cuts, -0.22, 0.18)
    return jnp.clip(raised(entries, jax.random.fold_in(rng, 3), *heavy), -reach, reach).astype(kind)


def setup_inputs(seed: int = 0) -> dict:
    key_list = jax.random.split(jax.random.key(seed), 5)
    tokens = draw_tokens(jax.random.fold_in(key_list[4], 71), 0)
    weights = noise_with(key_list[1], (2, D, F), D ** -0.5, 0.078125, ((0, 2), (1, 4), (2, 4)), (2, 1, 4, 2.0))
    gain = jnp.clip(1.0 + 0.18 * jax.random.normal(key_list[2], (D,), jnp.float32), 0.1, 1.9)
    cotangent = bell_draw(key_list[3], (TOKENS, D), 1.0, 6.0, ((0, 4), (1, 4)))
    return {"tokens": tokens, "weights": weights, "gain": gain, "cotangent": cotangent}


epsilon = 1e-05

def gelu_tanh(inputs):
    return jax.nn.gelu(inputs, approximate=True)

def gelu_back(preact, grad_hidden):
    return jax.vjp(gelu_tanh, preact)[1](grad_hidden.astype(jnp.float32))[0]

def block_sum(left, right, blocks):
    block_width = left.shape[1] // blocks

    def add_block(accumulated, block_index):
        offset = block_index * block_width
        left_block = lax.dynamic_slice_in_dim(left, offset, block_width, 1)
        right_block = lax.dynamic_slice_in_dim(right, offset, block_width, 0)
        product = jnp.dot(left_block, right_block, preferred_element_type=jnp.float32)
        rounded = lax.optimization_barrier(product.astype(jnp.bfloat16))
        return (accumulated + rounded.astype(jnp.float32), None)
    initial = jnp.zeros((left.shape[0], right.shape[1]), jnp.float32)
    result, unused = lax.scan(add_block, initial, jnp.arange(blocks, dtype=jnp.int32))
    return result

def reference(tokens, weights, gain, cotangent):
    values = tokens.astype(jnp.float32)
    average = lax.optimization_barrier(jnp.sum(values, 1)) / D
    squares = lax.optimization_barrier(jnp.sum(values * values, 1)) / D
    inverse_std = lax.rsqrt(squares - average * average + epsilon)
    centred = (values - average[:, None]) * inverse_std[:, None]
    normed = (centred * gain).astype(jnp.bfloat16)
    up_weight = weights[0]
    down_weight = weights[1]
    preact = block_sum(normed, up_weight, N_DP)
    hidden = gelu_tanh(preact).astype(jnp.bfloat16)
    output = block_sum(hidden, down_weight.T, N_MP).astype(jnp.bfloat16)
    grad_down = jnp.dot(cotangent.T, hidden, preferred_element_type=jnp.float32).astype(jnp.bfloat16)
    grad_hidden = block_sum(cotangent, down_weight, N_DP).astype(jnp.bfloat16)
    grad_preact = gelu_back(preact, grad_hidden).astype(jnp.bfloat16)
    grad_up = jnp.dot(normed.T, grad_preact, preferred_element_type=jnp.float32).astype(jnp.bfloat16)
    grad_normed = block_sum(grad_preact, up_weight.T, N_MP).astype(jnp.bfloat16)
    return (jnp.stack([grad_normed, output]), jnp.stack([grad_up, grad_down]))
```

```python
import jax
import jax.numpy as jnp
from jax import lax
from jax.sharding import PartitionSpec as P

D = 12288


epsilon = 1e-05


def gelu_tanh(inputs):
    return jax.nn.gelu(inputs, approximate=True)


def gelu_back(preact, grad_hidden):
    return jax.vjp(gelu_tanh, preact)[1](grad_hidden.astype(jnp.float32))[0]


def dot_f32(left, right, dims):
    return lax.dot_general(left, right, (dims, ((), ())), preferred_element_type=jnp.float32)


def from_peer(value, by):
    peers = lax.axis_size("mp")
    return lax.ppermute(value, "mp", [(i, i ^ by) for i in range(peers)])


def across_sections(value):
    return lax.ppermute(value, "section", [(0, 1), (1, 0)])


def add_bf16(left, right):
    return (left.astype(jnp.float32) + right.astype(jnp.float32)).astype(jnp.bfloat16)


def line_sum(part, activate):
    peers = lax.axis_size("dp")
    half = peers // 2
    index = lax.axis_index("dp")
    for hop in range(half - 1):
        arrived = lax.ppermute(part, "dp", [(hop, hop + 1), (peers - 1 - hop, peers - 2 - hop)])
        part = add_bf16(part, arrived)
    arrived = lax.ppermute(part, "dp", [(half - 1, half), (half, half - 1)])
    result = activate(add_bf16(part, arrived))
    for hop in reversed(range(half - 1)):
        arrived = lax.ppermute(result, "dp", [(hop + 1, hop), (peers - 2 - hop, peers - 1 - hop)])
        receives = jnp.logical_or(index == hop, index == peers - 1 - hop)
        result = jnp.where(receives, arrived, result)
    return result


def local(tokens, weights, gain, cotangent):
    first = lax.axis_index("section") == 0
    weight = weights[0]
    peers = lax.axis_size("mp")
    rows = tokens.shape[0]
    hidden_local = weight.shape[1]

    raw = jnp.where(first, tokens, cotangent)
    gathered = [raw] + [from_peer(raw, by) for by in range(1, peers)]

    values = tokens.astype(jnp.float32)
    sums = lax.psum(jnp.stack([jnp.sum(values, 1), jnp.sum(values * values, 1)]), "dp")
    average = sums[0] / D
    inverse_std = lax.rsqrt(sums[1] / D - average * average + epsilon)
    stats = jnp.stack([average, inverse_std])

    def prepared(block, scale):
        centred = (block.astype(jnp.float32) - scale[0][:, None]) * scale[1][:, None]
        return jnp.where(first, (centred * gain).astype(jnp.bfloat16), block)

    own = prepared(raw, stats)
    others = jnp.concatenate(
        [prepared(gathered[by], from_peer(stats, by)) for by in range(1, peers)], 0
    )

    def activate(total):
        other = across_sections(total)
        preact = jnp.where(first, total, other).astype(jnp.float32)
        grad_hidden = jnp.where(first, other, total)
        return jnp.where(first, gelu_back(preact, grad_hidden), gelu_tanh(preact)).astype(
            jnp.bfloat16
        )

    def chunk(block, start, stop):
        part = dot_f32(block, weight[:, start:stop], ((1,), (0,))).astype(jnp.bfloat16)
        return line_sum(part, activate)

    unit = hidden_local // 6
    own_hidden = [chunk(own, 0, 2 * unit)]
    others_hidden = [chunk(others, i * unit, (i + 1) * unit) for i in range(6)]
    own_hidden += [chunk(own, 2 * unit, 4 * unit)]
    own_hidden += [chunk(own, i * unit, (i + 1) * unit) for i in (4, 5)]
    others_hidden = jnp.concatenate(others_hidden, 1)
    own_hidden = jnp.concatenate(own_hidden, 1)

    partial = dot_f32(others_hidden, weight, ((1,), (1,))).astype(jnp.bfloat16)
    arrived = [
        from_peer(partial[(by - 1) * rows : by * rows], by) for by in range(1, peers)
    ]
    result = dot_f32(own_hidden, weight, ((1,), (1,))).astype(jnp.bfloat16).astype(jnp.float32)
    for block in arrived:
        result = result + block.astype(jnp.float32)
    section_results = result.astype(jnp.bfloat16)[None]

    weight_grads = dot_f32(
        jnp.concatenate([own, others], 0),
        jnp.concatenate([own_hidden, others_hidden], 0),
        ((0,), (0,)),
    ).astype(jnp.bfloat16)[None]
    return (section_results, weight_grads)


def solution(mesh):
    placed = (P("mp", "dp"), P("section", "dp", "mp"), P("dp"), P("mp", "dp"))
    return jax.shard_map(
        local,
        mesh=mesh,
        in_specs=placed,
        out_specs=(P("section", "mp", "dp"), P("section", "dp", "mp")),
        check_vma=False,
    )
```

```python
import jax
import jax.numpy as jnp
from jax import lax
from jax.experimental import pallas as pl
from jax.experimental.pallas import tpu as pltpu
from jax.sharding import PartitionSpec as P

D = 12288
GROUPS = 4
PARTS = 2
COLUMN_TILE = 512
WIDTH_TILE = 256
VMEM = 40 * 1024 * 1024


epsilon = 1e-05


def gelu_tanh(inputs):
    return jax.nn.gelu(inputs, approximate=True)


def gelu_back(preact, grad_hidden):
    return jax.vjp(gelu_tanh, preact)[1](grad_hidden.astype(jnp.float32))[0]


def dot_f32(left, right, contract):
    return lax.dot_general(
        left, right, ((contract[:1], contract[1:]), ((), ())), preferred_element_type=jnp.float32
    )


def params():
    return pltpu.CompilerParams(dimension_semantics=("arbitrary",), vmem_limit_bytes=VMEM)


def up_product(section, rows, weight, part, pieces):
    count, width = rows.shape
    columns = weight.shape[1] // PARTS
    tile = min(COLUMN_TILE, columns // 2)
    steps = columns // tile
    mine = steps // 2
    piece = count // pieces

    def kernel(section_ref, rows_ref, weight_ref, *results):
        product = dot_f32(rows_ref[...], weight_ref[...], (1, 0)).astype(jnp.bfloat16)

        def store(refs):
            for i, result in enumerate(refs):
                result[...] = product[i * piece : (i + 1) * piece]

        pl.when(pl.program_id(0) < mine)(lambda: store(results[:pieces]))
        pl.when(pl.program_id(0) >= mine)(lambda: store(results[pieces:]))

    def column(i, section_ref):
        return (0, part * steps + lax.rem(i + section_ref[0] * mine, steps))

    results = pl.pallas_call(
        kernel,
        grid_spec=pltpu.PrefetchScalarGridSpec(
            num_scalar_prefetch=1,
            grid=(steps,),
            in_specs=[
                pl.BlockSpec((count, width), lambda i, section_ref: (0, 0)),
                pl.BlockSpec((width, tile), column),
            ],
            out_specs=[pl.BlockSpec((piece, tile), lambda i, section_ref: (0, jnp.minimum(i, mine - 1)))]
            * pieces
            + [pl.BlockSpec((piece, tile), lambda i, section_ref: (0, jnp.maximum(i - mine, 0)))] * pieces,
        ),
        out_shape=[jax.ShapeDtypeStruct((piece, columns // 2), jnp.bfloat16)] * (2 * pieces),
        compiler_params=params(),
        name="up_product",
    )(section, rows, weight)
    return tuple(results)


def down_product(hidden, weight, part, before, kept):
    count, columns = hidden.shape
    width = weight.shape[0]
    tile = min(WIDTH_TILE, width)

    def kernel(hidden_ref, weight_ref, *refs):
        product = dot_f32(hidden_ref[...], weight_ref[...], (1, 1))
        if before is not None:
            product = product + refs[0][...]
        refs[-1][...] = product.astype(kept)

    rows_of = pl.BlockSpec((count, tile), lambda i: (0, i))
    added = [] if before is None else [before]
    return pl.pallas_call(
        kernel,
        grid=(width // tile,),
        in_specs=[
            pl.BlockSpec((count, columns), lambda i: (0, 0)),
            pl.BlockSpec((tile, columns), lambda i: (i, part)),
        ]
        + [rows_of] * len(added),
        out_specs=rows_of,
        out_shape=jax.ShapeDtypeStruct((count, width), kept),
        compiler_params=params(),
        name="down_product",
    )(hidden, weight, *added)


def weight_gradient(turned, hidden, part, into):
    width, count = turned.shape
    columns = hidden.shape[1]
    tile = min(WIDTH_TILE, width)

    def kernel(turned_ref, hidden_ref, *refs):
        refs[-1][...] = dot_f32(turned_ref[...], hidden_ref[...], (1, 0)).astype(jnp.bfloat16)

    held = [] if into is None else [into]
    return pl.pallas_call(
        kernel,
        grid=(width // tile,),
        in_specs=[
            pl.BlockSpec((tile, count), lambda i: (i, 0)),
            pl.BlockSpec((count, columns), lambda i: (0, 0)),
        ]
        + [pl.BlockSpec(memory_space=pl.ANY)] * len(held),
        out_specs=pl.BlockSpec((tile, columns), lambda i: (i, part)),
        out_shape=jax.ShapeDtypeStruct((width, columns * PARTS), jnp.bfloat16),
        input_output_aliases={2: 0} if held else {},
        compiler_params=params(),
        name="weight_gradient",
    )(turned, hidden, *held)


def from_peer(value, by):
    peers = lax.axis_size("mp")
    return lax.ppermute(value, "mp", [(i, i ^ by) for i in range(peers)])


def across_sections(value):
    return lax.ppermute(value, "section", [(0, 1), (1, 0)])


def add_bf16(left, right):
    return (left.astype(jnp.float32) + right.astype(jnp.float32)).astype(jnp.bfloat16)


def local(tokens, weights, gain, cotangent):
    first = lax.axis_index("section") == 0
    weight = weights[0]
    peers = lax.axis_size("mp")
    line = lax.axis_size("dp")
    half = line // 2
    place = lax.axis_index("dp")
    rows = tokens.shape[0]
    each = peers // GROUPS
    group_rows = each * rows

    last = []

    def run(work, anchor, *others):
        if last:
            held = last[-1]
            anchor, held["value"] = lax.optimization_barrier((anchor, held["value"]))
        held = {"value": work(anchor, *others)}
        last.append(held)
        return held

    raw = run(lambda a, b: jnp.where(first, a, b), tokens, cotangent)
    values = {0: raw}

    def row_sums(block):
        value = block.astype(jnp.float32)
        return jnp.stack([jnp.sum(value, 1), jnp.sum(value * value, 1)])

    sums = run(row_sums, tokens)
    arrived_raw = {by: from_peer(raw["value"], by) for by in range(1, peers)}
    total = sums["value"]
    by = 1
    while by < line:
        total = total + lax.ppermute(total, "dp", [(i, i ^ by) for i in range(line)])
        by *= 2

    def scale_of(total):
        average = total[0] / D
        return jnp.stack([average, lax.rsqrt(total[1] / D - average * average + epsilon)])

    scale = scale_of(total)
    arrived_scale = {by: from_peer(scale, by) for by in range(1, peers)}

    def prepared(gain, blocks, scales):
        def one(block, scale):
            centred = (block.astype(jnp.float32) - scale[0][:, None]) * scale[1][:, None]
            return jnp.where(first, (centred * gain).astype(jnp.bfloat16), block)

        return jnp.concatenate([one(b, s) for b, s in zip(blocks, scales)], 0)

    def prepare(group):
        members = range(group * each, (group + 1) * each)
        blocks = [arrived_raw[by] if by else raw["value"] for by in members]
        scales = [arrived_scale[by] if by else scale for by in members]
        return run(prepared, gain, blocks, scales)

    section = lax.axis_index("section").astype(jnp.int32).reshape(1)
    chunks = {}

    def multiply(rows_of, part, groups):
        pieces = len(groups)
        products = run(lambda r: up_product(section, r, weight, part, pieces), rows_of["value"])
        for i, group in enumerate(groups):
            chunks[part, group] = {"mine": (products, i), "theirs": (products, pieces + i)}

    def stack(chunk):
        held, at = chunk["mine"]
        other, other_at = chunk["theirs"]
        arrived = across_sections(other["value"][other_at])
        chunk["sum"] = run(lambda a, b: jnp.concatenate([a, b], 0), held["value"][at], arrived)

    def inward(chunk):
        for hop in range(half - 1):
            value = chunk["sum"]["value"]
            arrived = lax.ppermute(value, "dp", [(hop, hop + 1), (line - 1 - hop, line - 2 - hop)])
            chunk["sum"] = run(add_bf16, value, arrived)

    def activate(value, arrived):
        total = add_bf16(value, arrived)
        above, below = total[:group_rows], total[group_rows:]
        preact = jnp.where(first, above, below).astype(jnp.float32)
        grad_hidden = jnp.where(first, below, above)
        hidden = gelu_tanh(preact).astype(jnp.bfloat16)
        grad_preact = gelu_back(preact, grad_hidden).astype(jnp.bfloat16)
        return jnp.concatenate(
            [jnp.where(first, grad_preact, hidden), jnp.where(first, hidden, grad_preact)], 0
        )

    def middle(chunk):
        value = chunk["sum"]["value"]
        arrived = lax.ppermute(value, "dp", [(half - 1, half), (half, half - 1)])
        chunk["result"] = run(activate, value, arrived)

    def outward(chunk):
        for hop in reversed(range(half - 1)):
            value = chunk["result"]["value"]
            arrived = lax.ppermute(value, "dp", [(hop + 1, hop), (line - 2 - hop, line - 1 - hop)])
            receiving = jnp.logical_or(place == hop, place == line - 1 - hop)
            if hop:
                chunk["result"] = run(lambda a, b: jnp.where(receiving, b, a), value, arrived)

        def split(value, arrived):
            value = jnp.where(receiving, arrived, value)
            return value[:group_rows], value[group_rows:]

        chunk["halves"] = run(split, value, arrived)

    def joined(part, groups):
        kept = [chunks[part, g]["halves"]["value"][0] for g in groups]
        came = [across_sections(chunks[part, g]["halves"]["value"][1]) for g in groups]

        def join(anchor, rest, came):
            blocks = [
                jnp.concatenate([jnp.where(first, k, c), jnp.where(first, c, k)], 1)
                for k, c in zip([anchor] + rest, came)
            ]
            return jnp.concatenate(blocks, 0)

        return run(join, kept[0], kept[1:], came)

    def both(left, right):
        return run(lambda a, b: jnp.concatenate([a, b], 0), left["value"], right["value"])

    order = [(part, g) for part in range(PARTS - 1) for g in range(GROUPS)]
    order += [(PARTS - 1, g) for g in (1, 2, 3, 0)]

    def chunk_at(t):
        return chunks[order[t]]

    def tick(t):
        if 0 <= t < len(order):
            inward(chunk_at(t))
        if 0 <= t - 1 < len(order):
            middle(chunk_at(t - 1))
        if 0 <= t - 2 < len(order):
            outward(chunk_at(t - 2))
        if 0 <= t + 2 < len(order):
            stack(chunk_at(t + 2))

    x_own = prepare(0)
    multiply(x_own, 0, [0])
    stack(chunk_at(0))
    x_pair = both(prepare(1), prepare(2))
    multiply(x_pair, 0, [1, 2])
    stack(chunk_at(1))
    x_three = prepare(3)
    multiply(x_three, 0, [3])
    tick(0)
    multiply(x_pair, 1, [1, 2])
    x_rest = both(x_three, x_own)
    tick(1)
    multiply(x_rest, 1, [3, 0])
    tick(2)
    turned = run(
        lambda a, b: jnp.concatenate([b[group_rows:], a, b[:group_rows]], 0).T,
        x_pair["value"],
        x_rest["value"],
    )
    tick(3)
    tick(4)
    tick(5)
    tick(6)
    hidden = joined(0, range(GROUPS))
    partial = run(lambda h: down_product(h, weight, 0, None, jnp.float32), hidden["value"])
    tick(7)
    gradient = run(lambda h: weight_gradient(turned["value"], h, 0, None), hidden["value"])
    tick(8)

    def last_product(group, kept):
        one = joined(1, [group])
        before = partial["value"][group * group_rows : (group + 1) * group_rows]
        return run(lambda h: down_product(h, weight, 1, before, kept), one["value"])

    sent = {}
    for group in (1, 2, 3):
        sent[group] = last_product(group, jnp.bfloat16)
        if group == 2:
            tick(9)
    own = last_product(0, jnp.float32)
    hidden = joined(1, range(GROUPS))
    gradient = run(
        lambda h: weight_gradient(turned["value"], h, 1, gradient["value"]), hidden["value"]
    )
    result = own["value"][:rows]
    for by in range(1, peers):
        group, at = by // each, by % each
        block = own["value"].astype(jnp.bfloat16) if group == 0 else sent[group]["value"]
        result = result + from_peer(block[at * rows : (at + 1) * rows], by).astype(jnp.float32)
    return (result.astype(jnp.bfloat16)[None], gradient["value"][None])


def solution(mesh):
    placed = (P("mp", "dp"), P("section", "dp", "mp"), P("dp"), P("mp", "dp"))
    return jax.shard_map(
        local,
        mesh=mesh,
        in_specs=placed,
        out_specs=(P("section", "mp", "dp"), P("section", "dp", "mp")),
        check_vma=False,
    )
```

```python
import jax
import jax.numpy as jnp
from jax import lax
from jax.experimental import pallas as pl
from jax.experimental.pallas import tpu as pltpu
from jax.sharding import PartitionSpec as P

D = 12288
VMEM = 40 * 1024 * 1024
FAR, NEAR = 0, 1


epsilon = 1e-05


def dot_f32(left, right, contract):
    return lax.dot_general(
        left, right, ((contract[:1], contract[1:]), ((), ())), preferred_element_type=jnp.float32
    )


def tile_of(extent, limit):
    return max(t for t in range(128, limit + 1, 128) if extent % t == 0)


def call(kernel, name, grid, scalars, operands, in_specs, out_specs, out_shape, scratch=(), aliases={}):
    return pl.pallas_call(
        kernel,
        grid_spec=pltpu.PrefetchScalarGridSpec(
            num_scalar_prefetch=len(scalars),
            grid=grid,
            in_specs=in_specs,
            out_specs=out_specs,
            scratch_shapes=list(scratch),
        ),
        out_shape=out_shape,
        input_output_aliases=aliases,
        compiler_params=pltpu.CompilerParams(vmem_limit_bytes=VMEM),
        name=name,
    )(*scalars, *operands)


def normalize(first, blocks, scale, gain, group, into):
    rows, width = blocks[0].shape
    count = rows * len(blocks)
    tile = tile_of(width, 768)

    def kernel(first_ref, scale_ref, gain_ref, *refs):
        out = refs[-1]
        for i, ref in enumerate(refs[: len(blocks)]):
            own = pl.ds(i * rows, rows)
            value = ref[...].astype(jnp.float32)
            centred = (value - scale_ref[own, 0:1]) * scale_ref[own, 1:2]
            normed = (centred * gain_ref[...]).astype(jnp.bfloat16)
            out[own, :] = jnp.where(first_ref[0] == 1, normed, ref[...])

    column = lambda i, _: (0, i)
    extra = [] if into is None else [into]
    return call(
        kernel,
        "normalize",
        (width // tile,),
        [first],
        [scale, gain.reshape(1, width), *blocks, *extra],
        [pl.BlockSpec((count, 2), lambda i, _: (0, 0)), pl.BlockSpec((1, tile), column)]
        + [pl.BlockSpec((rows, tile), column)] * len(blocks)
        + [pl.BlockSpec(memory_space=pl.ANY)] * len(extra),
        pl.BlockSpec((count, tile), lambda i, _: (group, i)),
        jax.ShapeDtypeStruct((2 * count, width), jnp.bfloat16),
        aliases={3 + len(blocks): 0} if extra else {},
    )


def up_product(section, rows, weight, part, parts, groups):
    pieces = len(groups)
    count, width = rows.shape[0] // 2 * pieces, rows.shape[1]
    at = groups[0]
    columns = weight.shape[1] // parts
    tile = tile_of(columns // 2, 768)
    steps = columns // tile
    mine = steps // 2
    piece = count // pieces

    def kernel(section_ref, rows_ref, weight_ref, *results):
        product = dot_f32(rows_ref[...], weight_ref[...], (1, 0)).astype(jnp.bfloat16)

        def store(refs):
            for i, result in enumerate(refs):
                result[...] = product[i * piece : (i + 1) * piece]

        pl.when(pl.program_id(0) < mine)(lambda: store(results[:pieces]))
        pl.when(pl.program_id(0) >= mine)(lambda: store(results[pieces:]))

    column = lambda i, s: (0, part * steps + lax.rem(i + s[0] * mine, steps))
    return call(
        kernel,
        "up_product",
        (steps,),
        [section],
        [rows, weight],
        [pl.BlockSpec((count, width), lambda i, s: (at, 0)), pl.BlockSpec((width, tile), column)],
        [pl.BlockSpec((piece, tile), lambda i, s: (0, jnp.minimum(i, mine - 1)))] * pieces
        + [pl.BlockSpec((piece, tile), lambda i, s: (0, jnp.maximum(i - mine, 0)))] * pieces,
        [jax.ShapeDtypeStruct((piece, columns // 2), jnp.bfloat16)] * (2 * pieces),
    )


def elementwise(body, name, scalars, operands, out_rows):
    columns = operands[0].shape[1]
    tile = tile_of(columns, 256)
    column = lambda i, *_: (0, i)

    def kernel(*refs):
        scalar_refs = refs[: len(scalars)]
        ins = refs[len(scalars) : len(scalars) + len(operands)]
        outs = refs[len(scalars) + len(operands) :]
        for out, value in zip(outs, body(scalar_refs, ins)):
            out[...] = value

    return call(
        kernel,
        name,
        (columns // tile,),
        scalars,
        operands,
        [pl.BlockSpec((o.shape[0], tile), column) for o in operands],
        [pl.BlockSpec((r, tile), column) for r in out_rows],
        [jax.ShapeDtypeStruct((r, columns), jnp.bfloat16) for r in out_rows],
    )


def stacked(mine, arrived):
    rows = mine.shape[0]
    body = lambda _, ins: (jnp.concatenate([ins[0][...], ins[1][...]], 0),)
    return elementwise(body, "stacked", [], [mine, arrived], [2 * rows])[0]


def added(value, arrived):
    def body(_, ins):
        total = ins[0][...].astype(jnp.float32) + ins[1][...].astype(jnp.float32)
        return (total.astype(jnp.bfloat16),)

    return elementwise(body, "added", [], [value, arrived], [value.shape[0]])[0]


def activated(first, value, arrived):
    rows = value.shape[0] // 2

    def body(scalars, ins):
        is_first = scalars[0][0] == 1
        total = ins[0][...].astype(jnp.float32) + ins[1][...].astype(jnp.float32)
        above, below = total[:rows], total[rows:]
        v = jnp.where(is_first, above, below)
        grad = jnp.where(is_first, below, above)
        c = 0.7978845608028654
        t = jnp.tanh(c * (v + 0.044715 * (v * v * v)))
        hidden = (0.5 * v * (1.0 + t)).astype(jnp.bfloat16)
        slope = 0.5 * (1.0 + t) + 0.5 * v * (1.0 - t * t) * (c * (1.0 + 3.0 * 0.044715 * (v * v)))
        grad_preact = (grad * slope).astype(jnp.bfloat16)
        kept = jnp.where(is_first, grad_preact, hidden)
        sent = jnp.where(is_first, hidden, grad_preact)
        return (jnp.concatenate([kept, sent], 0),)

    return elementwise(body, "activated", [first], [value, arrived], [2 * rows])[0]


def chosen(receives, value, arrived, halves):
    rows = value.shape[0]

    def body(scalars, ins):
        result = jnp.where(scalars[0][0] == 1, ins[1][...], ins[0][...])
        return (result[: rows // 2], result[rows // 2 :]) if halves else (result,)

    out_rows = [rows // 2] * 2 if halves else [rows]
    return elementwise(body, "chosen", [receives], [value, arrived], out_rows)


def down_product(section, kept, came, weight, part, parts, before, before_row, kinds):
    counts = [k.shape[0] for k in kept]
    count, half = sum(counts), kept[0].shape[1]
    width = weight.shape[0]
    tile = tile_of(width, 256)
    piece = count // len(kinds)
    n = len(kept)

    def kernel(section_ref, *refs):
        weight_mine, weight_theirs = refs[2 * n : 2 * n + 2]
        results = refs[2 * n + 2 + (before is not None) : -2]
        held_mine, held_theirs = refs[-2:]

        @pl.when(pl.program_id(0) == 0)
        def _():
            at = 0
            for i, rows in enumerate(counts):
                held_mine[at : at + rows, :] = refs[i][...]
                held_theirs[at : at + rows, :] = refs[n + i][...]
                at += rows

        product = dot_f32(held_mine[...], weight_mine[...], (1, 1))
        product = product + dot_f32(held_theirs[...], weight_theirs[...], (1, 1))
        if before is not None:
            product = product + refs[2 * n + 2][...]
        for i, result in enumerate(results):
            result[...] = product[i * piece : (i + 1) * piece].astype(result.dtype)

    whole = [pl.BlockSpec((rows, half), lambda i, s: (0, 0)) for rows in counts]
    extra = [] if before is None else [before]
    return call(
        kernel,
        "down_product",
        (width // tile,),
        [section],
        [*kept, *came, weight, weight, *extra],
        whole
        + whole
        + [
            pl.BlockSpec((tile, half), lambda i, s: (i, 2 * part + s[0])),
            pl.BlockSpec((tile, half), lambda i, s: (i, 2 * part + 1 - s[0])),
        ]
        + [pl.BlockSpec((count, tile), lambda i, s: (before_row, i))] * len(extra),
        [pl.BlockSpec((piece, tile), lambda i, s: (0, i))] * len(kinds),
        [jax.ShapeDtypeStruct((piece, width), kind) for kind in kinds],
        [pltpu.VMEM((count, half), jnp.bfloat16)] * 2,
    )


def weight_gradient(section, turned, kept, came, part, parts, into):
    width, count = turned.shape
    counts = [k.shape[0] for k in kept]
    half = kept[0].shape[1]
    tile = tile_of(width, 512)
    n = len(kept)

    def kernel(section_ref, turned_ref, *refs):
        out, held = refs[-2:]

        def hold(blocks):
            at = 0
            for rows, block in zip(counts, blocks):
                held[at : at + rows, :] = block[...]
                at += rows

        start = pl.program_id(1) == 0
        pl.when(jnp.logical_and(start, pl.program_id(0) == 0))(lambda: hold(refs[:n]))
        pl.when(jnp.logical_and(start, pl.program_id(0) == 1))(lambda: hold(refs[n : 2 * n]))
        out[...] = dot_f32(turned_ref[...], held[...], (1, 0)).astype(jnp.bfloat16)

    whole = [pl.BlockSpec((rows, half), lambda j, i, s: (0, 0)) for rows in counts]
    extra = [] if into is None else [into]
    return call(
        kernel,
        "weight_gradient",
        (2, width // tile),
        [section],
        [turned, *kept, *came, *extra],
        [pl.BlockSpec((tile, count), lambda j, i, s: (i, 0))]
        + whole
        + whole
        + [pl.BlockSpec(memory_space=pl.ANY)] * len(extra),
        pl.BlockSpec((tile, half), lambda j, i, s: (i, 2 * part + lax.rem(j + s[0], 2))),
        jax.ShapeDtypeStruct((width, 2 * half * parts), jnp.bfloat16),
        [pltpu.VMEM((count, half), jnp.bfloat16)],
        {2 + 2 * n: 0} if extra else {},
    )


def from_peer(value, by):
    peers = lax.axis_size("mp")
    return lax.ppermute(value, "mp", [(i, i ^ by) for i in range(peers)])


def across_sections(value):
    return lax.ppermute(value, "section", [(0, 1), (1, 0)])


def local(tokens, weights, gain, cotangent):
    section = lax.axis_index("section").astype(jnp.int32).reshape(1)
    first = 1 - section
    weight = weights[0]
    peers = lax.axis_size("mp")
    line = lax.axis_size("dp")
    half = line // 2
    place = lax.axis_index("dp")
    rows = tokens.shape[0]
    each = peers // 4
    parts = 4 if weight.shape[1] % 1024 == 0 else 3

    last = []

    def run(work, anchor, *others):
        if last:
            held = last[-1]
            anchor, held["value"] = lax.optimization_barrier((anchor, held["value"]))
        held = {"value": work(anchor, *others)}
        last.append(held)
        return held

    raw = run(lambda a, b: jnp.where(first[0] == 1, a, b), tokens, cotangent)["value"]
    gathered = {by: from_peer(raw, by) for by in range(1, peers)}
    gathered[0] = raw

    values = tokens.astype(jnp.float32)
    sums = jnp.stack([jnp.sum(values, 1), jnp.sum(values * values, 1)], 1)
    mine = jnp.arange(peers)[:, None, None] == lax.axis_index("mp")
    sums = lax.psum(jnp.where(mine, sums[None], 0.0), ("dp", "mp"))
    average = sums[:, :, 0] / D
    inverse_std = lax.rsqrt(sums[:, :, 1] / D - average * average + epsilon)
    scale = jnp.stack([average, inverse_std], 2)

    far = list(range(2 * each, 4 * each))
    near = list(range(each, 2 * each)) + list(range(each))

    def prepare(members, group, into):
        mp = lax.axis_index("mp")
        scales = jnp.concatenate([lax.dynamic_index_in_dim(scale, mp ^ by, 0, False) for by in members], 0)
        return run(
            lambda s: normalize(first, [gathered[by] for by in members], s, gain, group, into), scales
        )["value"]

    chunks = {}

    def multiply(value, part, groups):
        products = run(lambda s: up_product(s, value, weight, part, parts, groups), section)
        for i, group in enumerate(groups):
            chunks[part, group] = {"products": products, "mine": i, "theirs": len(groups) + i}

    def stack(chunk):
        products = chunk["products"]
        arrived = across_sections(products["value"][chunk["theirs"]])
        chunk["sum"] = run(stacked, products["value"][chunk["mine"]], arrived)

    def inward(chunk):
        for hop in range(half - 1):
            value = chunk["sum"]["value"]
            arrived = lax.ppermute(value, "dp", [(hop, hop + 1), (line - 1 - hop, line - 2 - hop)])
            chunk["sum"] = run(added, value, arrived)

    def middle(chunk):
        value = chunk["sum"]["value"]
        arrived = lax.ppermute(value, "dp", [(half - 1, half), (half, half - 1)])
        chunk["result"] = run(lambda a, b: activated(first, a, b), value, arrived)

    def outward(chunk):
        for hop in reversed(range(half - 1)):
            value = chunk["result"]["value"]
            arrived = lax.ppermute(value, "dp", [(hop + 1, hop), (line - 2 - hop, line - 1 - hop)])
            receives = jnp.logical_or(place == hop, place == line - 1 - hop).astype(jnp.int32).reshape(1)
            if hop:
                chunk["result"] = run(lambda a, b: chosen(receives, a, b, False)[0], value, arrived)
            else:
                chunk["halves"] = run(lambda a, b: chosen(receives, a, b, True), value, arrived)

    def hidden(part, groups):
        kept = [chunks[part, g]["halves"]["value"][0] for g in groups]
        for g in groups:
            if "came" not in chunks[part, g]:
                chunks[part, g]["came"] = across_sections(chunks[part, g]["halves"]["value"][1])
        return kept, [chunks[part, g]["came"] for g in groups]

    both = (FAR, NEAR)
    order = [(part, g) for part in range(parts - 1) for g in (NEAR, FAR)]
    order += [(parts - 1, g) for g in (FAR, NEAR)]
    count = len(order)
    held = {"partial": None, "gradient": None}

    def tick(t):
        if 0 <= t - 1 < count:
            middle(chunks[order[t - 1]])
        if 0 <= t - 2 < count:
            outward(chunks[order[t - 2]])
        if 2 <= t + 2 < count:
            stack(chunks[order[t + 2]])

    def go_down(part):
        kept, came = hidden(part, both)
        before = None if held["partial"] is None else held["partial"]["value"][0]
        held["partial"] = run(
            lambda k: down_product(section, [k] + kept[1:], came, weight, part, parts, before, 0, [jnp.float32]),
            kept[0],
        )

    def go_gradient(part):
        kept, came = hidden(part, both)
        into = None if held["gradient"] is None else held["gradient"]["value"]
        held["gradient"] = run(
            lambda k: weight_gradient(section, turned, [k] + kept[1:], came, part, parts, into), kept[0]
        )

    def go_last(group, kinds):
        kept, came = hidden(parts - 1, [group])
        before = held["partial"]["value"][0]
        return run(
            lambda k: down_product(section, [k], came, weight, parts - 1, parts, before, group, kinds), kept[0]
        )

    x_near = prepare(near, NEAR, None)
    multiply(x_near, 0, [NEAR])
    stack(chunks[order[0]])
    x_all = prepare(far, FAR, x_near)
    multiply(x_all, 0, [FAR])
    stack(chunks[order[1]])
    for t in range(count + 2):
        if 0 <= t < count:
            inward(chunks[order[t]])
        if t == 0:
            multiply(x_all, 1, both)
        tick(t)
        if t == 0:
            turned = run(lambda a: a.T, x_all)["value"]
        part, odd = t // 2 + 2, t % 2 == 1
        if odd and part < parts:
            multiply(x_all, part, both)
        done, late = (t - 3) // 2, t % 2 == 1
        if t >= 3 and done < parts - 1:
            if late:
                go_down(done)
            else:
                go_gradient(done)
        if t == count:
            sent_far = go_last(FAR, [jnp.bfloat16] * 2)
    sent_near = go_last(NEAR, [jnp.bfloat16, jnp.float32])
    go_gradient(parts - 1)

    own = sent_near["value"][1]
    blocks = {0: own.astype(jnp.bfloat16), 1: sent_near["value"][0]}
    blocks[2], blocks[3] = sent_far["value"]
    result = own[:rows]
    for by in range(1, peers):
        at = (by % each) * rows
        result = result + from_peer(blocks[by // each][at : at + rows], by).astype(jnp.float32)
    return (result.astype(jnp.bfloat16)[None], held["gradient"]["value"][None])


def solution(mesh):
    placed = (P("mp", "dp"), P("section", "dp", "mp"), P("dp"), P("mp", "dp"))
    return jax.shard_map(
        local,
        mesh=mesh,
        in_specs=placed,
        out_specs=(P("section", "mp", "dp"), P("section", "dp", "mp")),
        check_vma=False,
    )
```

```python
import jax
import jax.numpy as jnp
from jax import lax
from jax.experimental import pallas as pl
from jax.experimental.pallas import tpu as pltpu
from jax.sharding import PartitionSpec as P

D = 12288
MATMUL_VMEM = 28 * 1024 * 1024
SMALL_VMEM = 8 * 1024 * 1024
FAR, NEAR = 0, 1


epsilon = 1e-05


def dot_f32(left, right, contract):
    return lax.dot_general(
        left, right, ((contract[:1], contract[1:]), ((), ())), preferred_element_type=jnp.float32
    )


def tile_of(extent, limit):
    return max(t for t in range(128, limit + 1, 128) if extent % t == 0)


def call(kernel, name, grid, scalars, operands, in_specs, out_specs, out_shape, scratch=(), aliases={}, vmem=MATMUL_VMEM):
    return pl.pallas_call(
        kernel,
        grid_spec=pltpu.PrefetchScalarGridSpec(
            num_scalar_prefetch=len(scalars),
            grid=grid,
            in_specs=in_specs,
            out_specs=out_specs,
            scratch_shapes=list(scratch),
        ),
        out_shape=out_shape,
        input_output_aliases=aliases,
        compiler_params=pltpu.CompilerParams(vmem_limit_bytes=vmem),
        name=name,
    )(*scalars, *operands)


def normalize(first, blocks, scales, gain, group, into):
    rows, width = blocks[0].shape
    count = rows * len(blocks)
    tile = tile_of(width, 768)

    def kernel(first_ref, gain_ref, *refs):
        out = refs[-1]
        for i in range(len(blocks)):
            ref, scale_ref = refs[i], refs[len(blocks) + i]
            value = ref[...].astype(jnp.float32)
            centred = (value - scale_ref[:, 0:1]) * scale_ref[:, 1:2]
            normed = (centred * gain_ref[...]).astype(jnp.bfloat16)
            out[i * rows : (i + 1) * rows, :] = jnp.where(first_ref[0] == 1, normed, ref[...])

    column = lambda i, _: (0, i)
    extra = [] if into is None else [into]
    return call(
        kernel,
        "normalize",
        (width // tile,),
        [first],
        [gain.reshape(1, width), *blocks, *scales, *extra],
        [pl.BlockSpec((1, tile), column)]
        + [pl.BlockSpec((rows, tile), column)] * len(blocks)
        + [pl.BlockSpec((rows, 2), lambda i, _: (0, 0))] * len(blocks)
        + [pl.BlockSpec(memory_space=pl.ANY)] * len(extra),
        pl.BlockSpec((count, tile), lambda i, _: (group, i)),
        jax.ShapeDtypeStruct((2 * count, width), jnp.bfloat16),
        aliases={2 + 2 * len(blocks): 0} if extra else {},
        vmem=SMALL_VMEM,
    )


def up_product(section, rows, weight, part, parts, groups):
    pieces = len(groups)
    count, width = rows.shape[0] // 2 * pieces, rows.shape[1]
    at = groups[0]
    columns = weight.shape[1] // parts
    tile = tile_of(columns // 2, 768)
    steps = columns // tile
    mine = steps // 2
    piece = count // pieces

    def kernel(section_ref, rows_ref, weight_ref, *results):
        product = dot_f32(rows_ref[...], weight_ref[...], (1, 0)).astype(jnp.bfloat16)

        def store(refs):
            for i, result in enumerate(refs):
                result[...] = product[i * piece : (i + 1) * piece]

        pl.when(pl.program_id(0) < mine)(lambda: store(results[:pieces]))
        pl.when(pl.program_id(0) >= mine)(lambda: store(results[pieces:]))

    column = lambda i, s: (0, part * steps + lax.rem(i + s[0] * mine, steps))
    return call(
        kernel,
        "up_product",
        (steps,),
        [section],
        [rows, weight],
        [pl.BlockSpec((count, width), lambda i, s: (at, 0)), pl.BlockSpec((width, tile), column)],
        [pl.BlockSpec((piece, tile), lambda i, s: (0, jnp.minimum(i, mine - 1)))] * pieces
        + [pl.BlockSpec((piece, tile), lambda i, s: (0, jnp.maximum(i - mine, 0)))] * pieces,
        [jax.ShapeDtypeStruct((piece, columns // 2), jnp.bfloat16)] * (2 * pieces),
    )


def elementwise(body, name, scalars, operands, out_rows):
    columns = operands[0].shape[1]
    tile = tile_of(columns, 256)
    column = lambda i, *_: (0, i)

    def kernel(*refs):
        scalar_refs = refs[: len(scalars)]
        ins = refs[len(scalars) : len(scalars) + len(operands)]
        outs = refs[len(scalars) + len(operands) :]
        for out, value in zip(outs, body(scalar_refs, ins)):
            out[...] = value

    return call(
        kernel,
        name,
        (columns // tile,),
        scalars,
        operands,
        [pl.BlockSpec((o.shape[0], tile), column) for o in operands],
        [pl.BlockSpec((r, tile), column) for r in out_rows],
        [jax.ShapeDtypeStruct((r, columns), jnp.bfloat16) for r in out_rows],
        vmem=SMALL_VMEM,
    )


def stacked(mine, arrived):
    rows = mine.shape[0]
    body = lambda _, ins: (jnp.concatenate([ins[0][...], ins[1][...]], 0),)
    return elementwise(body, "stacked", [], [mine, arrived], [2 * rows])[0]


def added(value, arrived):
    def body(_, ins):
        total = ins[0][...].astype(jnp.float32) + ins[1][...].astype(jnp.float32)
        return (total.astype(jnp.bfloat16),)

    return elementwise(body, "added", [], [value, arrived], [value.shape[0]])[0]


def activated(first, value, arrived):
    rows = value.shape[0] // 2

    def body(scalars, ins):
        is_first = scalars[0][0] == 1
        total = ins[0][...].astype(jnp.float32) + ins[1][...].astype(jnp.float32)
        above, below = total[:rows], total[rows:]
        v = jnp.where(is_first, above, below)
        grad = jnp.where(is_first, below, above)
        c = 0.7978845608028654
        t = jnp.tanh(c * (v + 0.044715 * (v * v * v)))
        hidden = (0.5 * v * (1.0 + t)).astype(jnp.bfloat16)
        slope = 0.5 * (1.0 + t) + 0.5 * v * (1.0 - t * t) * (c * (1.0 + 3.0 * 0.044715 * (v * v)))
        grad_preact = (grad * slope).astype(jnp.bfloat16)
        kept = jnp.where(is_first, grad_preact, hidden)
        sent = jnp.where(is_first, hidden, grad_preact)
        return (jnp.concatenate([kept, sent], 0),)

    return elementwise(body, "activated", [first], [value, arrived], [2 * rows])[0]


def chosen(receives, value, arrived, halves):
    rows = value.shape[0]

    def body(scalars, ins):
        result = jnp.where(scalars[0][0] == 1, ins[1][...], ins[0][...])
        return (result[: rows // 2], result[rows // 2 :]) if halves else (result,)

    out_rows = [rows // 2] * 2 if halves else [rows]
    return elementwise(body, "chosen", [receives], [value, arrived], out_rows)


def down_product(section, kept, came, weight, part, parts, before, group, kinds):
    counts = [k.shape[0] for k in kept]
    count, half = sum(counts), kept[0].shape[1]
    width = weight.shape[0]
    tile = tile_of(width, 512)
    n = len(kept)

    def kernel(section_ref, *refs):
        weight_mine, weight_theirs = refs[2 * n : 2 * n + 2]
        results = refs[2 * n + 2 + (before is not None) : -2]
        held_mine, held_theirs = refs[-2:]

        @pl.when(pl.program_id(0) == 0)
        def _():
            at = 0
            for i, rows in enumerate(counts):
                held_mine[:, at : at + rows] = refs[i][...].T
                held_theirs[:, at : at + rows] = refs[n + i][...].T
                at += rows

        product = dot_f32(weight_mine[...], held_mine[...], (1, 0))
        product = product + dot_f32(weight_theirs[...], held_theirs[...], (1, 0))
        if before is not None:
            product = product + refs[2 * n + 2][...]
        if kinds:
            product = product.T
            piece = count // len(kinds)
            for i, result in enumerate(results):
                result[...] = product[i * piece : (i + 1) * piece].astype(result.dtype)
        else:
            results[0][...] = product

    whole = [pl.BlockSpec((rows, half), lambda i, s: (0, 0)) for rows in counts]
    extra = [] if before is None else [before]
    if kinds:
        out_specs = [pl.BlockSpec((count // len(kinds), tile), lambda i, s: (0, i))] * len(kinds)
        out_shape = [jax.ShapeDtypeStruct((count // len(kinds), width), kind) for kind in kinds]
    else:
        out_specs = [pl.BlockSpec((tile, count), lambda i, s: (i, 0))]
        out_shape = [jax.ShapeDtypeStruct((width, count), jnp.float32)]
    return call(
        kernel,
        "down_product",
        (width // tile,),
        [section],
        [*kept, *came, weight, weight, *extra],
        whole
        + whole
        + [
            pl.BlockSpec((tile, half), lambda i, s: (i, 2 * part + s[0])),
            pl.BlockSpec((tile, half), lambda i, s: (i, 2 * part + 1 - s[0])),
        ]
        + [pl.BlockSpec((tile, count), lambda i, s: (i, group))] * len(extra),
        out_specs,
        out_shape,
        [pltpu.VMEM((half, count), jnp.bfloat16)] * 2,
    )


def weight_gradient(section, turned, kept, came, part, parts, into):
    width, count = turned.shape
    counts = [k.shape[0] for k in kept]
    half = kept[0].shape[1]
    tile = tile_of(width, 1024)
    n = len(kept)

    def kernel(section_ref, turned_ref, *refs):
        out, held = refs[-2:]

        def hold(blocks):
            at = 0
            for rows, block in zip(counts, blocks):
                held[at : at + rows, :] = block[...]
                at += rows

        start = pl.program_id(1) == 0
        pl.when(jnp.logical_and(start, pl.program_id(0) == 0))(lambda: hold(refs[:n]))
        pl.when(jnp.logical_and(start, pl.program_id(0) == 1))(lambda: hold(refs[n : 2 * n]))
        out[...] = dot_f32(turned_ref[...], held[...], (1, 0)).astype(jnp.bfloat16)

    whole = [pl.BlockSpec((rows, half), lambda j, i, s: (0, 0)) for rows in counts]
    extra = [] if into is None else [into]
    return call(
        kernel,
        "weight_gradient",
        (2, width // tile),
        [section],
        [turned, *kept, *came, *extra],
        [pl.BlockSpec((tile, count), lambda j, i, s: (i, 0))]
        + whole
        + whole
        + [pl.BlockSpec(memory_space=pl.ANY)] * len(extra),
        pl.BlockSpec((tile, half), lambda j, i, s: (i, 2 * part + lax.rem(j + s[0], 2))),
        jax.ShapeDtypeStruct((width, 2 * half * parts), jnp.bfloat16),
        [pltpu.VMEM((count, half), jnp.bfloat16)],
        {2 + 2 * n: 0} if extra else {},
    )


def from_peer(value, by):
    peers = lax.axis_size("mp")
    return lax.ppermute(value, "mp", [(i, i ^ by) for i in range(peers)])


def across_sections(value):
    return lax.ppermute(value, "section", [(0, 1), (1, 0)])


def local(tokens, weights, gain, cotangent):
    section = lax.axis_index("section").astype(jnp.int32).reshape(1)
    first = 1 - section
    weight = weights[0]
    peers = lax.axis_size("mp")
    line = lax.axis_size("dp")
    half = line // 2
    place = lax.axis_index("dp")
    rows = tokens.shape[0]
    each = peers // 4
    parts = 4 if weight.shape[1] % 1024 == 0 else 3

    last = []

    def run(work, anchor, *others):
        if last:
            held = last[-1]
            anchor, held["value"] = lax.optimization_barrier((anchor, held["value"]))
        held = {"value": work(anchor, *others)}
        last.append(held)
        return held

    raw = run(lambda a, b: jnp.where(first[0] == 1, a, b), tokens, cotangent)["value"]
    gathered = {by: from_peer(raw, by) for by in range(1, peers)}
    gathered[0] = raw

    values = tokens.astype(jnp.float32)
    row_total, row_squares = lax.psum((jnp.sum(values, 1), jnp.sum(values * values, 1)), "dp")
    average = row_total / D
    inverse_std = lax.rsqrt(row_squares / D - average * average + epsilon)
    own_scale = jnp.stack([average, inverse_std], 1)
    scale = {by: from_peer(own_scale, by) for by in range(1, peers)}
    scale[0] = own_scale

    far = list(range(2 * each, 4 * each))
    near = list(range(each, 2 * each)) + list(range(each))

    def prepare(members, group, into):
        blocks, scales = [gathered[by] for by in members], [scale[by] for by in members]
        return run(lambda g: normalize(first, blocks, scales, g, group, into), gain)["value"]

    chunks = {}

    def multiply(value, part, groups):
        products = run(lambda s: up_product(s, value, weight, part, parts, groups), section)
        for i, group in enumerate(groups):
            chunks[part, group] = {"products": products, "mine": i, "theirs": len(groups) + i}

    def stack(chunk):
        products = chunk["products"]
        arrived = across_sections(products["value"][chunk["theirs"]])
        chunk["sum"] = run(stacked, products["value"][chunk["mine"]], arrived)

    def inward(chunk):
        for hop in range(half - 1):
            value = chunk["sum"]["value"]
            arrived = lax.ppermute(value, "dp", [(hop, hop + 1), (line - 1 - hop, line - 2 - hop)])
            chunk["sum"] = run(added, value, arrived)

    def middle(chunk):
        value = chunk["sum"]["value"]
        arrived = lax.ppermute(value, "dp", [(half - 1, half), (half, half - 1)])
        chunk["result"] = run(lambda a, b: activated(first, a, b), value, arrived)

    def outward(chunk):
        for hop in reversed(range(half - 1)):
            value = chunk["result"]["value"]
            arrived = lax.ppermute(value, "dp", [(hop + 1, hop), (line - 2 - hop, line - 1 - hop)])
            receives = jnp.logical_or(place == hop, place == line - 1 - hop).astype(jnp.int32).reshape(1)
            if hop:
                chunk["result"] = run(lambda a, b: chosen(receives, a, b, False)[0], value, arrived)
            else:
                chunk["halves"] = run(lambda a, b: chosen(receives, a, b, True), value, arrived)

    def hidden(part, groups):
        kept = [chunks[part, g]["halves"]["value"][0] for g in groups]
        for g in groups:
            if "came" not in chunks[part, g]:
                chunks[part, g]["came"] = across_sections(chunks[part, g]["halves"]["value"][1])
        return kept, [chunks[part, g]["came"] for g in groups]

    both = (FAR, NEAR)
    order = [(part, g) for part in range(parts - 2) for g in (NEAR, FAR)]
    order += [(part, g) for g in (FAR, NEAR) for part in (parts - 2, parts - 1)]
    count = len(order)
    multiplied = {0}
    held = {"partial": None, "gradient": None}

    def need(c):
        if c < count and order[c][0] not in multiplied:
            multiplied.add(order[c][0])
            multiply(x_all, order[c][0], both)

    def tick(t):
        if 0 <= t - 1 < count:
            middle(chunks[order[t - 1]])
        if 0 <= t - 2 < count:
            outward(chunks[order[t - 2]])
        if 2 <= t + 2 < count:
            stack(chunks[order[t + 2]])

    def go_down(part, groups, before, column, kinds=()):
        kept, came = hidden(part, groups)
        before = None if before is None else before["value"][0]
        return run(
            lambda k: down_product(section, [k] + kept[1:], came, weight, part, parts, before, column, kinds),
            kept[0],
        )

    def go_gradient(part):
        kept, came = hidden(part, both)
        into = None if held["gradient"] is None else held["gradient"]["value"]
        held["gradient"] = run(
            lambda k: weight_gradient(section, turned, [k] + kept[1:], came, part, parts, into), kept[0]
        )

    x_near = prepare(near, NEAR, None)
    multiply(x_near, 0, [NEAR])
    stack(chunks[order[0]])
    x_all = prepare(far, FAR, x_near)
    multiply(x_all, 0, [FAR])
    stack(chunks[order[1]])
    for t in range(count + 2):
        if 0 <= t < count:
            inward(chunks[order[t]])
        if t == 0:
            need(2)
        tick(t)
        if t == 0:
            turned = run(lambda a: a.T, x_all)["value"]
        need(t + 3)
        if t >= 3 and (t - 3) // 2 < parts - 2:
            if t % 2 == 1:
                held["partial"] = go_down((t - 3) // 2, both, held["partial"], 0)
            else:
                go_gradient((t - 3) // 2)
        if t == count - 1:
            far_sum = go_down(parts - 2, [FAR], held["partial"], FAR)
        if t == count:
            sent_far = go_down(parts - 1, [FAR], far_sum, 0, [jnp.bfloat16] * 2)
            go_gradient(parts - 2)
            near_sum = go_down(parts - 2, [NEAR], held["partial"], NEAR)
    sent_near = go_down(parts - 1, [NEAR], near_sum, 0, [jnp.bfloat16, jnp.float32])
    go_gradient(parts - 1)

    own = sent_near["value"][1]
    blocks = {0: own.astype(jnp.bfloat16), 1: sent_near["value"][0]}
    blocks[2], blocks[3] = sent_far["value"]
    result = own[:rows]
    for by in range(1, peers):
        at = (by % each) * rows
        result = result + from_peer(blocks[by // each][at : at + rows], by).astype(jnp.float32)
    return (result.astype(jnp.bfloat16)[None], held["gradient"]["value"][None])


def solution(mesh):
    placed = (P("mp", "dp"), P("section", "dp", "mp"), P("dp"), P("mp", "dp"))
    return jax.shard_map(
        local,
        mesh=mesh,
        in_specs=placed,
        out_specs=(P("section", "mp", "dp"), P("section", "dp", "mp")),
        check_vma=False,
    )
```

```python
import jax
import jax.numpy as jnp
from jax import lax
from jax.experimental import pallas as pl
from jax.experimental.pallas import tpu as pltpu
from jax.sharding import PartitionSpec as P

D = 12288
MATMUL_VMEM = 18 * 1024 * 1024
SMALL_VMEM = 8 * 1024 * 1024
FAR, NEAR = 0, 1


epsilon = 1e-05


def dot_f32(left, right, contract):
    return lax.dot_general(
        left, right, ((contract[:1], contract[1:]), ((), ())), preferred_element_type=jnp.float32
    )


def tile_of(extent, limit):
    return max(t for t in range(128, limit + 1, 128) if extent % t == 0)


def fixed(shape, index):
    return pl.BlockSpec(shape, lambda *_: index, pipeline_mode=pl.Buffered(1))


def call(kernel, name, grid, scalars, operands, in_specs, out_specs, out_shape, scratch=(), aliases={}, vmem=MATMUL_VMEM):
    return pl.pallas_call(
        kernel,
        grid_spec=pltpu.PrefetchScalarGridSpec(
            num_scalar_prefetch=len(scalars),
            grid=grid,
            in_specs=in_specs,
            out_specs=out_specs,
            scratch_shapes=list(scratch),
        ),
        out_shape=out_shape,
        input_output_aliases=aliases,
        compiler_params=pltpu.CompilerParams(vmem_limit_bytes=vmem),
        name=name,
    )(*scalars, *operands)


def normalize(first, blocks, scale, gain, group, into):
    rows, width = blocks[0].shape
    count = rows * len(blocks)
    tile = tile_of(width, 768)

    def kernel(first_ref, gain_ref, scale_ref, *refs):
        out = refs[-1]
        for i in range(len(blocks)):
            own = slice(i * rows, (i + 1) * rows)
            value = refs[i][...].astype(jnp.float32)
            centred = (value - scale_ref[own, 0:1]) * scale_ref[own, 1:2]
            normed = (centred * gain_ref[...]).astype(jnp.bfloat16)
            out[own, :] = jnp.where(first_ref[0] == 1, normed, refs[i][...])

    column = lambda i, _: (0, i)
    extra = [] if into is None else [into]
    return call(
        kernel,
        "normalize",
        (width // tile,),
        [first],
        [gain.reshape(1, width), scale, *blocks, *extra],
        [pl.BlockSpec((1, tile), column), fixed((count, 2), (0, 0))]
        + [pl.BlockSpec((rows, tile), column)] * len(blocks)
        + [pl.BlockSpec(memory_space=pl.ANY)] * len(extra),
        pl.BlockSpec((count, tile), lambda i, _: (group, i)),
        jax.ShapeDtypeStruct((2 * count, width), jnp.bfloat16),
        aliases={3 + len(blocks): 0} if extra else {},
        vmem=SMALL_VMEM,
    )


def up_product(section, rows, weight, part, parts, groups):
    pieces = len(groups)
    count, width = rows.shape[0] // 2 * pieces, rows.shape[1]
    at = groups[0]
    columns = weight.shape[1] // parts
    tile = tile_of(columns // 2, 384)
    steps = columns // tile
    mine = steps // 2
    piece = count // pieces

    def kernel(section_ref, rows_ref, upper_ref, lower_ref, *results):
        product = dot_f32(rows_ref[:, : width // 2], upper_ref[...], (1, 0))
        product = product + dot_f32(rows_ref[:, width // 2 :], lower_ref[...], (1, 0))
        product = product.astype(jnp.bfloat16)

        def store(refs):
            for i, result in enumerate(refs):
                result[...] = product[i * piece : (i + 1) * piece]

        pl.when(pl.program_id(0) < mine)(lambda: store(results[:pieces]))
        pl.when(pl.program_id(0) >= mine)(lambda: store(results[pieces:]))

    def column(k):
        return lambda i, s: (k, part * steps + lax.rem(i + s[0] * mine, steps))

    return call(
        kernel,
        "up_product",
        (steps,),
        [section],
        [rows, weight, weight],
        [
            fixed((count, width), (at, 0)),
            pl.BlockSpec((width // 2, tile), column(0)),
            pl.BlockSpec((width // 2, tile), column(1)),
        ],
        [pl.BlockSpec((piece, tile), lambda i, s: (0, jnp.minimum(i, mine - 1)))] * pieces
        + [pl.BlockSpec((piece, tile), lambda i, s: (0, jnp.maximum(i - mine, 0)))] * pieces,
        [jax.ShapeDtypeStruct((piece, columns // 2), jnp.bfloat16)] * (2 * pieces),
    )


def elementwise(body, name, scalars, operands, out_rows):
    columns = operands[0].shape[1]
    tile = tile_of(columns, 256)
    column = lambda i, *_: (0, i)

    def kernel(*refs):
        scalar_refs = refs[: len(scalars)]
        ins = refs[len(scalars) : len(scalars) + len(operands)]
        outs = refs[len(scalars) + len(operands) :]
        for out, value in zip(outs, body(scalar_refs, ins)):
            out[...] = value

    return call(
        kernel,
        name,
        (columns // tile,),
        scalars,
        operands,
        [pl.BlockSpec((o.shape[0], tile), column) for o in operands],
        [pl.BlockSpec((r, tile), column) for r in out_rows],
        [jax.ShapeDtypeStruct((r, columns), jnp.bfloat16) for r in out_rows],
        vmem=SMALL_VMEM,
    )


def stacked(mine, arrived):
    rows = mine.shape[0]
    body = lambda _, ins: (jnp.concatenate([ins[0][...], ins[1][...]], 0),)
    return elementwise(body, "stacked", [], [mine, arrived], [2 * rows])[0]


def added(value, arrived):
    def body(_, ins):
        total = ins[0][...].astype(jnp.float32) + ins[1][...].astype(jnp.float32)
        return (total.astype(jnp.bfloat16),)

    return elementwise(body, "added", [], [value, arrived], [value.shape[0]])[0]


def activated(first, value, arrived):
    rows = value.shape[0] // 2

    def body(scalars, ins):
        is_first = scalars[0][0] == 1
        total = ins[0][...].astype(jnp.float32) + ins[1][...].astype(jnp.float32)
        above, below = total[:rows], total[rows:]
        v = jnp.where(is_first, above, below)
        grad = jnp.where(is_first, below, above)
        c = 0.7978845608028654
        t = jnp.tanh(c * (v + 0.044715 * (v * v * v)))
        hidden = (0.5 * v * (1.0 + t)).astype(jnp.bfloat16)
        slope = 0.5 * (1.0 + t) + 0.5 * v * (1.0 - t * t) * (c * (1.0 + 3.0 * 0.044715 * (v * v)))
        grad_preact = (grad * slope).astype(jnp.bfloat16)
        kept = jnp.where(is_first, grad_preact, hidden)
        sent = jnp.where(is_first, hidden, grad_preact)
        return (jnp.concatenate([kept, sent], 0),)

    return elementwise(body, "activated", [first], [value, arrived], [2 * rows])[0]


def chosen(receives, value, arrived, halves):
    rows = value.shape[0]

    def body(scalars, ins):
        result = jnp.where(scalars[0][0] == 1, ins[1][...], ins[0][...])
        return (result[: rows // 2], result[rows // 2 :]) if halves else (result,)

    out_rows = [rows // 2] * 2 if halves else [rows]
    return elementwise(body, "chosen", [receives], [value, arrived], out_rows)


def down_product(section, kept, came, weight, part, parts, before, group, arrived, kinds):
    counts = [k.shape[0] for k in kept]
    count, half = sum(counts), kept[0].shape[1]
    width = weight.shape[0]
    tile = 2 * tile_of(width // 2, 256)
    n = len(kept)
    extra = [] if before is None else [before]

    def kernel(section_ref, *refs):
        upper_ref, lower_ref = refs[2 * n : 2 * n + 2]
        added = refs[2 * n + 2 : 2 * n + 2 + len(extra)]
        others = refs[2 * n + 2 + len(extra) : 2 * n + 2 + len(extra) + len(arrived)]
        results = refs[2 * n + 2 + len(extra) + len(arrived) : -1]
        held = refs[-1]

        @pl.when(pl.program_id(0) == 0)
        def _():
            mine = pl.ds(pl.multiple_of(section_ref[0] * half, half), half)
            theirs = pl.ds(pl.multiple_of((1 - section_ref[0]) * half, half), half)
            at = 0
            for i, rows in enumerate(counts):
                held[mine, at : at + rows] = refs[i][...].T
                held[theirs, at : at + rows] = refs[n + i][...].T
                at += rows

        for k, weight_ref in enumerate((upper_ref, lower_ref)):
            own = slice(k * tile // 2, (k + 1) * tile // 2)
            product = dot_f32(weight_ref[...], held[...], (1, 0))
            for ref in added:
                product = product + ref[own, :]
            if kinds:
                product = product.T
                piece = count // len(kinds)
                for i, result in enumerate(results):
                    value = product[i * piece : (i + 1) * piece]
                    if arrived:
                        value = value + others[i][:, own].astype(jnp.float32)
                    result[:, own] = value.astype(result.dtype)
            else:
                results[0][own, :] = product

    whole = [fixed((rows, half), (0, 0)) for rows in counts]
    if kinds:
        piece_spec = pl.BlockSpec((count // len(kinds), tile), lambda i, s: (0, i))
        out_specs = [piece_spec] * len(kinds)
        out_shape = [jax.ShapeDtypeStruct((count // len(kinds), width), kind) for kind in kinds]
    else:
        out_specs = [pl.BlockSpec((tile, count), lambda i, s: (i, 0))]
        out_shape = [jax.ShapeDtypeStruct((width, count), jnp.float32)]
    return call(
        kernel,
        "down_product",
        (width // tile,),
        [section],
        [*kept, *came, weight, weight, *extra, *arrived],
        whole
        + whole
        + [
            pl.BlockSpec((tile // 2, 2 * half), lambda i, s: (2 * i, part)),
            pl.BlockSpec((tile // 2, 2 * half), lambda i, s: (2 * i + 1, part)),
        ]
        + [pl.BlockSpec((tile, count), lambda i, s: (i, group))] * len(extra)
        + [pl.BlockSpec((count // max(len(kinds), 1), tile), lambda i, s: (0, i))] * len(arrived),
        out_specs,
        out_shape,
        [pltpu.VMEM((2 * half, count), jnp.bfloat16)],
    )


def weight_gradient(section, turned, kept, came, part, parts, into):
    width, count = turned.shape
    counts = [k.shape[0] for k in kept]
    half = kept[0].shape[1]
    tile = tile_of(width, 512)
    n = len(kept)

    def kernel(section_ref, turned_ref, *refs):
        out, held = refs[-2:]

        @pl.when(pl.program_id(0) == 0)
        def _():
            mine = pl.ds(pl.multiple_of(section_ref[0] * half, half), half)
            theirs = pl.ds(pl.multiple_of((1 - section_ref[0]) * half, half), half)
            at = 0
            for i, rows in enumerate(counts):
                held[at : at + rows, mine] = refs[i][...]
                held[at : at + rows, theirs] = refs[n + i][...]
                at += rows

        out[...] = dot_f32(turned_ref[...], held[...], (1, 0)).astype(jnp.bfloat16)

    whole = [fixed((rows, half), (0, 0)) for rows in counts]
    extra = [] if into is None else [into]
    return call(
        kernel,
        "weight_gradient",
        (width // tile,),
        [section],
        [turned, *kept, *came, *extra],
        [pl.BlockSpec((tile, count), lambda i, s: (i, 0))]
        + whole
        + whole
        + [pl.BlockSpec(memory_space=pl.ANY)] * len(extra),
        pl.BlockSpec((tile, 2 * half), lambda i, s: (i, part)),
        jax.ShapeDtypeStruct((width, 2 * half * parts), jnp.bfloat16),
        [pltpu.VMEM((count, 2 * half), jnp.bfloat16)],
        {2 + 2 * n: 0} if extra else {},
    )


def from_peer(value, by):
    peers = lax.axis_size("mp")
    return lax.ppermute(value, "mp", [(i, i ^ by) for i in range(peers)])


def across_sections(value):
    return lax.ppermute(value, "section", [(0, 1), (1, 0)])


def local(tokens, weights, gain, cotangent):
    section = lax.axis_index("section").astype(jnp.int32).reshape(1)
    first = 1 - section
    weight = weights[0]
    peers = lax.axis_size("mp")
    line = lax.axis_size("dp")
    half = line // 2
    place = lax.axis_index("dp")
    rows = tokens.shape[0]
    each = peers // 4
    parts = 4 if weight.shape[1] % 1024 == 0 else 3

    last = []

    def run(work, anchor, *others):
        if last:
            held = last[-1]
            anchor, held["value"] = lax.optimization_barrier((anchor, held["value"]))
        held = {"value": work(anchor, *others)}
        last.append(held)
        return held

    raw = run(lambda a, b: jnp.where(first[0] == 1, a, b), tokens, cotangent)["value"]
    across = peers // 2
    near = list(range(each, 2 * each)) + list(range(each))
    far = [by ^ across for by in near]
    gathered = {by: from_peer(raw, by) if by else raw for by in near}
    gathered.update({by: from_peer(gathered[by ^ across], across) for by in far})

    values = tokens.astype(jnp.float32)
    row_total, row_squares = lax.psum((jnp.sum(values, 1), jnp.sum(values * values, 1)), "dp")
    average = row_total / D
    inverse_std = lax.rsqrt(row_squares / D - average * average + epsilon)
    own_scale = jnp.stack([average, inverse_std], 1)
    near_scale = jnp.concatenate([from_peer(own_scale, by) if by else own_scale for by in near], 0)
    far_scale = from_peer(near_scale, across)

    def prepare(members, scale, group, into):
        blocks = [gathered[by] for by in members]
        return run(lambda g: normalize(first, blocks, scale, g, group, into), gain)["value"]

    chunks = {}

    def multiply(value, part, groups):
        products = run(lambda s: up_product(s, value, weight, part, parts, groups), section)
        for i, group in enumerate(groups):
            chunks[part, group] = {"products": products, "mine": i, "theirs": len(groups) + i}

    def stack(chunk):
        products = chunk["products"]
        arrived = across_sections(products["value"][chunk["theirs"]])
        chunk["sum"] = run(stacked, products["value"][chunk["mine"]], arrived)

    def inward(chunk):
        for hop in range(half - 1):
            value = chunk["sum"]["value"]
            arrived = lax.ppermute(value, "dp", [(hop, hop + 1), (line - 1 - hop, line - 2 - hop)])
            chunk["sum"] = run(added, value, arrived)

    def middle(chunk):
        value = chunk["sum"]["value"]
        arrived = lax.ppermute(value, "dp", [(half - 1, half), (half, half - 1)])
        chunk["result"] = run(lambda a, b: activated(first, a, b), value, arrived)

    def outward(chunk):
        for hop in reversed(range(half - 1)):
            value = chunk["result"]["value"]
            arrived = lax.ppermute(value, "dp", [(hop + 1, hop), (line - 2 - hop, line - 1 - hop)])
            receives = jnp.logical_or(place == hop, place == line - 1 - hop).astype(jnp.int32).reshape(1)
            if hop:
                chunk["result"] = run(lambda a, b: chosen(receives, a, b, False)[0], value, arrived)
            else:
                chunk["halves"] = run(lambda a, b: chosen(receives, a, b, True), value, arrived)

    def hidden(part, groups):
        kept = [chunks[part, g]["halves"]["value"][0] for g in groups]
        for g in groups:
            if "came" not in chunks[part, g]:
                chunks[part, g]["came"] = across_sections(chunks[part, g]["halves"]["value"][1])
        return kept, [chunks[part, g]["came"] for g in groups]

    both = (FAR, NEAR)
    order = [(part, g) for part in range(parts - 2) for g in (NEAR, FAR)]
    order += [(part, g) for g in (FAR, NEAR) for part in (parts - 2, parts - 1)]
    count = len(order)
    multiplied = {0}
    held = {"partial": None, "gradient": None}

    def need(c):
        if c < count and order[c][0] not in multiplied:
            multiplied.add(order[c][0])
            multiply(x_all, order[c][0], both)

    def tick(t):
        if 0 <= t - 1 < count:
            middle(chunks[order[t - 1]])
        if 0 <= t - 2 < count:
            outward(chunks[order[t - 2]])
        if 2 <= t + 2 < count:
            stack(chunks[order[t + 2]])

    def go_down(part, groups, before, column, kinds=(), arrived=()):
        kept, came = hidden(part, groups)
        before = None if before is None else before["value"][0]
        return run(
            lambda k: down_product(section, [k] + kept[1:], came, weight, part, parts, before, column, arrived, kinds),
            kept[0],
        )

    def go_gradient(part):
        kept, came = hidden(part, both)
        into = None if held["gradient"] is None else held["gradient"]["value"]
        held["gradient"] = run(
            lambda k: weight_gradient(section, turned, [k] + kept[1:], came, part, parts, into), kept[0]
        )

    x_near = prepare(near, near_scale, NEAR, None)
    multiply(x_near, 0, [NEAR])
    stack(chunks[order[0]])
    x_all = prepare(far, far_scale, FAR, x_near)
    multiply(x_all, 0, [FAR])
    stack(chunks[order[1]])
    for t in range(count + 2):
        if 0 <= t < count:
            inward(chunks[order[t]])
        if t == 0:
            need(2)
        tick(t)
        if t == 0:
            turned = run(lambda a: a.T, x_all)["value"]
        need(t + 3)
        if t >= 3 and (t - 3) // 2 < parts - 2:
            if t % 2 == 1:
                held["partial"] = go_down((t - 3) // 2, both, held["partial"], 0)
            else:
                go_gradient((t - 3) // 2)
        if t == count - 1:
            far_sum = go_down(parts - 2, [FAR], held["partial"], FAR)
            sent_far = go_down(parts - 1, [FAR], far_sum, 0, [jnp.bfloat16] * 2)
        if t == count:
            go_gradient(parts - 2)
            near_sum = go_down(parts - 2, [NEAR], held["partial"], NEAR)
            arrived = [from_peer(value, across) for value in sent_far["value"]]
            near_sum["value"], arrived[0] = lax.optimization_barrier((near_sum["value"], arrived[0]))
    sent_near = go_down(parts - 1, [NEAR], near_sum, 0, [jnp.bfloat16, jnp.float32], arrived)
    go_gradient(parts - 1)

    own = sent_near["value"][1]
    blocks = {0: own.astype(jnp.bfloat16), 1: sent_near["value"][0]}
    result = own[:rows]
    for by in range(1, across):
        at = (by % each) * rows
        result = result + from_peer(blocks[by // each][at : at + rows], by).astype(jnp.float32)
    return (result.astype(jnp.bfloat16)[None], held["gradient"]["value"][None])


def solution(mesh):
    placed = (P("mp", "dp"), P("section", "dp", "mp"), P("dp"), P("mp", "dp"))
    return jax.shard_map(
        local,
        mesh=mesh,
        in_specs=placed,
        out_specs=(P("section", "mp", "dp"), P("section", "dp", "mp")),
        check_vma=False,
    )
```

```python
import jax
import jax.numpy as jnp
from jax import lax
from jax.experimental import pallas as pl
from jax.experimental.pallas import tpu as pltpu
from jax.sharding import PartitionSpec as P

D = 12288
MATMUL_VMEM = 22 * 1024 * 1024
SMALL_VMEM = 8 * 1024 * 1024
FAR, NEAR = 0, 1


epsilon = 1e-05


def dot_f32(left, right, contract):
    return lax.dot_general(
        left, right, ((contract[:1], contract[1:]), ((), ())), preferred_element_type=jnp.float32
    )


def tile_of(extent, limit):
    return max(t for t in range(128, limit + 1, 128) if extent % t == 0)


def fixed(shape, index):
    return pl.BlockSpec(shape, lambda *_: index, pipeline_mode=pl.Buffered(1))


def call(kernel, name, grid, scalars, operands, in_specs, out_specs, out_shape, scratch=(), aliases={}, vmem=MATMUL_VMEM):
    return pl.pallas_call(
        kernel,
        grid_spec=pltpu.PrefetchScalarGridSpec(
            num_scalar_prefetch=len(scalars),
            grid=grid,
            in_specs=in_specs,
            out_specs=out_specs,
            scratch_shapes=list(scratch),
        ),
        out_shape=out_shape,
        input_output_aliases=aliases,
        compiler_params=pltpu.CompilerParams(vmem_limit_bytes=vmem),
        name=name,
    )(*scalars, *operands)


def normalize(first, blocks, scale, gain, group, into):
    rows, width = blocks[0].shape
    count = rows * len(blocks)
    tile = tile_of(width, 768)

    def kernel(first_ref, gain_ref, scale_ref, *refs):
        out = refs[-1]
        for i in range(len(blocks)):
            own = slice(i * rows, (i + 1) * rows)
            value = refs[i][...].astype(jnp.float32)
            centred = (value - scale_ref[own, 0:1]) * scale_ref[own, 1:2]
            normed = (centred * gain_ref[...]).astype(jnp.bfloat16)
            out[own, :] = jnp.where(first_ref[0] == 1, normed, refs[i][...])

    column = lambda i, _: (0, i)
    extra = [] if into is None else [into]
    return call(
        kernel,
        "normalize",
        (width // tile,),
        [first],
        [gain.reshape(1, width), scale, *blocks, *extra],
        [pl.BlockSpec((1, tile), column), fixed((count, 2), (0, 0))]
        + [pl.BlockSpec((rows, tile), column)] * len(blocks)
        + [pl.BlockSpec(memory_space=pl.ANY)] * len(extra),
        pl.BlockSpec((count, tile), lambda i, _: (group, i)),
        jax.ShapeDtypeStruct((2 * count, width), jnp.bfloat16),
        aliases={3 + len(blocks): 0} if extra else {},
        vmem=SMALL_VMEM,
    )


def up_product(section, rows, weight, part, parts, groups):
    pieces = len(groups)
    count, width = rows.shape[0] // 2 * pieces, rows.shape[1]
    at = groups[0]
    columns = weight.shape[1] // parts
    tile = tile_of(columns // 2, 384)
    steps = columns // tile
    mine = steps // 2
    piece = count // pieces

    def kernel(section_ref, rows_ref, weight_ref, *results):
        product = dot_f32(rows_ref[...], weight_ref[...], (1, 0)).astype(jnp.bfloat16)

        def store(refs):
            for i, result in enumerate(refs):
                result[...] = product[i * piece : (i + 1) * piece]

        pl.when(pl.program_id(0) < mine)(lambda: store(results[:pieces]))
        pl.when(pl.program_id(0) >= mine)(lambda: store(results[pieces:]))

    column = lambda i, s: (0, part * steps + lax.rem(i + s[0] * mine, steps))
    return call(
        kernel,
        "up_product",
        (steps,),
        [section],
        [rows, weight],
        [
            fixed((count, width), (at, 0)),
            pl.BlockSpec((width, tile), column),
        ],
        [pl.BlockSpec((piece, tile), lambda i, s: (0, jnp.minimum(i, mine - 1)))] * pieces
        + [pl.BlockSpec((piece, tile), lambda i, s: (0, jnp.maximum(i - mine, 0)))] * pieces,
        [jax.ShapeDtypeStruct((piece, columns // 2), jnp.bfloat16)] * (2 * pieces),
    )


def elementwise(body, name, scalars, operands, out_rows):
    columns = operands[0].shape[1]
    tile = tile_of(columns, 256)
    column = lambda i, *_: (0, i)

    def kernel(*refs):
        scalar_refs = refs[: len(scalars)]
        ins = refs[len(scalars) : len(scalars) + len(operands)]
        outs = refs[len(scalars) + len(operands) :]
        for out, value in zip(outs, body(scalar_refs, ins)):
            out[...] = value

    return call(
        kernel,
        name,
        (columns // tile,),
        scalars,
        operands,
        [pl.BlockSpec((o.shape[0], tile), column) for o in operands],
        [pl.BlockSpec((r, tile), column) for r in out_rows],
        [jax.ShapeDtypeStruct((r, columns), jnp.bfloat16) for r in out_rows],
        vmem=SMALL_VMEM,
    )


def stacked(mine, arrived):
    rows = mine.shape[0]
    body = lambda _, ins: (jnp.concatenate([ins[0][...], ins[1][...]], 0),)
    return elementwise(body, "stacked", [], [mine, arrived], [2 * rows])[0]


def added(value, arrived):
    def body(_, ins):
        total = ins[0][...].astype(jnp.float32) + ins[1][...].astype(jnp.float32)
        return (total.astype(jnp.bfloat16),)

    return elementwise(body, "added", [], [value, arrived], [value.shape[0]])[0]


def activated(first, value, arrived):
    rows = value.shape[0] // 2

    def body(scalars, ins):
        is_first = scalars[0][0] == 1
        total = ins[0][...].astype(jnp.float32) + ins[1][...].astype(jnp.float32)
        above, below = total[:rows], total[rows:]
        v = jnp.where(is_first, above, below)
        grad = jnp.where(is_first, below, above)
        c = 0.7978845608028654
        t = jnp.tanh(c * (v + 0.044715 * (v * v * v)))
        hidden = (0.5 * v * (1.0 + t)).astype(jnp.bfloat16)
        slope = 0.5 * (1.0 + t) + 0.5 * v * (1.0 - t * t) * (c * (1.0 + 3.0 * 0.044715 * (v * v)))
        grad_preact = (grad * slope).astype(jnp.bfloat16)
        kept = jnp.where(is_first, grad_preact, hidden)
        sent = jnp.where(is_first, hidden, grad_preact)
        return (jnp.concatenate([kept, sent], 0),)

    return elementwise(body, "activated", [first], [value, arrived], [2 * rows])[0]


def chosen(receives, value, arrived, halves):
    rows = value.shape[0]

    def body(scalars, ins):
        result = jnp.where(scalars[0][0] == 1, ins[1][...], ins[0][...])
        return (result[: rows // 2], result[rows // 2 :]) if halves else (result,)

    out_rows = [rows // 2] * 2 if halves else [rows]
    return elementwise(body, "chosen", [receives], [value, arrived], out_rows)


def down_product(section, kept, came, weight, part, parts, before, group, arrived, kinds):
    counts = [k.shape[0] for k in kept]
    count, half = sum(counts), kept[0].shape[1]
    width = weight.shape[0]
    tile = tile_of(width, 1024)
    n = len(kept)
    extra = [] if before is None else [before]

    def kernel(section_ref, *refs):
        weight_ref = refs[2 * n]
        added = refs[2 * n + 1 : 2 * n + 1 + len(extra)]
        others = refs[2 * n + 1 + len(extra) : 2 * n + 1 + len(extra) + len(arrived)]
        results = refs[2 * n + 1 + len(extra) + len(arrived) : -1]
        held = refs[-1]

        @pl.when(pl.program_id(0) == 0)
        def _():
            mine = pl.ds(pl.multiple_of(section_ref[0] * half, half), half)
            theirs = pl.ds(pl.multiple_of((1 - section_ref[0]) * half, half), half)
            at = 0
            for i, rows in enumerate(counts):
                held[mine, at : at + rows] = refs[i][...].T
                held[theirs, at : at + rows] = refs[n + i][...].T
                at += rows

        for at in range(0, count, 256):
            own = slice(at, at + 256)
            product = dot_f32(weight_ref[...], held[:, own], (1, 0))
            for ref in added:
                product = product + ref[:, own]
            if kinds:
                product = product.T
                piece = count // len(kinds)
                for i, result in enumerate(results):
                    value = product[i * piece : (i + 1) * piece]
                    if arrived:
                        value = value + others[i][...].astype(jnp.float32)
                    result[...] = value.astype(result.dtype)
            else:
                results[0][:, own] = product

    whole = [fixed((rows, half), (0, 0)) for rows in counts]
    if kinds:
        piece_spec = pl.BlockSpec((count // len(kinds), tile), lambda i, s: (0, i))
        out_specs = [piece_spec] * len(kinds)
        out_shape = [jax.ShapeDtypeStruct((count // len(kinds), width), kind) for kind in kinds]
    else:
        out_specs = [pl.BlockSpec((tile, count), lambda i, s: (i, 0))]
        out_shape = [jax.ShapeDtypeStruct((width, count), jnp.float32)]
    return call(
        kernel,
        "down_product",
        (width // tile,),
        [section],
        [*kept, *came, weight, *extra, *arrived],
        whole
        + whole
        + [pl.BlockSpec((tile, 2 * half), lambda i, s: (i, part))]
        + [pl.BlockSpec((tile, count), lambda i, s: (i, group))] * len(extra)
        + [pl.BlockSpec((count // max(len(kinds), 1), tile), lambda i, s: (0, i))] * len(arrived),
        out_specs,
        out_shape,
        [pltpu.VMEM((2 * half, count), jnp.bfloat16)],
    )


def weight_gradient(section, turned, kept, came, part, parts, into):
    width, count = turned.shape
    counts = [k.shape[0] for k in kept]
    half = kept[0].shape[1]
    tile = tile_of(width, 1024)
    step = tile_of(2 * half, 256)
    n = len(kept)

    def kernel(section_ref, turned_ref, *refs):
        out, held = refs[-2:]

        @pl.when(pl.program_id(0) == 0)
        def _():
            mine = pl.ds(pl.multiple_of(section_ref[0] * half, half), half)
            theirs = pl.ds(pl.multiple_of((1 - section_ref[0]) * half, half), half)
            at = 0
            for i, rows in enumerate(counts):
                held[at : at + rows, mine] = refs[i][...]
                held[at : at + rows, theirs] = refs[n + i][...]
                at += rows

        for at in range(0, 2 * half, step):
            own = slice(at, at + step)
            out[:, own] = dot_f32(turned_ref[...], held[:, own], (1, 0)).astype(jnp.bfloat16)

    whole = [fixed((rows, half), (0, 0)) for rows in counts]
    extra = [] if into is None else [into]
    return call(
        kernel,
        "weight_gradient",
        (width // tile,),
        [section],
        [turned, *kept, *came, *extra],
        [pl.BlockSpec((tile, count), lambda i, s: (i, 0))]
        + whole
        + whole
        + [pl.BlockSpec(memory_space=pl.ANY)] * len(extra),
        pl.BlockSpec((tile, 2 * half), lambda i, s: (i, part)),
        jax.ShapeDtypeStruct((width, 2 * half * parts), jnp.bfloat16),
        [pltpu.VMEM((count, 2 * half), jnp.bfloat16)],
        {2 + 2 * n: 0} if extra else {},
    )


def transposed(value):
    count, width = value.shape
    tile = tile_of(width, 512)

    def kernel(value_ref, out):
        out[...] = value_ref[...].T

    return call(
        kernel,
        "transposed",
        (width // tile,),
        [],
        [value],
        [pl.BlockSpec((count, tile), lambda i: (0, i))],
        pl.BlockSpec((tile, count), lambda i: (i, 0)),
        jax.ShapeDtypeStruct((width, count), value.dtype),
        vmem=SMALL_VMEM,
    )


def from_peer(value, by):
    peers = lax.axis_size("mp")
    return lax.ppermute(value, "mp", [(i, i ^ by) for i in range(peers)])


def across_sections(value):
    return lax.ppermute(value, "section", [(0, 1), (1, 0)])


def local(tokens, weights, gain, cotangent):
    section = lax.axis_index("section").astype(jnp.int32).reshape(1)
    first = 1 - section
    weight = weights[0]
    peers = lax.axis_size("mp")
    line = lax.axis_size("dp")
    half = line // 2
    place = lax.axis_index("dp")
    rows = tokens.shape[0]
    each = peers // 4
    parts = 4 if weight.shape[1] % 1024 == 0 else 3

    last = []

    def run(work, anchor, *others):
        if last:
            held = last[-1]
            anchor, held["value"] = lax.optimization_barrier((anchor, held["value"]))
        held = {"value": work(anchor, *others)}
        last.append(held)
        return held

    receives = {
        hop: jnp.logical_or(place == hop, place == line - 1 - hop).astype(jnp.int32).reshape(1)
        for hop in range(half - 1)
    }
    tokens, section, first, receives = lax.optimization_barrier((tokens, section, first, receives))

    raw = run(lambda a, b: jnp.where(first[0] == 1, a, b), tokens, cotangent)["value"]
    across = peers // 2
    near = list(range(each, 2 * each)) + list(range(each))
    far = [by ^ across for by in near]
    gathered = {by: from_peer(raw, by) if by else raw for by in near}

    values = tokens.astype(jnp.float32)
    row_total, row_squares = lax.psum((jnp.sum(values, 1), jnp.sum(values * values, 1)), "dp")
    average = row_total / D
    inverse_std = lax.rsqrt(row_squares / D - average * average + epsilon)
    own_scale = jnp.stack([average, inverse_std], 1)
    near_scale = jnp.concatenate([from_peer(own_scale, by) if by else own_scale for by in near], 0)
    gathered[across] = from_peer(raw, across)
    gathered, near_scale = lax.optimization_barrier((gathered, near_scale))
    gathered.update({by: from_peer(gathered[by ^ across], across) for by in far if by != across})
    far_scale = from_peer(near_scale, across)

    def prepare(members, scale, group, into):
        blocks = [gathered[by] for by in members]
        return run(lambda g: normalize(first, blocks, scale, g, group, into), gain)["value"]

    chunks = {}

    def multiply(value, part, groups):
        products = run(lambda s: up_product(s, value, weight, part, parts, groups), section)
        for i, group in enumerate(groups):
            chunks[part, group] = {"products": products, "mine": i, "theirs": len(groups) + i}

    def stack(chunk):
        products = chunk["products"]
        arrived = across_sections(products["value"][chunk["theirs"]])
        chunk["sum"] = run(stacked, products["value"][chunk["mine"]], arrived)

    def inward(chunk):
        for hop in range(half - 1):
            value = chunk["sum"]["value"]
            arrived = lax.ppermute(value, "dp", [(hop, hop + 1), (line - 1 - hop, line - 2 - hop)])
            chunk["sum"] = run(added, value, arrived)

    def middle(chunk):
        value = chunk["sum"]["value"]
        arrived = lax.ppermute(value, "dp", [(half - 1, half), (half, half - 1)])
        chunk["result"] = run(lambda a, b: activated(first, a, b), value, arrived)

    def outward(chunk):
        for hop in reversed(range(half - 1)):
            value = chunk["result"]["value"]
            arrived = lax.ppermute(value, "dp", [(hop + 1, hop), (line - 2 - hop, line - 1 - hop)])
            if hop:
                chunk["result"] = run(lambda a, b: chosen(receives[hop], a, b, False)[0], value, arrived)
            else:
                chunk["halves"] = run(lambda a, b: chosen(receives[hop], a, b, True), value, arrived)

    def hidden(part, groups):
        kept = [chunks[part, g]["halves"]["value"][0] for g in groups]
        for g in groups:
            if "came" not in chunks[part, g]:
                chunks[part, g]["came"] = across_sections(chunks[part, g]["halves"]["value"][1])
        return kept, [chunks[part, g]["came"] for g in groups]

    both = (FAR, NEAR)
    order = [(0, NEAR)] + [(part, FAR) for part in range(parts)] + [(part, NEAR) for part in range(1, parts)]
    count = len(order)
    multiplied = {0}
    held = {"gradient": None}

    def need(c):
        if c < count and order[c][0] not in multiplied:
            multiplied.add(order[c][0])
            multiply(x_all, order[c][0], both)

    def tick(t):
        if 0 <= t - 1 < count:
            middle(chunks[order[t - 1]])
        if 0 <= t - 2 < count:
            outward(chunks[order[t - 2]])
        if 2 <= t + 2 < count:
            stack(chunks[order[t + 2]])

    def go_down(part, groups, before, column, kinds=(), arrived=()):
        kept, came = hidden(part, groups)
        before = None if before is None else before["value"][0]
        return run(
            lambda k: down_product(section, [k] + kept[1:], came, weight, part, parts, before, column, arrived, kinds),
            kept[0],
        )

    def go_gradient(part):
        kept, came = hidden(part, both)
        into = None if held["gradient"] is None else held["gradient"]["value"]
        held["gradient"] = run(
            lambda k: weight_gradient(section, turned, [k] + kept[1:], came, part, parts, into), kept[0]
        )

    x_near = prepare(near, near_scale, NEAR, None)
    multiply(x_near, 0, [NEAR])
    stack(chunks[order[0]])
    x_all = prepare(far, far_scale, FAR, x_near)
    multiply(x_all, 0, [FAR])
    stack(chunks[order[1]])
    for t in range(count + 2):
        if 0 <= t < count:
            inward(chunks[order[t]])
        if t == 0:
            need(2)
        tick(t)
        if t == 0:
            turned = run(transposed, x_all)["value"]
        need(t + 3)
        far_part, near_part = t - 3, t - 2 - parts
        if far_part == 0:
            near_sum = far_sum = go_down(0, both, None, 0)
        elif 0 < far_part < parts - 1:
            far_sum = go_down(far_part, [FAR], far_sum, FAR if far_part == 1 else 0)
            if far_part == 1:
                go_gradient(0)
        elif far_part == parts - 1:
            sent_far = go_down(far_part, [FAR], far_sum, FAR if far_part == 1 else 0, [jnp.bfloat16] * 2)
            arrived = [from_peer(value, across) for value in sent_far["value"]]
        elif 0 < near_part < parts - 1:
            go_gradient(near_part)
            near_sum = go_down(near_part, [NEAR], near_sum, NEAR if near_part == 1 else 0)
            if near_part == 1:
                near_sum["value"], arrived[0] = lax.optimization_barrier((near_sum["value"], arrived[0]))
    column = NEAR if parts == 2 else 0
    sent_near = go_down(parts - 1, [NEAR], near_sum, column, [jnp.bfloat16, jnp.float32], arrived)
    go_gradient(parts - 1)

    own = sent_near["value"][1]
    blocks = {0: own.astype(jnp.bfloat16), 1: sent_near["value"][0]}
    result = own[:rows]
    for by in range(1, across):
        at = (by % each) * rows
        result = result + from_peer(blocks[by // each][at : at + rows], by).astype(jnp.float32)
    return (result.astype(jnp.bfloat16)[None], held["gradient"]["value"][None])


def solution(mesh):
    placed = (P("mp", "dp"), P("section", "dp", "mp"), P("dp"), P("mp", "dp"))
    return jax.shard_map(
        local,
        mesh=mesh,
        in_specs=placed,
        out_specs=(P("section", "mp", "dp"), P("section", "dp", "mp")),
        check_vma=False,
    )
```

```python
import jax
import jax.numpy as jnp
from jax import lax
from jax.experimental import pallas as pl
from jax.experimental.pallas import tpu as pltpu
from jax.sharding import PartitionSpec as P

D = 12288
MATMUL_VMEM = 22 * 1024 * 1024
SMALL_VMEM = 8 * 1024 * 1024
FAR, NEAR = 0, 1


epsilon = 1e-05


def dot_f32(left, right, contract):
    return lax.dot_general(
        left, right, ((contract[:1], contract[1:]), ((), ())), preferred_element_type=jnp.float32
    )


def tile_of(extent, limit):
    return max(t for t in range(128, limit + 1, 128) if extent % t == 0)


def fixed(shape, index):
    return pl.BlockSpec(shape, lambda *_: index, pipeline_mode=pl.Buffered(1))


def call(kernel, name, grid, scalars, operands, in_specs, out_specs, out_shape, scratch=(), aliases={}, vmem=MATMUL_VMEM):
    return pl.pallas_call(
        kernel,
        grid_spec=pltpu.PrefetchScalarGridSpec(
            num_scalar_prefetch=len(scalars),
            grid=grid,
            in_specs=in_specs,
            out_specs=out_specs,
            scratch_shapes=list(scratch),
        ),
        out_shape=out_shape,
        input_output_aliases=aliases,
        compiler_params=pltpu.CompilerParams(vmem_limit_bytes=vmem),
        name=name,
    )(*scalars, *operands)


def normalize(first, blocks, scale, gain, group, into):
    rows, width = blocks[0].shape
    count = rows * len(blocks)
    tile = tile_of(width, 768)

    def kernel(first_ref, gain_ref, scale_ref, *refs):
        out = refs[-1]
        for i in range(len(blocks)):
            own = slice(i * rows, (i + 1) * rows)
            value = refs[i][...].astype(jnp.float32)
            centred = (value - scale_ref[own, 0:1]) * scale_ref[own, 1:2]
            normed = (centred * gain_ref[...]).astype(jnp.bfloat16)
            out[own, :] = jnp.where(first_ref[0] == 1, normed, refs[i][...])

    column = lambda i, _: (0, i)
    extra = [] if into is None else [into]
    return call(
        kernel,
        "normalize",
        (width // tile,),
        [first],
        [gain.reshape(1, width), scale, *blocks, *extra],
        [pl.BlockSpec((1, tile), column), fixed((count, 2), (0, 0))]
        + [pl.BlockSpec((rows, tile), column)] * len(blocks)
        + [pl.BlockSpec(memory_space=pl.ANY)] * len(extra),
        pl.BlockSpec((count, tile), lambda i, _: (group, i)),
        jax.ShapeDtypeStruct((2 * count, width), jnp.bfloat16),
        aliases={3 + len(blocks): 0} if extra else {},
        vmem=SMALL_VMEM,
    )


def up_product(section, rows, weight, part, parts, groups):
    pieces = len(groups)
    count, width = rows.shape[0] // 2 * pieces, rows.shape[1]
    at = groups[0]
    columns = weight.shape[1] // parts
    tile = columns // 2
    narrow = tile_of(tile, 256)
    copies = tile // narrow
    piece = count // pieces

    def kernel(section_ref, rows_ref, *refs):
        results = refs[copies:]
        for k in range(copies):
            own = slice(k * narrow, (k + 1) * narrow)
            product = dot_f32(rows_ref[...], refs[k][...], (1, 0)).astype(jnp.bfloat16)

            def store(refs):
                for i, result in enumerate(refs):
                    result[:, own] = product[i * piece : (i + 1) * piece]

            pl.when(pl.program_id(0) == 0)(lambda: store(results[:pieces]))
            pl.when(pl.program_id(0) == 1)(lambda: store(results[pieces:]))

    def column(k):
        return lambda i, s: (0, (2 * part + lax.rem(i + s[0], 2)) * copies + k)

    return call(
        kernel,
        "up_product",
        (2,),
        [section],
        [rows] + [weight] * copies,
        [
            fixed((count, width), (at, 0)),
            *[pl.BlockSpec((width, narrow), column(k)) for k in range(copies)],
        ],
        [fixed((piece, tile), (0, 0))] * (2 * pieces),
        [jax.ShapeDtypeStruct((piece, columns // 2), jnp.bfloat16)] * (2 * pieces),
    )


def elementwise(body, name, scalars, operands, out_rows):
    columns = operands[0].shape[1]
    tile = tile_of(columns, 256)
    column = lambda i, *_: (0, i)

    def kernel(*refs):
        scalar_refs = refs[: len(scalars)]
        ins = refs[len(scalars) : len(scalars) + len(operands)]
        outs = refs[len(scalars) + len(operands) :]
        for out, value in zip(outs, body(scalar_refs, ins)):
            out[...] = value

    return call(
        kernel,
        name,
        (columns // tile,),
        scalars,
        operands,
        [pl.BlockSpec((o.shape[0], tile), column) for o in operands],
        [pl.BlockSpec((r, tile), column) for r in out_rows],
        [jax.ShapeDtypeStruct((r, columns), jnp.bfloat16) for r in out_rows],
        vmem=SMALL_VMEM,
    )


def stacked(mine, arrived):
    rows = mine.shape[0]
    body = lambda _, ins: (jnp.concatenate([ins[0][...], ins[1][...]], 0),)
    return elementwise(body, "stacked", [], [mine, arrived], [2 * rows])[0]


def added(value, arrived):
    def body(_, ins):
        total = ins[0][...].astype(jnp.float32) + ins[1][...].astype(jnp.float32)
        return (total.astype(jnp.bfloat16),)

    return elementwise(body, "added", [], [value, arrived], [value.shape[0]])[0]


def activated(first, value, arrived):
    rows = value.shape[0] // 2

    def body(scalars, ins):
        is_first = scalars[0][0] == 1
        total = ins[0][...].astype(jnp.float32) + ins[1][...].astype(jnp.float32)
        above, below = total[:rows], total[rows:]
        v = jnp.where(is_first, above, below)
        grad = jnp.where(is_first, below, above)
        c = 0.7978845608028654
        t = jnp.tanh(c * (v + 0.044715 * (v * v * v)))
        hidden = (0.5 * v * (1.0 + t)).astype(jnp.bfloat16)
        slope = 0.5 * (1.0 + t) + 0.5 * v * (1.0 - t * t) * (c * (1.0 + 3.0 * 0.044715 * (v * v)))
        grad_preact = (grad * slope).astype(jnp.bfloat16)
        kept = jnp.where(is_first, grad_preact, hidden)
        sent = jnp.where(is_first, hidden, grad_preact)
        return (jnp.concatenate([kept, sent], 0),)

    return elementwise(body, "activated", [first], [value, arrived], [2 * rows])[0]


def chosen(receives, value, arrived, halves):
    rows = value.shape[0]

    def body(scalars, ins):
        result = jnp.where(scalars[0][0] == 1, ins[1][...], ins[0][...])
        return (result[: rows // 2], result[rows // 2 :]) if halves else (result,)

    out_rows = [rows // 2] * 2 if halves else [rows]
    return elementwise(body, "chosen", [receives], [value, arrived], out_rows)


def down_product(section, kept, came, weight, part, parts, before, group, arrived, kinds):
    counts = [k.shape[0] for k in kept]
    count, half = sum(counts), kept[0].shape[1]
    width = weight.shape[0]
    tile = tile_of(width, 1024)
    copies = 2 if tile % 256 == 0 else 1
    short = tile // copies
    n = len(kept)
    extra = [] if before is None else [before]

    def kernel(section_ref, *refs):
        weight_refs = refs[2 * n : 2 * n + copies]
        added = refs[2 * n + copies : 2 * n + copies + len(extra)]
        others = refs[2 * n + copies + len(extra) : 2 * n + copies + len(extra) + len(arrived)]
        results = refs[2 * n + copies + len(extra) + len(arrived) : -1]
        held = refs[-1]

        @pl.when(pl.program_id(0) == 0)
        def _():
            mine = pl.ds(pl.multiple_of(section_ref[0] * half, half), half)
            theirs = pl.ds(pl.multiple_of((1 - section_ref[0]) * half, half), half)
            at = 0
            for i, rows in enumerate(counts):
                held[mine, at : at + rows] = refs[i][...].T
                held[theirs, at : at + rows] = refs[n + i][...].T
                at += rows

        for k, at in [(k, at) for k in range(copies) for at in range(0, count, 256)]:
            there, own = slice(k * short, (k + 1) * short), slice(at, at + 256)
            product = dot_f32(weight_refs[k][...], held[:, own], (1, 0))
            for ref in added:
                product = product + ref[there, own]
            if kinds:
                product = product.T
                piece = count // len(kinds)
                for i, result in enumerate(results):
                    value = product[i * piece : (i + 1) * piece]
                    if arrived:
                        value = value + others[i][:, there].astype(jnp.float32)
                    result[:, there] = value.astype(result.dtype)
            else:
                results[0][there, own] = product

    whole = [fixed((rows, half), (0, 0)) for rows in counts]
    if kinds:
        piece_spec = pl.BlockSpec((count // len(kinds), tile), lambda i, s: (0, i))
        out_specs = [piece_spec] * len(kinds)
        out_shape = [jax.ShapeDtypeStruct((count // len(kinds), width), kind) for kind in kinds]
    else:
        out_specs = [pl.BlockSpec((tile, count), lambda i, s: (i, 0))]
        out_shape = [jax.ShapeDtypeStruct((width, count), jnp.float32)]
    return call(
        kernel,
        "down_product",
        (width // tile,),
        [section],
        [*kept, *came, *[weight] * copies, *extra, *arrived],
        whole
        + whole
        + [pl.BlockSpec((short, 2 * half), lambda i, s, k=k: (copies * i + k, part)) for k in range(copies)]
        + [pl.BlockSpec((tile, count), lambda i, s: (i, group))] * len(extra)
        + [pl.BlockSpec((count // max(len(kinds), 1), tile), lambda i, s: (0, i))] * len(arrived),
        out_specs,
        out_shape,
        [pltpu.VMEM((2 * half, count), jnp.bfloat16)],
    )


def weight_gradient(section, turned, kept, came, part, parts, into):
    width, count = turned.shape
    counts = [k.shape[0] for k in kept]
    half = kept[0].shape[1]
    tile = tile_of(width, 1024)
    step = tile_of(2 * half, 256)
    n = len(kept)

    def kernel(section_ref, turned_ref, *refs):
        out, held = refs[-2:]

        @pl.when(pl.program_id(0) == 0)
        def _():
            mine = pl.ds(pl.multiple_of(section_ref[0] * half, half), half)
            theirs = pl.ds(pl.multiple_of((1 - section_ref[0]) * half, half), half)
            at = 0
            for i, rows in enumerate(counts):
                held[at : at + rows, mine] = refs[i][...]
                held[at : at + rows, theirs] = refs[n + i][...]
                at += rows

        for at in range(0, 2 * half, step):
            own = slice(at, at + step)
            out[:, own] = dot_f32(turned_ref[...], held[:, own], (1, 0)).astype(jnp.bfloat16)

    whole = [fixed((rows, half), (0, 0)) for rows in counts]
    extra = [] if into is None else [into]
    return call(
        kernel,
        "weight_gradient",
        (width // tile,),
        [section],
        [turned, *kept, *came, *extra],
        [pl.BlockSpec((tile, count), lambda i, s: (i, 0))]
        + whole
        + whole
        + [pl.BlockSpec(memory_space=pl.ANY)] * len(extra),
        pl.BlockSpec((tile, 2 * half), lambda i, s: (i, part)),
        jax.ShapeDtypeStruct((width, 2 * half * parts), jnp.bfloat16),
        [pltpu.VMEM((count, 2 * half), jnp.bfloat16)],
        {2 + 2 * n: 0} if extra else {},
    )


def transposed(value):
    count, width = value.shape
    tile = tile_of(width, 512)

    def kernel(value_ref, out):
        out[...] = value_ref[...].T

    return call(
        kernel,
        "transposed",
        (width // tile,),
        [],
        [value],
        [pl.BlockSpec((count, tile), lambda i: (0, i))],
        pl.BlockSpec((tile, count), lambda i: (i, 0)),
        jax.ShapeDtypeStruct((width, count), value.dtype),
        vmem=SMALL_VMEM,
    )


def from_peer(value, by):
    peers = lax.axis_size("mp")
    return lax.ppermute(value, "mp", [(i, i ^ by) for i in range(peers)])


def across_sections(value):
    return lax.ppermute(value, "section", [(0, 1), (1, 0)])


def local(tokens, weights, gain, cotangent):
    section = lax.axis_index("section").astype(jnp.int32).reshape(1)
    first = 1 - section
    weight = weights[0]
    peers = lax.axis_size("mp")
    line = lax.axis_size("dp")
    half = line // 2
    place = lax.axis_index("dp")
    rows = tokens.shape[0]
    each = peers // 4
    parts = 4 if weight.shape[1] % 1024 == 0 else 3

    last = []

    def run(work, anchor, *others):
        if last:
            held = last[-1]
            anchor, held["value"] = lax.optimization_barrier((anchor, held["value"]))
        held = {"value": work(anchor, *others)}
        last.append(held)
        return held

    receives = {
        hop: jnp.logical_or(place == hop, place == line - 1 - hop).astype(jnp.int32).reshape(1)
        for hop in range(half - 1)
    }
    tokens, section, first, receives = lax.optimization_barrier((tokens, section, first, receives))

    raw = run(lambda a, b: jnp.where(first[0] == 1, a, b), tokens, cotangent)["value"]
    across = peers // 2
    near = list(range(each, 2 * each)) + list(range(each))
    far = [by ^ across for by in near]
    gathered = {by: from_peer(raw, by) if by else raw for by in near}

    values = tokens.astype(jnp.float32)
    row_total, row_squares = lax.psum((jnp.sum(values, 1), jnp.sum(values * values, 1)), "dp")
    average = row_total / D
    inverse_std = lax.rsqrt(row_squares / D - average * average + epsilon)
    own_scale = jnp.stack([average, inverse_std], 1)
    near_scale = jnp.concatenate([from_peer(own_scale, by) if by else own_scale for by in near], 0)
    gathered[across] = from_peer(raw, across)
    gathered, near_scale = lax.optimization_barrier((gathered, near_scale))
    gathered.update({by: from_peer(gathered[by ^ across], across) for by in far if by != across})
    far_scale = from_peer(near_scale, across)

    def prepare(members, scale, group, into):
        blocks = [gathered[by] for by in members]
        return run(lambda g: normalize(first, blocks, scale, g, group, into), gain)["value"]

    chunks = {}

    def multiply(value, part, groups):
        products = run(lambda s: up_product(s, value, weight, part, parts, groups), section)
        for i, group in enumerate(groups):
            chunks[part, group] = {"products": products, "mine": i, "theirs": len(groups) + i}

    def stack(chunk):
        products = chunk["products"]
        arrived = across_sections(products["value"][chunk["theirs"]])
        chunk["sum"] = run(stacked, products["value"][chunk["mine"]], arrived)

    def inward(chunk):
        for hop in range(half - 1):
            value = chunk["sum"]["value"]
            arrived = lax.ppermute(value, "dp", [(hop, hop + 1), (line - 1 - hop, line - 2 - hop)])
            chunk["sum"] = run(added, value, arrived)

    def middle(chunk):
        value = chunk["sum"]["value"]
        arrived = lax.ppermute(value, "dp", [(half - 1, half), (half, half - 1)])
        chunk["result"] = run(lambda a, b: activated(first, a, b), value, arrived)

    def outward(chunk):
        for hop in reversed(range(half - 1)):
            value = chunk["result"]["value"]
            arrived = lax.ppermute(value, "dp", [(hop + 1, hop), (line - 2 - hop, line - 1 - hop)])
            if hop:
                chunk["result"] = run(lambda a, b: chosen(receives[hop], a, b, False)[0], value, arrived)
            else:
                chunk["halves"] = run(lambda a, b: chosen(receives[hop], a, b, True), value, arrived)

    def hidden(part, groups):
        kept = [chunks[part, g]["halves"]["value"][0] for g in groups]
        for g in groups:
            if "came" not in chunks[part, g]:
                chunks[part, g]["came"] = across_sections(chunks[part, g]["halves"]["value"][1])
        return kept, [chunks[part, g]["came"] for g in groups]

    both = (FAR, NEAR)
    order = [(part, g) for part in (0, 1) for g in (NEAR, FAR)]
    order += [(part, g) for g in (FAR, NEAR) for part in range(2, parts)]
    count = len(order)
    held = {"gradient": None}

    def need(c):
        if c < count and order[c] not in chunks:
            part, group = order[c]
            multiply(x_all, part, [group] if part < 2 else both)

    def tick(t):
        if 0 <= t - 1 < count:
            middle(chunks[order[t - 1]])
        if 0 <= t - 2 < count:
            outward(chunks[order[t - 2]])
        if 2 <= t + 2 < count:
            stack(chunks[order[t + 2]])

    def go_down(part, groups, before, column, kinds=(), arrived=()):
        kept, came = hidden(part, groups)
        before = None if before is None else before["value"][0]
        return run(
            lambda k: down_product(section, [k] + kept[1:], came, weight, part, parts, before, column, arrived, kinds),
            kept[0],
        )

    def go_gradient(part):
        kept, came = hidden(part, both)
        into = None if held["gradient"] is None else held["gradient"]["value"]
        held["gradient"] = run(
            lambda k: weight_gradient(section, turned, [k] + kept[1:], came, part, parts, into), kept[0]
        )

    x_near = prepare(near, near_scale, NEAR, None)
    multiply(x_near, 0, [NEAR])
    stack(chunks[order[0]])
    multiply(x_near, 1, [NEAR])
    x_all = prepare(far, far_scale, FAR, x_near)
    multiply(x_all, 0, [FAR])
    inward(chunks[order[0]])
    stack(chunks[order[1]])
    for t in range(count + 2):
        if 0 < t < count:
            inward(chunks[order[t]])
        tick(t)
        need(t + 3)
        far_part, near_part = t - 4, t - 2 - parts
        if t == 3:
            turned = run(transposed, x_all)["value"]
            near_sum = go_down(0, both, None, 0)
        elif t == 4:
            go_gradient(0)
        elif t == 5:
            near_sum = far_sum = go_down(1, both, near_sum, 0)
        if 2 <= far_part < parts - 1:
            far_sum = go_down(far_part, [FAR], far_sum, FAR if far_part == 2 else 0)
        elif far_part == parts - 1:
            sent_far = go_down(far_part, [FAR], far_sum, FAR if far_part == 2 else 0, [jnp.bfloat16] * 2)
            arrived = [from_peer(value, across) for value in sent_far["value"]]
        if t == 6:
            go_gradient(1)
        if 2 <= near_part < parts - 1:
            go_gradient(near_part)
            near_sum = go_down(near_part, [NEAR], near_sum, NEAR if near_part == 2 else 0)
            near_sum["value"], arrived[0] = lax.optimization_barrier((near_sum["value"], arrived[0]))
    column = NEAR if parts == 3 else 0
    sent_near = go_down(parts - 1, [NEAR], near_sum, column, [jnp.bfloat16, jnp.float32], arrived)
    go_gradient(parts - 1)

    own = sent_near["value"][1]
    blocks = {0: own.astype(jnp.bfloat16), 1: sent_near["value"][0]}
    result = own[:rows]
    for by in range(1, across):
        at = (by % each) * rows
        result = result + from_peer(blocks[by // each][at : at + rows], by).astype(jnp.float32)
    return (result.astype(jnp.bfloat16)[None], held["gradient"]["value"][None])


def solution(mesh):
    placed = (P("mp", "dp"), P("section", "dp", "mp"), P("dp"), P("mp", "dp"))
    return jax.shard_map(
        local,
        mesh=mesh,
        in_specs=placed,
        out_specs=(P("section", "mp", "dp"), P("section", "dp", "mp")),
        check_vma=False,
    )
```

```python
import jax
import jax.numpy as jnp
from jax import lax
from jax.experimental import pallas as pl
from jax.experimental.pallas import tpu as pltpu
from jax.sharding import PartitionSpec as P

D = 12288
MATMUL_VMEM = 22 * 1024 * 1024
SMALL_VMEM = 8 * 1024 * 1024
FAR, NEAR = 0, 1


epsilon = 1e-05


def dot_f32(left, right, contract):
    return lax.dot_general(
        left, right, ((contract[:1], contract[1:]), ((), ())), preferred_element_type=jnp.float32
    )


def tile_of(extent, limit):
    return max(t for t in range(128, limit + 1, 128) if extent % t == 0)


def fixed(shape, index):
    return pl.BlockSpec(shape, lambda *_: index, pipeline_mode=pl.Buffered(1))


def call(kernel, name, grid, scalars, operands, in_specs, out_specs, out_shape, scratch=(), aliases={}, vmem=MATMUL_VMEM):
    return pl.pallas_call(
        kernel,
        grid_spec=pltpu.PrefetchScalarGridSpec(
            num_scalar_prefetch=len(scalars),
            grid=grid,
            in_specs=in_specs,
            out_specs=out_specs,
            scratch_shapes=list(scratch),
        ),
        out_shape=out_shape,
        input_output_aliases=aliases,
        compiler_params=pltpu.CompilerParams(vmem_limit_bytes=vmem),
        name=name,
    )(*scalars, *operands)


def normalize(first, blocks, scale, gain, group, into):
    rows, width = blocks[0].shape
    count = rows * len(blocks)
    tile = tile_of(width, 768)

    def kernel(first_ref, gain_ref, scale_ref, *refs):
        out = refs[-1]
        for i in range(len(blocks)):
            own = slice(i * rows, (i + 1) * rows)
            value = refs[i][...].astype(jnp.float32)
            centred = (value - scale_ref[own, 0:1]) * scale_ref[own, 1:2]
            normed = (centred * gain_ref[...]).astype(jnp.bfloat16)
            out[own, :] = jnp.where(first_ref[0] == 1, normed, refs[i][...])

    column = lambda i, _: (0, i)
    extra = [] if into is None else [into]
    return call(
        kernel,
        "normalize",
        (width // tile,),
        [first],
        [gain.reshape(1, width), scale, *blocks, *extra],
        [pl.BlockSpec((1, tile), column), fixed((count, 2), (0, 0))]
        + [pl.BlockSpec((rows, tile), column)] * len(blocks)
        + [pl.BlockSpec(memory_space=pl.ANY)] * len(extra),
        pl.BlockSpec((count, tile), lambda i, _: (group, i)),
        jax.ShapeDtypeStruct((2 * count, width), jnp.bfloat16),
        aliases={3 + len(blocks): 0} if extra else {},
        vmem=SMALL_VMEM,
    )


def up_product(section, rows, weight, part, parts, groups):
    pieces = len(groups)
    count, width = rows.shape[0] // 2 * pieces, rows.shape[1]
    at = groups[0]
    columns = weight.shape[1] // parts
    tile = tile_of(columns // 2, 768)
    steps = columns // tile
    mine = steps // 2
    piece = count // pieces

    def kernel(section_ref, rows_ref, weight_ref, *results):
        product = dot_f32(rows_ref[...], weight_ref[...], (1, 0)).astype(jnp.bfloat16)

        def store(refs):
            for i, result in enumerate(refs):
                result[...] = product[i * piece : (i + 1) * piece]

        pl.when(pl.program_id(0) < mine)(lambda: store(results[:pieces]))
        pl.when(pl.program_id(0) >= mine)(lambda: store(results[pieces:]))

    return call(
        kernel,
        "up_product",
        (steps,),
        [section],
        [rows, weight],
        [
            fixed((count, width), (at, 0)),
            pl.BlockSpec((width, tile), lambda i, s: (0, part * steps + lax.rem(i + s[0] * mine, steps))),
        ],
        [pl.BlockSpec((piece, tile), lambda i, s: (0, jnp.minimum(i, mine - 1)))] * pieces
        + [pl.BlockSpec((piece, tile), lambda i, s: (0, jnp.maximum(i - mine, 0)))] * pieces,
        [jax.ShapeDtypeStruct((piece, columns // 2), jnp.bfloat16)] * (2 * pieces),
    )


def elementwise(body, name, scalars, operands, out_rows):
    columns = operands[0].shape[1]
    tile = tile_of(columns, 256)
    column = lambda i, *_: (0, i)

    def kernel(*refs):
        scalar_refs = refs[: len(scalars)]
        ins = refs[len(scalars) : len(scalars) + len(operands)]
        outs = refs[len(scalars) + len(operands) :]
        for out, value in zip(outs, body(scalar_refs, ins)):
            out[...] = value

    return call(
        kernel,
        name,
        (columns // tile,),
        scalars,
        operands,
        [pl.BlockSpec((o.shape[0], tile), column) for o in operands],
        [pl.BlockSpec((r, tile), column) for r in out_rows],
        [jax.ShapeDtypeStruct((r, columns), jnp.bfloat16) for r in out_rows],
        vmem=SMALL_VMEM,
    )


def stacked(mine, arrived):
    rows = mine.shape[0]
    body = lambda _, ins: (jnp.concatenate([ins[0][...], ins[1][...]], 0),)
    return elementwise(body, "stacked", [], [mine, arrived], [2 * rows])[0]


def added(value, arrived):
    def body(_, ins):
        total = ins[0][...].astype(jnp.float32) + ins[1][...].astype(jnp.float32)
        return (total.astype(jnp.bfloat16),)

    return elementwise(body, "added", [], [value, arrived], [value.shape[0]])[0]


def activated(first, value, arrived):
    rows = value.shape[0] // 2

    def body(scalars, ins):
        is_first = scalars[0][0] == 1
        total = ins[0][...].astype(jnp.float32) + ins[1][...].astype(jnp.float32)
        above, below = total[:rows], total[rows:]
        v = jnp.where(is_first, above, below)
        grad = jnp.where(is_first, below, above)
        c = 0.7978845608028654
        t = jnp.tanh(c * (v + 0.044715 * (v * v * v)))
        hidden = (0.5 * v * (1.0 + t)).astype(jnp.bfloat16)
        slope = 0.5 * (1.0 + t) + 0.5 * v * (1.0 - t * t) * (c * (1.0 + 3.0 * 0.044715 * (v * v)))
        grad_preact = (grad * slope).astype(jnp.bfloat16)
        kept = jnp.where(is_first, grad_preact, hidden)
        sent = jnp.where(is_first, hidden, grad_preact)
        return (jnp.concatenate([kept, sent], 0),)

    return elementwise(body, "activated", [first], [value, arrived], [2 * rows])[0]


def chosen(receives, value, arrived, halves):
    rows = value.shape[0]

    def body(scalars, ins):
        result = jnp.where(scalars[0][0] == 1, ins[1][...], ins[0][...])
        return (result[: rows // 2], result[rows // 2 :]) if halves else (result,)

    out_rows = [rows // 2] * 2 if halves else [rows]
    return elementwise(body, "chosen", [receives], [value, arrived], out_rows)


def down_product(section, kept, came, weight, part, parts, before, group, arrived, kinds):
    counts = [k.shape[0] for k in kept]
    count, half = sum(counts), kept[0].shape[1]
    width = weight.shape[0]
    tile = tile_of(width, 1024)
    n = len(kept)
    extra = [] if before is None else [before]
    others = list(arrived)

    def kernel(section_ref, *refs):
        weight_ref = refs[2 * n]
        added = refs[2 * n + 1 : 2 * n + 1 + len(extra)]
        arrived_refs = refs[2 * n + 1 + len(extra) : 2 * n + 1 + len(extra) + len(others)]
        results = refs[2 * n + 1 + len(extra) + len(others) : -1]
        held = refs[-1]

        @pl.when(pl.program_id(0) == 0)
        def _():
            mine = pl.ds(pl.multiple_of(section_ref[0] * half, half), half)
            theirs = pl.ds(pl.multiple_of((1 - section_ref[0]) * half, half), half)
            at = 0
            for i, rows in enumerate(counts):
                held[mine, at : at + rows] = refs[i][...].T
                held[theirs, at : at + rows] = refs[n + i][...].T
                at += rows

        product = dot_f32(weight_ref[...], held[...], (1, 0))
        for ref in added:
            product = product + ref[...]
        if kinds:
            product = product.T
            piece = count // len(kinds)
            for i, result in enumerate(results):
                value = product[i * piece : (i + 1) * piece]
                if others:
                    value = value + arrived_refs[i][...].astype(jnp.float32)
                result[...] = value.astype(result.dtype)
        else:
            results[0][...] = product

    whole = [fixed((rows, half), (0, 0)) for rows in counts]
    if kinds:
        out_specs = [pl.BlockSpec((count // len(kinds), tile), lambda i, s: (0, i))] * len(kinds)
        out_shape = [jax.ShapeDtypeStruct((count // len(kinds), width), kind) for kind in kinds]
    else:
        out_specs = [pl.BlockSpec((tile, count), lambda i, s: (i, 0))]
        out_shape = [jax.ShapeDtypeStruct((width, count), jnp.float32)]
    return call(
        kernel,
        "down_product",
        (width // tile,),
        [section],
        [*kept, *came, weight, *extra, *others],
        whole
        + whole
        + [pl.BlockSpec((tile, 2 * half), lambda i, s: (i, part))]
        + [pl.BlockSpec((tile, count), lambda i, s: (i, group))] * len(extra)
        + [pl.BlockSpec((count // max(len(kinds), 1), tile), lambda i, s: (0, i))] * len(others),
        out_specs,
        out_shape,
        [pltpu.VMEM((2 * half, count), jnp.bfloat16)],
    )


def weight_gradient(section, turned, kept, came, part, parts, into):
    width, count = turned.shape
    counts = [k.shape[0] for k in kept]
    half = kept[0].shape[1]
    tile = tile_of(width, 1024)
    step = half
    n = len(kept)

    def kernel(section_ref, turned_ref, *refs):
        out, held = refs[-2:]

        @pl.when(pl.program_id(0) == 0)
        def _():
            mine = pl.ds(pl.multiple_of(section_ref[0] * half, half), half)
            theirs = pl.ds(pl.multiple_of((1 - section_ref[0]) * half, half), half)
            at = 0
            for i, rows in enumerate(counts):
                held[at : at + rows, mine] = refs[i][...]
                held[at : at + rows, theirs] = refs[n + i][...]
                at += rows

        for at in range(0, 2 * half, step):
            own = slice(at, at + step)
            out[:, own] = dot_f32(turned_ref[...], held[:, own], (1, 0)).astype(jnp.bfloat16)

    whole = [fixed((rows, half), (0, 0)) for rows in counts]
    extra = [] if into is None else [into]
    return call(
        kernel,
        "weight_gradient",
        (width // tile,),
        [section],
        [turned, *kept, *came, *extra],
        [pl.BlockSpec((tile, count), lambda i, s: (i, 0))]
        + whole
        + whole
        + [pl.BlockSpec(memory_space=pl.ANY)] * len(extra),
        pl.BlockSpec((tile, 2 * half), lambda i, s: (i, part)),
        jax.ShapeDtypeStruct((width, 2 * half * parts), jnp.bfloat16),
        [pltpu.VMEM((count, 2 * half), jnp.bfloat16)],
        {2 + 2 * n: 0} if extra else {},
    )


def transposed(value):
    count, width = value.shape
    tile = tile_of(width, 512)

    def kernel(value_ref, out):
        out[...] = value_ref[...].T

    return call(
        kernel,
        "transposed",
        (width // tile,),
        [],
        [value],
        [pl.BlockSpec((count, tile), lambda i: (0, i))],
        pl.BlockSpec((tile, count), lambda i: (i, 0)),
        jax.ShapeDtypeStruct((width, count), value.dtype),
        vmem=SMALL_VMEM,
    )


def from_peer(value, by):
    peers = lax.axis_size("mp")
    return lax.ppermute(value, "mp", [(i, i ^ by) for i in range(peers)])


def across_sections(value):
    return lax.ppermute(value, "section", [(0, 1), (1, 0)])


def local(tokens, weights, gain, cotangent):
    section = lax.axis_index("section").astype(jnp.int32).reshape(1)
    first = 1 - section
    weight = weights[0]
    peers = lax.axis_size("mp")
    line = lax.axis_size("dp")
    half = line // 2
    place = lax.axis_index("dp")
    rows = tokens.shape[0]
    each = peers // 4
    parts = 4 if weight.shape[1] % 1024 == 0 else 3

    last = []

    def run(work, anchor, *others):
        if last:
            held = last[-1]
            anchor, held["value"] = lax.optimization_barrier((anchor, held["value"]))
        held = {"value": work(anchor, *others)}
        last.append(held)
        return held

    receives = {
        hop: jnp.logical_or(place == hop, place == line - 1 - hop).astype(jnp.int32).reshape(1)
        for hop in range(half - 1)
    }
    tokens, section, first, receives = lax.optimization_barrier((tokens, section, first, receives))

    raw = run(lambda a, b: jnp.where(first[0] == 1, a, b), tokens, cotangent)["value"]
    across = peers // 2
    near = list(range(each, 2 * each)) + list(range(each))
    far = [by ^ across for by in near]
    gathered = {by: from_peer(raw, by) if by else raw for by in near}

    values = tokens.astype(jnp.float32)
    row_total, row_squares = lax.psum((jnp.sum(values, 1), jnp.sum(values * values, 1)), "dp")
    average = row_total / D
    inverse_std = lax.rsqrt(row_squares / D - average * average + epsilon)
    own_scale = jnp.stack([average, inverse_std], 1)
    near_scale = jnp.concatenate([from_peer(own_scale, by) if by else own_scale for by in near], 0)
    gathered[across] = from_peer(raw, across)
    gathered, near_scale = lax.optimization_barrier((gathered, near_scale))
    gathered.update({by: from_peer(gathered[by ^ across], across) for by in far if by != across})
    far_scale = from_peer(near_scale, across)

    def prepare(members, scale, group, into):
        blocks = [gathered[by] for by in members]
        return run(lambda g: normalize(first, blocks, scale, g, group, into), gain)["value"]

    chunks = {}

    def multiply(value, part, groups):
        products = run(lambda s: up_product(s, value, weight, part, parts, groups), section)
        for i, group in enumerate(groups):
            chunks[part, group] = {"products": products, "mine": i, "theirs": len(groups) + i}

    def stack(chunk):
        products = chunk["products"]
        arrived = across_sections(products["value"][chunk["theirs"]])
        chunk["sum"] = run(stacked, products["value"][chunk["mine"]], arrived)

    def inward(chunk):
        for hop in range(half - 1):
            value = chunk["sum"]["value"]
            arrived = lax.ppermute(value, "dp", [(hop, hop + 1), (line - 1 - hop, line - 2 - hop)])
            chunk["sum"] = run(added, value, arrived)

    def middle(chunk):
        value = chunk["sum"]["value"]
        arrived = lax.ppermute(value, "dp", [(half - 1, half), (half, half - 1)])
        chunk["result"] = run(lambda a, b: activated(first, a, b), value, arrived)

    def outward(chunk):
        for hop in reversed(range(half - 1)):
            value = chunk["result"]["value"]
            arrived = lax.ppermute(value, "dp", [(hop + 1, hop), (line - 2 - hop, line - 1 - hop)])
            if hop:
                chunk["result"] = run(lambda a, b: chosen(receives[hop], a, b, False)[0], value, arrived)
            else:
                chunk["halves"] = run(lambda a, b: chosen(receives[hop], a, b, True), value, arrived)

    def hidden(part, groups):
        kept = [chunks[part, g]["halves"]["value"][0] for g in groups]
        for g in groups:
            if "came" not in chunks[part, g]:
                chunks[part, g]["came"] = across_sections(chunks[part, g]["halves"]["value"][1])
        return kept, [chunks[part, g]["came"] for g in groups]

    both = (FAR, NEAR)
    order = [(part, g) for part in (0, 1) for g in (NEAR, FAR)]
    order += [(part, g) for g in (FAR, NEAR) for part in range(2, parts)]
    count = len(order)
    held = {"gradient": None}

    def need(c):
        if c < count and order[c] not in chunks:
            part, group = order[c]
            multiply(x_all, part, [group] if part < 2 else both)

    def tick(t):
        if 0 <= t - 1 < count:
            middle(chunks[order[t - 1]])
        if 0 <= t - 2 < count:
            outward(chunks[order[t - 2]])
        if 2 <= t + 2 < count:
            stack(chunks[order[t + 2]])

    def go_down(part, groups, before, column, kinds=(), arrived=()):
        kept, came = hidden(part, groups)
        before = None if before is None else before["value"][0]
        return run(
            lambda k: down_product(section, [k] + kept[1:], came, weight, part, parts, before, column, arrived, kinds),
            kept[0],
        )

    def go_gradient(part):
        kept, came = hidden(part, both)
        into = None if held["gradient"] is None else held["gradient"]["value"]
        held["gradient"] = run(
            lambda k: weight_gradient(section, turned, [k] + kept[1:], came, part, parts, into), kept[0]
        )

    x_near = prepare(near, near_scale, NEAR, None)
    multiply(x_near, 0, [NEAR])
    stack(chunks[order[0]])
    multiply(x_near, 1, [NEAR])
    x_all = prepare(far, far_scale, FAR, x_near)
    multiply(x_all, 0, [FAR])
    inward(chunks[order[0]])
    stack(chunks[order[1]])
    for t in range(count + 2):
        if 0 < t < count:
            inward(chunks[order[t]])
        tick(t)
        need(t + 3)
        far_part, near_part = t - 4, t - 2 - parts
        if t == 3:
            turned = run(transposed, x_all)["value"]
            near_sum = go_down(0, both, None, 0)
        elif t == 4:
            hidden(1, [NEAR])
            kept = chunks[0, NEAR]["halves"]
            waited = chunks[1, NEAR]
            kept["value"], waited["came"] = lax.optimization_barrier((kept["value"], waited["came"]))
            go_gradient(0)
        elif t == 5:
            near_sum = far_sum = go_down(1, both, near_sum, 0)
        if 2 <= far_part < parts - 1:
            far_sum = go_down(far_part, [FAR], far_sum, FAR if far_part == 2 else 0)
        elif far_part == parts - 1:
            sent_far = go_down(far_part, [FAR], far_sum, FAR if far_part == 2 else 0, [jnp.bfloat16] * 2)
            arrived = [from_peer(value, across) for value in sent_far["value"]]
        if t == 6:
            go_gradient(1)
        if 2 <= near_part < parts - 1:
            go_gradient(near_part)
            near_sum = go_down(near_part, [NEAR], near_sum, NEAR if near_part == 2 else 0)
            near_sum["value"], arrived = lax.optimization_barrier((near_sum["value"], arrived))
    column = NEAR if parts == 3 else 0
    sent_near = go_down(parts - 1, [NEAR], near_sum, column, [jnp.bfloat16, jnp.float32], arrived)
    go_gradient(parts - 1)

    own = sent_near["value"][1]
    blocks = {0: own.astype(jnp.bfloat16), 1: sent_near["value"][0]}
    result = own[:rows]
    for by in range(1, across):
        at = (by % each) * rows
        result = result + from_peer(blocks[by // each][at : at + rows], by).astype(jnp.float32)
    return (result.astype(jnp.bfloat16)[None], held["gradient"]["value"][None])


def solution(mesh):
    placed = (P("mp", "dp"), P("section", "dp", "mp"), P("dp"), P("mp", "dp"))
    return jax.shard_map(
        local,
        mesh=mesh,
        in_specs=placed,
        out_specs=(P("section", "mp", "dp"), P("section", "dp", "mp")),
        check_vma=False,
    )
```

```python
import jax
import jax.numpy as jnp
from jax import lax
from jax.experimental import pallas as pl
from jax.experimental.pallas import tpu as pltpu
from jax.sharding import PartitionSpec as P

D = 12288
MATMUL_VMEM = 22 * 1024 * 1024
SMALL_VMEM = 8 * 1024 * 1024
FAR, NEAR, PEER, OWN = (0, 2), (2, 2), (2, 1), (3, 1)


epsilon = 1e-05


def dot_f32(left, right, contract):
    return lax.dot_general(
        left, right, ((contract[:1], contract[1:]), ((), ())), preferred_element_type=jnp.float32
    )


def tile_of(extent, limit):
    return max(t for t in range(128, limit + 1, 128) if extent % t == 0)


def fixed(shape, index):
    return pl.BlockSpec(shape, lambda *_: index, pipeline_mode=pl.Buffered(1))


def call(kernel, name, grid, scalars, operands, in_specs, out_specs, out_shape, scratch=(), aliases={}, vmem=MATMUL_VMEM):
    return pl.pallas_call(
        kernel,
        grid_spec=pltpu.PrefetchScalarGridSpec(
            num_scalar_prefetch=len(scalars),
            grid=grid,
            in_specs=in_specs,
            out_specs=out_specs,
            scratch_shapes=list(scratch),
        ),
        out_shape=out_shape,
        input_output_aliases=aliases,
        compiler_params=pltpu.CompilerParams(vmem_limit_bytes=vmem),
        name=name,
    )(*scalars, *operands)


def normalize(first, blocks, scale, gain, group, into):
    rows, width = blocks[0].shape
    count = rows * len(blocks)
    tile = tile_of(width, 768)

    def kernel(first_ref, gain_ref, scale_ref, *refs):
        out = refs[-1]
        for i in range(len(blocks)):
            own = slice(i * rows, (i + 1) * rows)
            value = refs[i][...].astype(jnp.float32)
            centred = (value - scale_ref[own, 0:1]) * scale_ref[own, 1:2]
            normed = (centred * gain_ref[...]).astype(jnp.bfloat16)
            out[own, :] = jnp.where(first_ref[0] == 1, normed, refs[i][...])

    column = lambda i, _: (0, i)
    extra = [] if into is None else [into]
    return call(
        kernel,
        "normalize",
        (width // tile,),
        [first],
        [gain.reshape(1, width), scale, *blocks, *extra],
        [pl.BlockSpec((1, tile), column), fixed((count, 2), (0, 0))]
        + [pl.BlockSpec((rows, tile), column)] * len(blocks)
        + [pl.BlockSpec(memory_space=pl.ANY)] * len(extra),
        pl.BlockSpec((count, tile), lambda i, _: (group[0] // group[1], i)),
        jax.ShapeDtypeStruct((2 * count, width), jnp.bfloat16),
        aliases={3 + len(blocks): 0} if extra else {},
        vmem=SMALL_VMEM,
    )


def up_product(section, rows, weight, part, parts, groups):
    pieces = len(groups)
    quarter, width = rows.shape[0] // 4, rows.shape[1]
    total = sum(group[1] for group in groups)
    count, at = quarter * total, groups[0][0] // total
    places = [((g[0] - groups[0][0]) * quarter, g[1] * quarter) for g in groups]
    columns = weight.shape[1] // parts
    tile = tile_of(columns // 2, 768)
    steps = columns // tile
    mine = steps // 2

    def kernel(section_ref, rows_ref, weight_ref, *results):
        product = dot_f32(rows_ref[...], weight_ref[...], (1, 0)).astype(jnp.bfloat16)

        def store(refs):
            for (first, size), result in zip(places, refs):
                result[...] = product[first : first + size]

        pl.when(pl.program_id(0) < mine)(lambda: store(results[:pieces]))
        pl.when(pl.program_id(0) >= mine)(lambda: store(results[pieces:]))

    return call(
        kernel,
        "up_product",
        (steps,),
        [section],
        [rows, weight],
        [
            fixed((count, width), (at, 0)),
            pl.BlockSpec((width, tile), lambda i, s: (0, part * steps + lax.rem(i + s[0] * mine, steps))),
        ],
        [pl.BlockSpec((size, tile), lambda i, s: (0, jnp.minimum(i, mine - 1))) for _, size in places]
        + [pl.BlockSpec((size, tile), lambda i, s: (0, jnp.maximum(i - mine, 0))) for _, size in places],
        [jax.ShapeDtypeStruct((size, columns // 2), jnp.bfloat16) for _, size in places] * 2,
    )


def elementwise(body, name, scalars, operands, out_rows):
    columns = operands[0].shape[1]
    tile = tile_of(columns, 256)
    column = lambda i, *_: (0, i)

    def kernel(*refs):
        scalar_refs = refs[: len(scalars)]
        ins = refs[len(scalars) : len(scalars) + len(operands)]
        outs = refs[len(scalars) + len(operands) :]
        for out, value in zip(outs, body(scalar_refs, ins)):
            out[...] = value

    return call(
        kernel,
        name,
        (columns // tile,),
        scalars,
        operands,
        [pl.BlockSpec((o.shape[0], tile), column) for o in operands],
        [pl.BlockSpec((r, tile), column) for r in out_rows],
        [jax.ShapeDtypeStruct((r, columns), jnp.bfloat16) for r in out_rows],
        vmem=SMALL_VMEM,
    )


def stacked(mine, arrived):
    rows = mine.shape[0]
    body = lambda _, ins: (jnp.concatenate([ins[0][...], ins[1][...]], 0),)
    return elementwise(body, "stacked", [], [mine, arrived], [2 * rows])[0]


def added(value, arrived):
    def body(_, ins):
        total = ins[0][...].astype(jnp.float32) + ins[1][...].astype(jnp.float32)
        return (total.astype(jnp.bfloat16),)

    return elementwise(body, "added", [], [value, arrived], [value.shape[0]])[0]


def activated(first, value, arrived):
    rows = value.shape[0] // 2

    def body(scalars, ins):
        is_first = scalars[0][0] == 1
        total = ins[0][...].astype(jnp.float32) + ins[1][...].astype(jnp.float32)
        above, below = total[:rows], total[rows:]
        v = jnp.where(is_first, above, below)
        grad = jnp.where(is_first, below, above)
        c = 0.7978845608028654
        t = jnp.tanh(c * (v + 0.044715 * (v * v * v)))
        hidden = (0.5 * v * (1.0 + t)).astype(jnp.bfloat16)
        slope = 0.5 * (1.0 + t) + 0.5 * v * (1.0 - t * t) * (c * (1.0 + 3.0 * 0.044715 * (v * v)))
        grad_preact = (grad * slope).astype(jnp.bfloat16)
        kept = jnp.where(is_first, grad_preact, hidden)
        sent = jnp.where(is_first, hidden, grad_preact)
        return (jnp.concatenate([kept, sent], 0),)

    return elementwise(body, "activated", [first], [value, arrived], [2 * rows])[0]


def chosen(receives, value, arrived, halves):
    rows = value.shape[0]

    def body(scalars, ins):
        result = jnp.where(scalars[0][0] == 1, ins[1][...], ins[0][...])
        return (result[: rows // 2], result[rows // 2 :]) if halves else (result,)

    out_rows = [rows // 2] * 2 if halves else [rows]
    return elementwise(body, "chosen", [receives], [value, arrived], out_rows)


def down_product(section, kept, came, weight, part, parts, before, group, arrived, kinds):
    counts = [k.shape[0] for k in kept]
    count, half = sum(counts), kept[0].shape[1]
    width = weight.shape[0]
    tile = tile_of(width, 1024)
    n = len(kept)
    extra = [] if before is None else [before]
    others = list(arrived)

    def kernel(section_ref, *refs):
        weight_ref = refs[2 * n]
        added = refs[2 * n + 1 : 2 * n + 1 + len(extra)]
        arrived_refs = refs[2 * n + 1 + len(extra) : 2 * n + 1 + len(extra) + len(others)]
        results = refs[2 * n + 1 + len(extra) + len(others) : -1]
        held = refs[-1]

        @pl.when(pl.program_id(0) == 0)
        def _():
            mine = pl.ds(pl.multiple_of(section_ref[0] * half, half), half)
            theirs = pl.ds(pl.multiple_of((1 - section_ref[0]) * half, half), half)
            at = 0
            for i, rows in enumerate(counts):
                held[mine, at : at + rows] = refs[i][...].T
                held[theirs, at : at + rows] = refs[n + i][...].T
                at += rows

        product = dot_f32(weight_ref[...], held[...], (1, 0))
        for ref in added:
            product = product + ref[...]
        if kinds:
            product = product.T
            piece = count // len(kinds)
            for i, result in enumerate(results):
                value = product[i * piece : (i + 1) * piece]
                if others:
                    value = value + arrived_refs[i][...].astype(jnp.float32)
                result[...] = value.astype(result.dtype)
        else:
            results[0][...] = product

    whole = [fixed((rows, half), (0, 0)) for rows in counts]
    if kinds:
        out_specs = [pl.BlockSpec((count // len(kinds), tile), lambda i, s: (0, i))] * len(kinds)
        out_shape = [jax.ShapeDtypeStruct((count // len(kinds), width), kind) for kind in kinds]
    else:
        out_specs = [pl.BlockSpec((tile, count), lambda i, s: (i, 0))]
        out_shape = [jax.ShapeDtypeStruct((width, count), jnp.float32)]
    return call(
        kernel,
        "down_product",
        (width // tile,),
        [section],
        [*kept, *came, weight, *extra, *others],
        whole
        + whole
        + [pl.BlockSpec((tile, 2 * half), lambda i, s: (i, part))]
        + [pl.BlockSpec((tile, count), lambda i, s: (i, group))] * len(extra)
        + [pl.BlockSpec((count // max(len(kinds), 1), tile), lambda i, s: (0, i))] * len(others),
        out_specs,
        out_shape,
        [pltpu.VMEM((2 * half, count), jnp.bfloat16)],
    )


def weight_gradient(section, turned, kept, came, part, parts, into):
    width, count = turned.shape
    counts = [k.shape[0] for k in kept]
    half = kept[0].shape[1]
    tile = tile_of(width, 1024)
    step = half
    n = len(kept)

    def kernel(section_ref, turned_ref, *refs):
        out, held = refs[-2:]

        @pl.when(pl.program_id(0) == 0)
        def _():
            mine = pl.ds(pl.multiple_of(section_ref[0] * half, half), half)
            theirs = pl.ds(pl.multiple_of((1 - section_ref[0]) * half, half), half)
            at = 0
            for i, rows in enumerate(counts):
                held[at : at + rows, mine] = refs[i][...]
                held[at : at + rows, theirs] = refs[n + i][...]
                at += rows

        for at in range(0, 2 * half, step):
            own = slice(at, at + step)
            out[:, own] = dot_f32(turned_ref[...], held[:, own], (1, 0)).astype(jnp.bfloat16)

    whole = [fixed((rows, half), (0, 0)) for rows in counts]
    extra = [] if into is None else [into]
    return call(
        kernel,
        "weight_gradient",
        (width // tile,),
        [section],
        [turned, *kept, *came, *extra],
        [pl.BlockSpec((tile, count), lambda i, s: (i, 0))]
        + whole
        + whole
        + [pl.BlockSpec(memory_space=pl.ANY)] * len(extra),
        pl.BlockSpec((tile, 2 * half), lambda i, s: (i, part)),
        jax.ShapeDtypeStruct((width, 2 * half * parts), jnp.bfloat16),
        [pltpu.VMEM((count, 2 * half), jnp.bfloat16)],
        {2 + 2 * n: 0} if extra else {},
    )


def transposed(value):
    count, width = value.shape
    tile = tile_of(width, 512)

    def kernel(value_ref, out):
        out[...] = value_ref[...].T

    return call(
        kernel,
        "transposed",
        (width // tile,),
        [],
        [value],
        [pl.BlockSpec((count, tile), lambda i: (0, i))],
        pl.BlockSpec((tile, count), lambda i: (i, 0)),
        jax.ShapeDtypeStruct((width, count), value.dtype),
        vmem=SMALL_VMEM,
    )


def from_peer(value, by):
    peers = lax.axis_size("mp")
    return lax.ppermute(value, "mp", [(i, i ^ by) for i in range(peers)])


def across_sections(value):
    return lax.ppermute(value, "section", [(0, 1), (1, 0)])


def local(tokens, weights, gain, cotangent):
    section = lax.axis_index("section").astype(jnp.int32).reshape(1)
    first = 1 - section
    weight = weights[0]
    peers = lax.axis_size("mp")
    line = lax.axis_size("dp")
    half = line // 2
    place = lax.axis_index("dp")
    rows = tokens.shape[0]
    each = peers // 4
    parts = 4 if weight.shape[1] % 1024 == 0 else 3

    last = []

    def run(work, anchor, *others):
        if last:
            held = last[-1]
            anchor, held["value"] = lax.optimization_barrier((anchor, held["value"]))
        held = {"value": work(anchor, *others)}
        last.append(held)
        return held

    receives = {
        hop: jnp.logical_or(place == hop, place == line - 1 - hop).astype(jnp.int32).reshape(1)
        for hop in range(half - 1)
    }
    tokens, section, first, receives = lax.optimization_barrier((tokens, section, first, receives))

    raw = run(lambda a, b: jnp.where(first[0] == 1, a, b), tokens, cotangent)["value"]
    across = peers // 2
    near = list(range(each, 2 * each)) + list(range(each))
    far = [by ^ across for by in near]
    gathered = {by: from_peer(raw, by) if by else raw for by in near}

    values = tokens.astype(jnp.float32)
    row_total, row_squares = lax.psum((jnp.sum(values, 1), jnp.sum(values * values, 1)), "dp")
    average = row_total / D
    inverse_std = lax.rsqrt(row_squares / D - average * average + epsilon)
    own_scale = jnp.stack([average, inverse_std], 1)
    near_scale = jnp.concatenate([from_peer(own_scale, by) if by else own_scale for by in near], 0)
    gathered[across] = from_peer(raw, across)
    gathered, near_scale = lax.optimization_barrier((gathered, near_scale))
    gathered.update({by: from_peer(gathered[by ^ across], across) for by in far if by != across})
    far_scale = from_peer(near_scale, across)

    def prepare(members, scale, group, into):
        blocks = [gathered[by] for by in members]
        return run(lambda g: normalize(first, blocks, scale, g, group, into), gain)["value"]

    chunks = {}

    def multiply(value, part, groups):
        products = run(lambda s: up_product(s, value, weight, part, parts, groups), section)
        for i, group in enumerate(groups):
            chunks[part, group] = {"products": products, "mine": i, "theirs": len(groups) + i}

    def stack(chunk):
        products = chunk["products"]
        arrived = across_sections(products["value"][chunk["theirs"]])
        chunk["sum"] = run(stacked, products["value"][chunk["mine"]], arrived)

    def inward(chunk):
        for hop in range(half - 1):
            value = chunk["sum"]["value"]
            arrived = lax.ppermute(value, "dp", [(hop, hop + 1), (line - 1 - hop, line - 2 - hop)])
            chunk["sum"] = run(added, value, arrived)

    def middle(chunk):
        value = chunk["sum"]["value"]
        arrived = lax.ppermute(value, "dp", [(half - 1, half), (half, half - 1)])
        chunk["result"] = run(lambda a, b: activated(first, a, b), value, arrived)

    def outward(chunk):
        for hop in reversed(range(half - 1)):
            value = chunk["result"]["value"]
            arrived = lax.ppermute(value, "dp", [(hop + 1, hop), (line - 2 - hop, line - 1 - hop)])
            if hop:
                chunk["result"] = run(lambda a, b: chosen(receives[hop], a, b, False)[0], value, arrived)
            else:
                chunk["halves"] = run(lambda a, b: chosen(receives[hop], a, b, True), value, arrived)

    def hidden(part, groups):
        kept = [chunks[part, g]["halves"]["value"][0] for g in groups]
        for g in groups:
            if "came" not in chunks[part, g]:
                chunks[part, g]["came"] = across_sections(chunks[part, g]["halves"]["value"][1])
        return kept, [chunks[part, g]["came"] for g in groups]

    def groups_of(part):
        return (FAR, NEAR) if part < parts - 1 else (FAR, PEER, OWN)

    order = [(part, g) for g in (NEAR, FAR) for part in (0, 1)]
    order += [(part, FAR) for part in range(2, parts)] + [(part, NEAR) for part in range(2, parts - 1)]
    order += [(parts - 1, PEER), (parts - 1, OWN)]
    count = len(order)
    held = {"gradient": None}

    def need(c):
        if c < count and order[c] not in chunks:
            part, group = order[c]
            multiply(x_all, part, [group] if part < 2 else groups_of(part))

    def tick(t):
        if 0 < t < count - 1:
            inward(chunks[order[t]])
        if 0 <= t - 1 < count - 2:
            middle(chunks[order[t - 1]])
        if 0 <= t - 2 < count:
            outward(chunks[order[t - 2]])
        if t == count - 1:
            inward(chunks[order[t]])
        if count - 2 <= t - 1 < count:
            middle(chunks[order[t - 1]])
        if 2 <= t + 2 < count:
            stack(chunks[order[t + 2]])

    def go_down(part, groups, before, column, kinds=(), arrived=()):
        kept, came = hidden(part, groups)
        before = None if before is None else before["value"][0]
        return run(
            lambda k: down_product(section, [k] + kept[1:], came, weight, part, parts, before, column, arrived, kinds),
            kept[0],
        )

    def go_gradient(part):
        kept, came = hidden(part, groups_of(part))
        into = None if held["gradient"] is None else held["gradient"]["value"]
        held["gradient"] = run(
            lambda k: weight_gradient(section, turned, [k] + kept[1:], came, part, parts, into), kept[0]
        )

    x_near = prepare(near, near_scale, NEAR, None)
    multiply(x_near, 0, [NEAR])
    stack(chunks[order[0]])
    multiply(x_near, 1, [NEAR])
    stack(chunks[order[1]])
    x_all = prepare(far, far_scale, FAR, x_near)
    multiply(x_all, 0, [FAR])
    inward(chunks[order[0]])
    for t in range(count + 2):
        tick(t)
        need(t + 3)
        far_part, near_part = t - 4, t - 2 - parts
        if t == 3:
            turned = run(transposed, x_all)["value"]
        elif t == 4:
            near_sum = go_down(0, (FAR, NEAR), None, 0)
        elif t == 5:
            near_sum = far_sum = go_down(1, (FAR, NEAR), near_sum, 0)
        if 2 <= far_part < parts - 1:
            far_sum = go_down(far_part, [FAR], far_sum, 0)
        elif far_part == parts - 1:
            sent_far = go_down(far_part, [FAR], far_sum, 0, [jnp.bfloat16] * 2)
            arrived = [from_peer(value, across) for value in sent_far["value"]]
        if t in (6, 7):
            go_gradient(t - 6)
        if 2 <= near_part < parts - 1:
            go_gradient(near_part)
            near_sum = go_down(near_part, [NEAR], near_sum, 1 if near_part == 2 else 0)
        if t == count:
            first_column = 2 if parts == 3 else 0
            peer_sum = go_down(parts - 1, [PEER], near_sum, first_column, [jnp.bfloat16], arrived[:1])
    go_gradient(parts - 1)
    own_sum = go_down(parts - 1, [OWN], near_sum, first_column + 1, [jnp.float32], arrived[1:])

    own = own_sum["value"][0]
    blocks = {0: own.astype(jnp.bfloat16), 1: peer_sum["value"][0]}
    result = own[:rows]
    for by in range(1, across):
        at = (by % each) * rows
        result = result + from_peer(blocks[by // each][at : at + rows], by).astype(jnp.float32)
    return (result.astype(jnp.bfloat16)[None], held["gradient"]["value"][None])


def solution(mesh):
    placed = (P("mp", "dp"), P("section", "dp", "mp"), P("dp"), P("mp", "dp"))
    return jax.shard_map(
        local,
        mesh=mesh,
        in_specs=placed,
        out_specs=(P("section", "mp", "dp"), P("section", "dp", "mp")),
        check_vma=False,
    )
```

```python
import jax
import jax.numpy as jnp
from jax import lax
from jax.experimental import pallas as pl
from jax.experimental.pallas import tpu as pltpu
from jax.sharding import PartitionSpec as P

D = 12288
MATMUL_VMEM = 22 * 1024 * 1024
SMALL_VMEM = 8 * 1024 * 1024
FAR, NEAR = 0, 1


epsilon = 1e-05


def dot_f32(left, right, contract):
    return lax.dot_general(
        left, right, ((contract[:1], contract[1:]), ((), ())), preferred_element_type=jnp.float32
    )


def tile_of(extent, limit):
    return max(t for t in range(128, limit + 1, 128) if extent % t == 0)


def fixed(shape, index):
    return pl.BlockSpec(shape, lambda *_: index, pipeline_mode=pl.Buffered(1))


def call(kernel, name, grid, scalars, operands, in_specs, out_specs, out_shape, scratch=(), aliases={}, vmem=MATMUL_VMEM):
    return pl.pallas_call(
        kernel,
        grid_spec=pltpu.PrefetchScalarGridSpec(
            num_scalar_prefetch=len(scalars),
            grid=grid,
            in_specs=in_specs,
            out_specs=out_specs,
            scratch_shapes=list(scratch),
        ),
        out_shape=out_shape,
        input_output_aliases=aliases,
        compiler_params=pltpu.CompilerParams(vmem_limit_bytes=vmem),
        name=name,
    )(*scalars, *operands)


def normalize(first, blocks, scale, gain, group, into):
    rows, width = blocks[0].shape
    count = rows * len(blocks)
    tile = tile_of(width, 768)

    def kernel(first_ref, gain_ref, scale_ref, *refs):
        out = refs[-1]
        for i in range(len(blocks)):
            own = slice(i * rows, (i + 1) * rows)
            value = refs[i][...].astype(jnp.float32)
            centred = (value - scale_ref[own, 0:1]) * scale_ref[own, 1:2]
            normed = (centred * gain_ref[...]).astype(jnp.bfloat16)
            out[own, :] = jnp.where(first_ref[0] == 1, normed, refs[i][...])

    column = lambda i, _: (0, i)
    extra = [] if into is None else [into]
    return call(
        kernel,
        "normalize",
        (width // tile,),
        [first],
        [gain.reshape(1, width), scale, *blocks, *extra],
        [pl.BlockSpec((1, tile), column), fixed((count, 2), (0, 0))]
        + [pl.BlockSpec((rows, tile), column)] * len(blocks)
        + [pl.BlockSpec(memory_space=pl.ANY)] * len(extra),
        pl.BlockSpec((count, tile), lambda i, _: (group, i)),
        jax.ShapeDtypeStruct((2 * count, width), jnp.bfloat16),
        aliases={3 + len(blocks): 0} if extra else {},
        vmem=SMALL_VMEM,
    )


def up_product(section, rows, weight, part, parts, groups):
    pieces = len(groups)
    count, width = rows.shape[0] // 2 * pieces, rows.shape[1]
    at = groups[0]
    columns = weight.shape[1] // parts
    tile = tile_of(columns // 2, 768)
    steps = columns // tile
    mine = steps // 2
    piece = count // pieces

    def kernel(section_ref, rows_ref, weight_ref, *results):
        product = dot_f32(rows_ref[...], weight_ref[...], (1, 0)).astype(jnp.bfloat16)

        def store(refs):
            for i, result in enumerate(refs):
                result[...] = product[i * piece : (i + 1) * piece]

        pl.when(pl.program_id(0) < mine)(lambda: store(results[:pieces]))
        pl.when(pl.program_id(0) >= mine)(lambda: store(results[pieces:]))

    return call(
        kernel,
        "up_product",
        (steps,),
        [section],
        [rows, weight],
        [
            fixed((count, width), (at, 0)),
            pl.BlockSpec((width, tile), lambda i, s: (0, part * steps + lax.rem(i + s[0] * mine, steps))),
        ],
        [pl.BlockSpec((piece, tile), lambda i, s: (0, jnp.minimum(i, mine - 1)))] * pieces
        + [pl.BlockSpec((piece, tile), lambda i, s: (0, jnp.maximum(i - mine, 0)))] * pieces,
        [jax.ShapeDtypeStruct((piece, columns // 2), jnp.bfloat16)] * (2 * pieces),
    )


def elementwise(body, name, scalars, operands, out_rows):
    columns = operands[0].shape[1]
    tile = tile_of(columns, 256)
    column = lambda i, *_: (0, i)

    def kernel(*refs):
        scalar_refs = refs[: len(scalars)]
        ins = refs[len(scalars) : len(scalars) + len(operands)]
        outs = refs[len(scalars) + len(operands) :]
        for out, value in zip(outs, body(scalar_refs, ins)):
            out[...] = value

    return call(
        kernel,
        name,
        (columns // tile,),
        scalars,
        operands,
        [pl.BlockSpec((o.shape[0], tile), column) for o in operands],
        [pl.BlockSpec((r, tile), column) for r in out_rows],
        [jax.ShapeDtypeStruct((r, columns), jnp.bfloat16) for r in out_rows],
        vmem=SMALL_VMEM,
    )


def stacked(mine, arrived):
    rows = mine.shape[0]
    body = lambda _, ins: (jnp.concatenate([ins[0][...], ins[1][...]], 0),)
    return elementwise(body, "stacked", [], [mine, arrived], [2 * rows])[0]


def added(value, arrived):
    def body(_, ins):
        total = ins[0][...].astype(jnp.float32) + ins[1][...].astype(jnp.float32)
        return (total.astype(jnp.bfloat16),)

    return elementwise(body, "added", [], [value, arrived], [value.shape[0]])[0]


def activated(first, value, arrived):
    rows = value.shape[0] // 2

    def body(scalars, ins):
        is_first = scalars[0][0] == 1
        total = ins[0][...].astype(jnp.float32) + ins[1][...].astype(jnp.float32)
        above, below = total[:rows], total[rows:]
        v = jnp.where(is_first, above, below)
        grad = jnp.where(is_first, below, above)
        c = 0.7978845608028654
        t = jnp.tanh(c * (v + 0.044715 * (v * v * v)))
        hidden = (0.5 * v * (1.0 + t)).astype(jnp.bfloat16)
        slope = 0.5 * (1.0 + t) + 0.5 * v * (1.0 - t * t) * (c * (1.0 + 3.0 * 0.044715 * (v * v)))
        grad_preact = (grad * slope).astype(jnp.bfloat16)
        kept = jnp.where(is_first, grad_preact, hidden)
        sent = jnp.where(is_first, hidden, grad_preact)
        return (jnp.concatenate([kept, sent], 0),)

    return elementwise(body, "activated", [first], [value, arrived], [2 * rows])[0]


def chosen(receives, value, arrived, halves):
    rows = value.shape[0]

    def body(scalars, ins):
        result = jnp.where(scalars[0][0] == 1, ins[1][...], ins[0][...])
        return (result[: rows // 2], result[rows // 2 :]) if halves else (result,)

    out_rows = [rows // 2] * 2 if halves else [rows]
    return elementwise(body, "chosen", [receives], [value, arrived], out_rows)


def down_product(section, kept, came, weight, part, parts, before, group, arrived, kinds):
    counts = [k.shape[0] for k in kept]
    count, half = sum(counts), kept[0].shape[1]
    width = weight.shape[0]
    tile = tile_of(width, 1024)
    n = len(kept)
    extra = [] if before is None else [before]
    others = list(arrived)

    def kernel(section_ref, *refs):
        weight_ref = refs[2 * n]
        added = refs[2 * n + 1 : 2 * n + 1 + len(extra)]
        arrived_refs = refs[2 * n + 1 + len(extra) : 2 * n + 1 + len(extra) + len(others)]
        results = refs[2 * n + 1 + len(extra) + len(others) : -1]
        held = refs[-1]

        @pl.when(pl.program_id(0) == 0)
        def _():
            mine = pl.ds(pl.multiple_of(section_ref[0] * half, half), half)
            theirs = pl.ds(pl.multiple_of((1 - section_ref[0]) * half, half), half)
            at = 0
            for i, rows in enumerate(counts):
                held[mine, at : at + rows] = refs[i][...].T
                held[theirs, at : at + rows] = refs[n + i][...].T
                at += rows

        product = dot_f32(weight_ref[...], held[...], (1, 0))
        for ref in added:
            product = product + ref[...]
        if kinds:
            product = product.T
            piece = count // len(kinds)
            for i, result in enumerate(results):
                value = product[i * piece : (i + 1) * piece]
                if others:
                    value = value + arrived_refs[i][...].astype(jnp.float32)
                result[...] = value.astype(result.dtype)
        else:
            results[0][...] = product

    whole = [fixed((rows, half), (0, 0)) for rows in counts]
    if kinds:
        out_specs = [pl.BlockSpec((count // len(kinds), tile), lambda i, s: (0, i))] * len(kinds)
        out_shape = [jax.ShapeDtypeStruct((count // len(kinds), width), kind) for kind in kinds]
    else:
        out_specs = [pl.BlockSpec((tile, count), lambda i, s: (i, 0))]
        out_shape = [jax.ShapeDtypeStruct((width, count), jnp.float32)]
    return call(
        kernel,
        "down_product",
        (width // tile,),
        [section],
        [*kept, *came, weight, *extra, *others],
        whole
        + whole
        + [pl.BlockSpec((tile, 2 * half), lambda i, s: (i, part))]
        + [pl.BlockSpec((tile, count), lambda i, s: (i, group))] * len(extra)
        + [pl.BlockSpec((count // max(len(kinds), 1), tile), lambda i, s: (0, i))] * len(others),
        out_specs,
        out_shape,
        [pltpu.VMEM((2 * half, count), jnp.bfloat16)],
    )


def weight_gradient(section, turned, kept, came, part, parts, into):
    width, count = turned.shape
    counts = [k.shape[0] for k in kept]
    half = kept[0].shape[1]
    tile = tile_of(width, 1024)
    step = half
    n = len(kept)

    def kernel(section_ref, turned_ref, *refs):
        out, held = refs[-2:]

        @pl.when(pl.program_id(0) == 0)
        def _():
            mine = pl.ds(pl.multiple_of(section_ref[0] * half, half), half)
            theirs = pl.ds(pl.multiple_of((1 - section_ref[0]) * half, half), half)
            at = 0
            for i, rows in enumerate(counts):
                held[at : at + rows, mine] = refs[i][...]
                held[at : at + rows, theirs] = refs[n + i][...]
                at += rows

        for at in range(0, 2 * half, step):
            own = slice(at, at + step)
            out[:, own] = dot_f32(turned_ref[...], held[:, own], (1, 0)).astype(jnp.bfloat16)

    whole = [fixed((rows, half), (0, 0)) for rows in counts]
    extra = [] if into is None else [into]
    return call(
        kernel,
        "weight_gradient",
        (width // tile,),
        [section],
        [turned, *kept, *came, *extra],
        [pl.BlockSpec((tile, count), lambda i, s: (i, 0))]
        + whole
        + whole
        + [pl.BlockSpec(memory_space=pl.ANY)] * len(extra),
        pl.BlockSpec((tile, 2 * half), lambda i, s: (i, part)),
        jax.ShapeDtypeStruct((width, 2 * half * parts), jnp.bfloat16),
        [pltpu.VMEM((count, 2 * half), jnp.bfloat16)],
        {2 + 2 * n: 0} if extra else {},
    )


def transposed(value):
    count, width = value.shape
    tile = tile_of(width, 512)

    def kernel(value_ref, out):
        out[...] = value_ref[...].T

    return call(
        kernel,
        "transposed",
        (width // tile,),
        [],
        [value],
        [pl.BlockSpec((count, tile), lambda i: (0, i))],
        pl.BlockSpec((tile, count), lambda i: (i, 0)),
        jax.ShapeDtypeStruct((width, count), value.dtype),
        vmem=SMALL_VMEM,
    )


def from_peer(value, by):
    peers = lax.axis_size("mp")
    return lax.ppermute(value, "mp", [(i, i ^ by) for i in range(peers)])


def across_sections(value):
    return lax.ppermute(value, "section", [(0, 1), (1, 0)])


def local(tokens, weights, gain, cotangent):
    section = lax.axis_index("section").astype(jnp.int32).reshape(1)
    first = 1 - section
    weight = weights[0]
    peers = lax.axis_size("mp")
    line = lax.axis_size("dp")
    half = line // 2
    place = lax.axis_index("dp")
    rows = tokens.shape[0]
    each = peers // 4
    parts = 4 if weight.shape[1] % 1024 == 0 else 3

    last = []

    def run(work, anchor, *others):
        if last:
            held = last[-1]
            anchor, held["value"] = lax.optimization_barrier((anchor, held["value"]))
        held = {"value": work(anchor, *others)}
        last.append(held)
        return held

    receives = {
        hop: jnp.logical_or(place == hop, place == line - 1 - hop).astype(jnp.int32).reshape(1)
        for hop in range(half - 1)
    }
    tokens, section, first, receives = lax.optimization_barrier((tokens, section, first, receives))

    raw = run(lambda a, b: jnp.where(first[0] == 1, a, b), tokens, cotangent)["value"]
    across = peers // 2
    near = list(range(each, 2 * each)) + list(range(each))
    far = [by ^ across for by in near]
    gathered = {by: from_peer(raw, by) if by else raw for by in near}

    values = tokens.astype(jnp.float32)
    row_total, row_squares = lax.psum((jnp.sum(values, 1), jnp.sum(values * values, 1)), "dp")
    average = row_total / D
    inverse_std = lax.rsqrt(row_squares / D - average * average + epsilon)
    own_scale = jnp.stack([average, inverse_std], 1)
    near_scale = jnp.concatenate([from_peer(own_scale, by) if by else own_scale for by in near], 0)
    gathered[across] = from_peer(raw, across)
    gathered, near_scale = lax.optimization_barrier((gathered, near_scale))
    gathered.update({by: from_peer(gathered[by ^ across], across) for by in far if by != across})
    far_scale = from_peer(near_scale, across)

    def prepare(members, scale, group, into):
        blocks = [gathered[by] for by in members]
        return run(lambda g: normalize(first, blocks, scale, g, group, into), gain)["value"]

    chunks = {}

    def multiply(value, part, groups):
        products = run(lambda s: up_product(s, value, weight, part, parts, groups), section)
        for i, group in enumerate(groups):
            chunks[part, group] = {"products": products, "mine": i, "theirs": len(groups) + i}

    def stack(chunk):
        products = chunk["products"]
        arrived = across_sections(products["value"][chunk["theirs"]])
        chunk["sum"] = run(stacked, products["value"][chunk["mine"]], arrived)

    def inward(chunk):
        for hop in range(half - 1):
            value = chunk["sum"]["value"]
            arrived = lax.ppermute(value, "dp", [(hop, hop + 1), (line - 1 - hop, line - 2 - hop)])
            chunk["sum"] = run(added, value, arrived)

    def middle(chunk):
        value = chunk["sum"]["value"]
        arrived = lax.ppermute(value, "dp", [(half - 1, half), (half, half - 1)])
        chunk["result"] = run(lambda a, b: activated(first, a, b), value, arrived)

    def outward(chunk):
        for hop in reversed(range(half - 1)):
            value = chunk["result"]["value"]
            arrived = lax.ppermute(value, "dp", [(hop + 1, hop), (line - 2 - hop, line - 1 - hop)])
            if hop:
                chunk["result"] = run(lambda a, b: chosen(receives[hop], a, b, False)[0], value, arrived)
            else:
                chunk["halves"] = run(lambda a, b: chosen(receives[hop], a, b, True), value, arrived)

    def hidden(part, groups):
        kept = [chunks[part, g]["halves"]["value"][0] for g in groups]
        for g in groups:
            if "came" not in chunks[part, g]:
                chunks[part, g]["came"] = across_sections(chunks[part, g]["halves"]["value"][1])
        return kept, [chunks[part, g]["came"] for g in groups]

    both = (FAR, NEAR)
    order = [(part, g) for part in (0, 1) for g in (NEAR, FAR)]
    order += [(part, g) for g in (FAR, NEAR) for part in range(2, parts)]
    count = len(order)
    held = {"gradient": None}

    def need(c):
        if c < count and order[c] not in chunks:
            part, group = order[c]
            multiply(x_all, part, [group] if part < 2 else both)

    def tick(t):
        if 0 <= t - 1 < count:
            middle(chunks[order[t - 1]])
        if 0 <= t - 2 < count:
            outward(chunks[order[t - 2]])
        if 2 <= t + 2 < count:
            stack(chunks[order[t + 2]])

    def go_down(part, groups, before, column, kinds=(), arrived=()):
        kept, came = hidden(part, groups)
        before = None if before is None else before["value"][0]
        return run(
            lambda k: down_product(section, [k] + kept[1:], came, weight, part, parts, before, column, arrived, kinds),
            kept[0],
        )

    def go_gradient(part):
        kept, came = hidden(part, both)
        into = None if held["gradient"] is None else held["gradient"]["value"]
        held["gradient"] = run(
            lambda k: weight_gradient(section, turned, [k] + kept[1:], came, part, parts, into), kept[0]
        )

    x_near = prepare(near, near_scale, NEAR, None)
    multiply(x_near, 0, [NEAR])
    stack(chunks[order[0]])
    multiply(x_near, 1, [NEAR])
    x_all = prepare(far, far_scale, FAR, x_near)
    multiply(x_all, 0, [FAR])
    inward(chunks[order[0]])
    stack(chunks[order[1]])
    for t in range(count + 2):
        if 0 < t < count:
            inward(chunks[order[t]])
        tick(t)
        need(t + 3)
        far_part, near_part = t - 4, t - 2 - parts
        if t == 3:
            turned = run(transposed, x_all)["value"]
            near_sum = go_down(0, both, None, 0)
        elif t == 4:
            hidden(1, [NEAR])
            kept = chunks[0, NEAR]["halves"]
            waited = chunks[1, NEAR]
            kept["value"], waited["came"] = lax.optimization_barrier((kept["value"], waited["came"]))
            go_gradient(0)
        elif t == 5:
            near_sum = far_sum = go_down(1, both, near_sum, 0)
        if 2 <= far_part < parts - 1:
            far_sum = go_down(far_part, [FAR], far_sum, FAR if far_part == 2 else 0)
        elif far_part == parts - 1:
            sent_far = go_down(far_part, [FAR], far_sum, FAR if far_part == 2 else 0, [jnp.bfloat16] * 2)
            arrived = [from_peer(value, across) for value in sent_far["value"]]
        if t == count - 1:
            go_gradient(1)
        if 2 <= near_part < parts - 1:
            near_sum = go_down(near_part, [NEAR], near_sum, NEAR if near_part == 2 else 0)
            near_sum["value"], arrived = lax.optimization_barrier((near_sum["value"], arrived))
    column = NEAR if parts == 3 else 0
    sent_near = go_down(parts - 1, [NEAR], near_sum, column, [jnp.bfloat16, jnp.float32], arrived)
    for part in range(2, parts):
        go_gradient(part)

    own = sent_near["value"][1]
    blocks = {0: own.astype(jnp.bfloat16), 1: sent_near["value"][0]}
    result = own[:rows]
    for by in range(1, across):
        at = (by % each) * rows
        result = result + from_peer(blocks[by // each][at : at + rows], by).astype(jnp.float32)
    return (result.astype(jnp.bfloat16)[None], held["gradient"]["value"][None])


def solution(mesh):
    placed = (P("mp", "dp"), P("section", "dp", "mp"), P("dp"), P("mp", "dp"))
    return jax.shard_map(
        local,
        mesh=mesh,
        in_specs=placed,
        out_specs=(P("section", "mp", "dp"), P("section", "dp", "mp")),
        check_vma=False,
    )
```

```python
import jax
import jax.numpy as jnp
from jax import lax
from jax.experimental import pallas as pl
from jax.experimental.pallas import tpu as pltpu
from jax.sharding import PartitionSpec as P

D = 12288
MATMUL_VMEM = 22 * 1024 * 1024
SMALL_VMEM = 8 * 1024 * 1024
FAR, NEAR = 0, 1


epsilon = 1e-05


def dot_f32(left, right, contract):
    return lax.dot_general(
        left, right, ((contract[:1], contract[1:]), ((), ())), preferred_element_type=jnp.float32
    )


def tile_of(extent, limit):
    return max(t for t in range(128, limit + 1, 128) if extent % t == 0)


def fixed(shape, index):
    return pl.BlockSpec(shape, lambda *_: index, pipeline_mode=pl.Buffered(1))


def call(kernel, name, grid, scalars, operands, in_specs, out_specs, out_shape, scratch=(), aliases={}, vmem=MATMUL_VMEM):
    return pl.pallas_call(
        kernel,
        grid_spec=pltpu.PrefetchScalarGridSpec(
            num_scalar_prefetch=len(scalars),
            grid=grid,
            in_specs=in_specs,
            out_specs=out_specs,
            scratch_shapes=list(scratch),
        ),
        out_shape=out_shape,
        input_output_aliases=aliases,
        compiler_params=pltpu.CompilerParams(vmem_limit_bytes=vmem),
        name=name,
    )(*scalars, *operands)


def normalize(first, blocks, scale, gain, group, into):
    rows, width = blocks[0].shape
    count = rows * len(blocks)
    tile = tile_of(width, 768)

    def kernel(first_ref, gain_ref, scale_ref, *refs):
        out = refs[-1]
        for i in range(len(blocks)):
            own = slice(i * rows, (i + 1) * rows)
            value = refs[i][...].astype(jnp.float32)
            centred = (value - scale_ref[own, 0:1]) * scale_ref[own, 1:2]
            normed = (centred * gain_ref[...]).astype(jnp.bfloat16)
            out[own, :] = jnp.where(first_ref[0] == 1, normed, refs[i][...])

    column = lambda i, _: (0, i)
    extra = [] if into is None else [into]
    return call(
        kernel,
        "normalize",
        (width // tile,),
        [first],
        [gain.reshape(1, width), scale, *blocks, *extra],
        [pl.BlockSpec((1, tile), column), fixed((count, 2), (0, 0))]
        + [pl.BlockSpec((rows, tile), column)] * len(blocks)
        + [pl.BlockSpec(memory_space=pl.ANY)] * len(extra),
        pl.BlockSpec((count, tile), lambda i, _: (group, i)),
        jax.ShapeDtypeStruct((2 * count, width), jnp.bfloat16),
        aliases={3 + len(blocks): 0} if extra else {},
        vmem=SMALL_VMEM,
    )


def up_product(section, rows, weight, part, parts, groups):
    pieces = len(groups)
    count, width = rows.shape[0] // 2 * pieces, rows.shape[1]
    at = groups[0]
    columns = weight.shape[1] // parts
    tile = tile_of(columns // 2, 768)
    steps = columns // tile
    mine = steps // 2
    piece = count // pieces

    def kernel(section_ref, rows_ref, weight_ref, *results):
        product = dot_f32(rows_ref[...], weight_ref[...], (1, 0)).astype(jnp.bfloat16)

        def store(refs):
            for i, result in enumerate(refs):
                result[...] = product[i * piece : (i + 1) * piece]

        pl.when(pl.program_id(0) < mine)(lambda: store(results[:pieces]))
        pl.when(pl.program_id(0) >= mine)(lambda: store(results[pieces:]))

    return call(
        kernel,
        "up_product",
        (steps,),
        [section],
        [rows, weight],
        [
            fixed((count, width), (at, 0)),
            pl.BlockSpec((width, tile), lambda i, s: (0, part * steps + lax.rem(i + s[0] * mine, steps))),
        ],
        [pl.BlockSpec((piece, tile), lambda i, s: (0, jnp.minimum(i, mine - 1)))] * pieces
        + [pl.BlockSpec((piece, tile), lambda i, s: (0, jnp.maximum(i - mine, 0)))] * pieces,
        [jax.ShapeDtypeStruct((piece, columns // 2), jnp.bfloat16)] * (2 * pieces),
    )


def elementwise(body, name, scalars, operands, out_rows):
    columns = operands[0].shape[1]
    tile = tile_of(columns, 256)
    column = lambda i, *_: (0, i)

    def kernel(*refs):
        scalar_refs = refs[: len(scalars)]
        ins = refs[len(scalars) : len(scalars) + len(operands)]
        outs = refs[len(scalars) + len(operands) :]
        for out, value in zip(outs, body(scalar_refs, ins)):
            out[...] = value

    return call(
        kernel,
        name,
        (columns // tile,),
        scalars,
        operands,
        [pl.BlockSpec((o.shape[0], tile), column) for o in operands],
        [pl.BlockSpec((r, tile), column) for r in out_rows],
        [jax.ShapeDtypeStruct((r, columns), jnp.bfloat16) for r in out_rows],
        vmem=SMALL_VMEM,
    )


def stacked(mine, arrived):
    rows = mine.shape[0]
    body = lambda _, ins: (jnp.concatenate([ins[0][...], ins[1][...]], 0),)
    return elementwise(body, "stacked", [], [mine, arrived], [2 * rows])[0]


def added(value, arrived):
    def body(_, ins):
        total = ins[0][...].astype(jnp.float32) + ins[1][...].astype(jnp.float32)
        return (total.astype(jnp.bfloat16),)

    return elementwise(body, "added", [], [value, arrived], [value.shape[0]])[0]


def activated(first, value, arrived):
    rows = value.shape[0] // 2

    def body(scalars, ins):
        is_first = scalars[0][0] == 1
        total = ins[0][...].astype(jnp.float32) + ins[1][...].astype(jnp.float32)
        above, below = total[:rows], total[rows:]
        v = jnp.where(is_first, above, below)
        grad = jnp.where(is_first, below, above)
        c = 0.7978845608028654
        t = jnp.tanh(c * (v + 0.044715 * (v * v * v)))
        hidden = (0.5 * v * (1.0 + t)).astype(jnp.bfloat16)
        slope = 0.5 * (1.0 + t) + 0.5 * v * (1.0 - t * t) * (c * (1.0 + 3.0 * 0.044715 * (v * v)))
        grad_preact = (grad * slope).astype(jnp.bfloat16)
        kept = jnp.where(is_first, grad_preact, hidden)
        sent = jnp.where(is_first, hidden, grad_preact)
        return (jnp.concatenate([kept, sent], 0),)

    return elementwise(body, "activated", [first], [value, arrived], [2 * rows])[0]


def chosen(receives, value, arrived, halves):
    rows = value.shape[0]

    def body(scalars, ins):
        result = jnp.where(scalars[0][0] == 1, ins[1][...], ins[0][...])
        return (result[: rows // 2], result[rows // 2 :]) if halves else (result,)

    out_rows = [rows // 2] * 2 if halves else [rows]
    return elementwise(body, "chosen", [receives], [value, arrived], out_rows)


def down_product(section, kept, came, weight, part, parts, before, group, arrived, kinds):
    counts = [k.shape[0] for k in kept]
    count, half = sum(counts), kept[0].shape[1]
    width = weight.shape[0]
    tile = tile_of(width, 1024)
    n = len(kept)
    extra = [] if before is None else [before]
    others = list(arrived)

    def kernel(section_ref, *refs):
        weight_ref = refs[2 * n]
        added = refs[2 * n + 1 : 2 * n + 1 + len(extra)]
        arrived_refs = refs[2 * n + 1 + len(extra) : 2 * n + 1 + len(extra) + len(others)]
        results = refs[2 * n + 1 + len(extra) + len(others) : -1]
        held = refs[-1]

        @pl.when(pl.program_id(0) == 0)
        def _():
            mine = pl.ds(pl.multiple_of(section_ref[0] * half, half), half)
            theirs = pl.ds(pl.multiple_of((1 - section_ref[0]) * half, half), half)
            at = 0
            for i, rows in enumerate(counts):
                held[mine, at : at + rows] = refs[i][...].T
                held[theirs, at : at + rows] = refs[n + i][...].T
                at += rows

        product = dot_f32(weight_ref[...], held[...], (1, 0))
        for ref in added:
            product = product + ref[...]
        if kinds:
            product = product.T
            piece = count // len(kinds)
            for i, result in enumerate(results):
                value = product[i * piece : (i + 1) * piece]
                if others:
                    value = value + arrived_refs[i][...].astype(jnp.float32)
                result[...] = value.astype(result.dtype)
        else:
            results[0][...] = product

    whole = [fixed((rows, half), (0, 0)) for rows in counts]
    if kinds:
        out_specs = [pl.BlockSpec((count // len(kinds), tile), lambda i, s: (0, i))] * len(kinds)
        out_shape = [jax.ShapeDtypeStruct((count // len(kinds), width), kind) for kind in kinds]
    else:
        out_specs = [pl.BlockSpec((tile, count), lambda i, s: (i, 0))]
        out_shape = [jax.ShapeDtypeStruct((width, count), jnp.float32)]
    return call(
        kernel,
        "down_product",
        (width // tile,),
        [section],
        [*kept, *came, weight, *extra, *others],
        whole
        + whole
        + [pl.BlockSpec((tile, 2 * half), lambda i, s: (i, part))]
        + [pl.BlockSpec((tile, count), lambda i, s: (i, group))] * len(extra)
        + [pl.BlockSpec((count // max(len(kinds), 1), tile), lambda i, s: (0, i))] * len(others),
        out_specs,
        out_shape,
        [pltpu.VMEM((2 * half, count), jnp.bfloat16)],
    )


def weight_gradient(section, turned, kept, came, part, parts, into):
    width, count = turned.shape
    counts = [k.shape[0] for k in kept]
    half = kept[0].shape[1]
    tile = tile_of(width, 1024)
    step = half
    n = len(kept)

    def kernel(section_ref, turned_ref, *refs):
        out, held = refs[-2:]

        @pl.when(pl.program_id(0) == 0)
        def _():
            mine = pl.ds(pl.multiple_of(section_ref[0] * half, half), half)
            theirs = pl.ds(pl.multiple_of((1 - section_ref[0]) * half, half), half)
            at = 0
            for i, rows in enumerate(counts):
                held[at : at + rows, mine] = refs[i][...]
                held[at : at + rows, theirs] = refs[n + i][...]
                at += rows

        for at in range(0, 2 * half, step):
            own = slice(at, at + step)
            out[:, own] = dot_f32(turned_ref[...], held[:, own], (1, 0)).astype(jnp.bfloat16)

    whole = [fixed((rows, half), (0, 0)) for rows in counts]
    extra = [] if into is None else [into]
    return call(
        kernel,
        "weight_gradient",
        (width // tile,),
        [section],
        [turned, *kept, *came, *extra],
        [pl.BlockSpec((tile, count), lambda i, s: (i, 0))]
        + whole
        + whole
        + [pl.BlockSpec(memory_space=pl.ANY)] * len(extra),
        pl.BlockSpec((tile, 2 * half), lambda i, s: (i, part)),
        jax.ShapeDtypeStruct((width, 2 * half * parts), jnp.bfloat16),
        [pltpu.VMEM((count, 2 * half), jnp.bfloat16)],
        {2 + 2 * n: 0} if extra else {},
    )


def transposed(value):
    count, width = value.shape
    tile = tile_of(width, 512)

    def kernel(value_ref, out):
        out[...] = value_ref[...].T

    return call(
        kernel,
        "transposed",
        (width // tile,),
        [],
        [value],
        [pl.BlockSpec((count, tile), lambda i: (0, i))],
        pl.BlockSpec((tile, count), lambda i: (i, 0)),
        jax.ShapeDtypeStruct((width, count), value.dtype),
        vmem=SMALL_VMEM,
    )


def from_peer(value, by):
    peers = lax.axis_size("mp")
    return lax.ppermute(value, "mp", [(i, i ^ by) for i in range(peers)])


def across_sections(value):
    return lax.ppermute(value, "section", [(0, 1), (1, 0)])


def local(tokens, weights, gain, cotangent):
    section = lax.axis_index("section").astype(jnp.int32).reshape(1)
    first = 1 - section
    weight = weights[0]
    peers = lax.axis_size("mp")
    line = lax.axis_size("dp")
    half = line // 2
    place = lax.axis_index("dp")
    rows = tokens.shape[0]
    each = peers // 4
    parts = 4 if weight.shape[1] % 1024 == 0 else 3

    last = []

    def run(work, anchor, *others):
        if last:
            held = last[-1]
            anchor, held["value"] = lax.optimization_barrier((anchor, held["value"]))
        held = {"value": work(anchor, *others)}
        last.append(held)
        return held

    receives = {
        hop: jnp.logical_or(place == hop, place == line - 1 - hop).astype(jnp.int32).reshape(1)
        for hop in range(half - 1)
    }
    tokens, section, first, receives = lax.optimization_barrier((tokens, section, first, receives))

    raw = run(lambda a, b: jnp.where(first[0] == 1, a, b), tokens, cotangent)["value"]
    across = peers // 2
    near = list(range(each, 2 * each)) + list(range(each))
    far = [by ^ across for by in near]
    gathered = {by: from_peer(raw, by) if by else raw for by in near}

    values = tokens.astype(jnp.float32)
    row_total, row_squares = lax.psum((jnp.sum(values, 1), jnp.sum(values * values, 1)), "dp")
    average = row_total / D
    inverse_std = lax.rsqrt(row_squares / D - average * average + epsilon)
    own_scale = jnp.stack([average, inverse_std], 1)
    near_scale = jnp.concatenate([from_peer(own_scale, by) if by else own_scale for by in near], 0)
    gathered[across] = from_peer(raw, across)
    gathered, near_scale = lax.optimization_barrier((gathered, near_scale))
    gathered.update({by: from_peer(gathered[by ^ across], across) for by in far if by != across})
    far_scale = from_peer(near_scale, across)

    def prepare(members, scale, group, into):
        blocks = [gathered[by] for by in members]
        return run(lambda g: normalize(first, blocks, scale, g, group, into), gain)["value"]

    chunks = {}

    def multiply(value, part, groups):
        products = run(lambda s: up_product(s, value, weight, part, parts, groups), section)
        for i, group in enumerate(groups):
            chunks[part, group] = {"products": products, "mine": i, "theirs": len(groups) + i}

    def stack(chunk):
        products = chunk["products"]
        arrived = across_sections(products["value"][chunk["theirs"]])
        chunk["sum"] = run(stacked, products["value"][chunk["mine"]], arrived)

    def inward(chunk):
        for hop in range(half - 1):
            value = chunk["sum"]["value"]
            arrived = lax.ppermute(value, "dp", [(hop, hop + 1), (line - 1 - hop, line - 2 - hop)])
            chunk["sum"] = run(added, value, arrived)

    def middle(chunk):
        value = chunk["sum"]["value"]
        arrived = lax.ppermute(value, "dp", [(half - 1, half), (half, half - 1)])
        chunk["result"] = run(lambda a, b: activated(first, a, b), value, arrived)

    def outward(chunk):
        for hop in reversed(range(half - 1)):
            value = chunk["result"]["value"]
            arrived = lax.ppermute(value, "dp", [(hop + 1, hop), (line - 2 - hop, line - 1 - hop)])
            if hop:
                chunk["result"] = run(lambda a, b: chosen(receives[hop], a, b, False)[0], value, arrived)
            else:
                chunk["halves"] = run(lambda a, b: chosen(receives[hop], a, b, True), value, arrived)

    def hidden(part, groups):
        kept = [chunks[part, g]["halves"]["value"][0] for g in groups]
        for g in groups:
            if "came" not in chunks[part, g]:
                chunks[part, g]["came"] = across_sections(chunks[part, g]["halves"]["value"][1])
        return kept, [chunks[part, g]["came"] for g in groups]

    both = (FAR, NEAR)
    order = [(0, NEAR)] + [(part, FAR) for part in range(parts)] + [(part, NEAR) for part in range(1, parts)]
    count = len(order)
    held = {"gradient": None}

    def need(c):
        if c < count and order[c] not in chunks:
            part, group = order[c]
            multiply(x_all, part, [group] if part < 2 else both)

    def tick(t):
        if 0 <= t - 1 < count:
            middle(chunks[order[t - 1]])
        if 0 <= t - 2 < count:
            outward(chunks[order[t - 2]])
        if 2 <= t + 2 < count:
            stack(chunks[order[t + 2]])

    def go_down(part, groups, before, column, kinds=(), arrived=()):
        kept, came = hidden(part, groups)
        before = None if before is None else before["value"][0]
        return run(
            lambda k: down_product(section, [k] + kept[1:], came, weight, part, parts, before, column, arrived, kinds),
            kept[0],
        )

    def go_gradient(part):
        kept, came = hidden(part, both)
        into = None if held["gradient"] is None else held["gradient"]["value"]
        held["gradient"] = run(
            lambda k: weight_gradient(section, turned, [k] + kept[1:], came, part, parts, into), kept[0]
        )

    x_near = prepare(near, near_scale, NEAR, None)
    multiply(x_near, 0, [NEAR])
    stack(chunks[order[0]])
    multiply(x_near, 1, [NEAR])
    x_all = prepare(far, far_scale, FAR, x_near)
    multiply(x_all, 0, [FAR])
    inward(chunks[order[0]])
    stack(chunks[order[1]])
    need(2)
    for t in range(count + 2):
        if 0 < t < count:
            inward(chunks[order[t]])
        tick(t)
        need(t + 3)
        far_part, near_part = t - 3, t - 2 - parts
        if far_part == 0:
            turned = run(transposed, x_all)["value"]
            near_sum = far_sum = go_down(0, both, None, 0)
        elif 0 < far_part < parts - 1:
            far_sum = go_down(far_part, [FAR], far_sum, FAR if far_part == 1 else 0)
        elif far_part == parts - 1:
            sent_far = go_down(far_part, [FAR], far_sum, 0, [jnp.bfloat16] * 2)
            arrived = [from_peer(value, across) for value in sent_far["value"]]
            go_gradient(0)
        elif 0 < near_part < parts - 1:
            near_sum = go_down(near_part, [NEAR], near_sum, NEAR if near_part == 1 else 0)
        if t == count:
            go_gradient(1)
        if t >= count - 1 and t <= count:
            k = t - count + 1
            last[-1]["value"], arrived[k] = lax.optimization_barrier((last[-1]["value"], arrived[k]))
    sent_near = go_down(parts - 1, [NEAR], near_sum, 0, [jnp.bfloat16, jnp.float32], arrived)
    for part in range(2, parts):
        go_gradient(part)

    own = sent_near["value"][1]
    blocks = {0: own.astype(jnp.bfloat16), 1: sent_near["value"][0]}
    result = own[:rows]
    for by in range(1, across):
        at = (by % each) * rows
        result = result + from_peer(blocks[by // each][at : at + rows], by).astype(jnp.float32)
    return (result.astype(jnp.bfloat16)[None], held["gradient"]["value"][None])


def solution(mesh):
    placed = (P("mp", "dp"), P("section", "dp", "mp"), P("dp"), P("mp", "dp"))
    return jax.shard_map(
        local,
        mesh=mesh,
        in_specs=placed,
        out_specs=(P("section", "mp", "dp"), P("section", "dp", "mp")),
        check_vma=False,
    )
```

```python
import jax
import jax.numpy as jnp
from jax import lax
from jax.experimental import pallas as pl
from jax.experimental.pallas import tpu as pltpu
from jax.sharding import PartitionSpec as P

D = 12288
MATMUL_VMEM = 22 * 1024 * 1024
SMALL_VMEM = 8 * 1024 * 1024
FAR, NEAR = 0, 1


epsilon = 1e-05


def dot_f32(left, right, contract):
    return lax.dot_general(
        left, right, ((contract[:1], contract[1:]), ((), ())), preferred_element_type=jnp.float32
    )


def tile_of(extent, limit):
    return max(t for t in range(128, limit + 1, 128) if extent % t == 0)


def fixed(shape, index):
    return pl.BlockSpec(shape, lambda *_: index, pipeline_mode=pl.Buffered(1))


def call(kernel, name, grid, scalars, operands, in_specs, out_specs, out_shape, scratch=(), aliases={}, vmem=MATMUL_VMEM):
    return pl.pallas_call(
        kernel,
        grid_spec=pltpu.PrefetchScalarGridSpec(
            num_scalar_prefetch=len(scalars),
            grid=grid,
            in_specs=in_specs,
            out_specs=out_specs,
            scratch_shapes=list(scratch),
        ),
        out_shape=out_shape,
        input_output_aliases=aliases,
        compiler_params=pltpu.CompilerParams(vmem_limit_bytes=vmem),
        name=name,
    )(*scalars, *operands)


def normalize(first, blocks, scale, gain, group, into):
    rows, width = blocks[0].shape
    count = rows * len(blocks)
    tile = tile_of(width, 768)

    def kernel(first_ref, gain_ref, scale_ref, *refs):
        out = refs[-1]
        for i in range(len(blocks)):
            own = slice(i * rows, (i + 1) * rows)
            value = refs[i][...].astype(jnp.float32)
            centred = (value - scale_ref[own, 0:1]) * scale_ref[own, 1:2]
            normed = (centred * gain_ref[...]).astype(jnp.bfloat16)
            out[own, :] = jnp.where(first_ref[0] == 1, normed, refs[i][...])

    column = lambda i, _: (0, i)
    extra = [] if into is None else [into]
    return call(
        kernel,
        "normalize",
        (width // tile,),
        [first],
        [gain.reshape(1, width), scale, *blocks, *extra],
        [pl.BlockSpec((1, tile), column), fixed((count, 2), (0, 0))]
        + [pl.BlockSpec((rows, tile), column)] * len(blocks)
        + [pl.BlockSpec(memory_space=pl.ANY)] * len(extra),
        pl.BlockSpec((count, tile), lambda i, _: (group, i)),
        jax.ShapeDtypeStruct((2 * count, width), jnp.bfloat16),
        aliases={3 + len(blocks): 0} if extra else {},
        vmem=SMALL_VMEM,
    )


def up_product(section, rows, weight, part, parts, groups):
    pieces = len(groups)
    count, width = rows.shape[0] // 2 * pieces, rows.shape[1]
    at = groups[0]
    columns = weight.shape[1] // parts
    tile = tile_of(columns // 2, 768)
    steps = columns // tile
    mine = steps // 2
    piece = count // pieces

    def kernel(section_ref, rows_ref, weight_ref, *results):
        product = dot_f32(rows_ref[...], weight_ref[...], (1, 0)).astype(jnp.bfloat16)

        def store(refs):
            for i, result in enumerate(refs):
                result[...] = product[i * piece : (i + 1) * piece]

        pl.when(pl.program_id(0) < mine)(lambda: store(results[:pieces]))
        pl.when(pl.program_id(0) >= mine)(lambda: store(results[pieces:]))

    return call(
        kernel,
        "up_product",
        (steps,),
        [section],
        [rows, weight],
        [
            fixed((count, width), (at, 0)),
            pl.BlockSpec((width, tile), lambda i, s: (0, part * steps + lax.rem(i + s[0] * mine, steps))),
        ],
        [pl.BlockSpec((piece, tile), lambda i, s: (0, jnp.minimum(i, mine - 1)))] * pieces
        + [pl.BlockSpec((piece, tile), lambda i, s: (0, jnp.maximum(i - mine, 0)))] * pieces,
        [jax.ShapeDtypeStruct((piece, columns // 2), jnp.bfloat16)] * (2 * pieces),
    )


def elementwise(body, name, scalars, operands, out_rows):
    columns = operands[0].shape[1]
    tile = tile_of(columns, 256)
    column = lambda i, *_: (0, i)

    def kernel(*refs):
        scalar_refs = refs[: len(scalars)]
        ins = refs[len(scalars) : len(scalars) + len(operands)]
        outs = refs[len(scalars) + len(operands) :]
        for out, value in zip(outs, body(scalar_refs, ins)):
            out[...] = value

    return call(
        kernel,
        name,
        (columns // tile,),
        scalars,
        operands,
        [pl.BlockSpec((o.shape[0], tile), column) for o in operands],
        [pl.BlockSpec((r, tile), column) for r in out_rows],
        [jax.ShapeDtypeStruct((r, columns), jnp.bfloat16) for r in out_rows],
        vmem=SMALL_VMEM,
    )


def stacked(mine, arrived):
    rows = mine.shape[0]
    body = lambda _, ins: (jnp.concatenate([ins[0][...], ins[1][...]], 0),)
    return elementwise(body, "stacked", [], [mine, arrived], [2 * rows])[0]


def added(value, arrived):
    def body(_, ins):
        total = ins[0][...].astype(jnp.float32) + ins[1][...].astype(jnp.float32)
        return (total.astype(jnp.bfloat16),)

    return elementwise(body, "added", [], [value, arrived], [value.shape[0]])[0]


def activated(first, value, arrived):
    rows = value.shape[0] // 2

    def body(scalars, ins):
        is_first = scalars[0][0] == 1
        total = ins[0][...].astype(jnp.float32) + ins[1][...].astype(jnp.float32)
        above, below = total[:rows], total[rows:]
        v = jnp.where(is_first, above, below)
        grad = jnp.where(is_first, below, above)
        c = 0.7978845608028654
        t = jnp.tanh(c * (v + 0.044715 * (v * v * v)))
        hidden = (0.5 * v * (1.0 + t)).astype(jnp.bfloat16)
        slope = 0.5 * (1.0 + t) + 0.5 * v * (1.0 - t * t) * (c * (1.0 + 3.0 * 0.044715 * (v * v)))
        grad_preact = (grad * slope).astype(jnp.bfloat16)
        kept = jnp.where(is_first, grad_preact, hidden)
        sent = jnp.where(is_first, hidden, grad_preact)
        return (jnp.concatenate([kept, sent], 0),)

    return elementwise(body, "activated", [first], [value, arrived], [2 * rows])[0]


def chosen(receives, value, arrived, halves):
    rows = value.shape[0]

    def body(scalars, ins):
        result = jnp.where(scalars[0][0] == 1, ins[1][...], ins[0][...])
        return (result[: rows // 2], result[rows // 2 :]) if halves else (result,)

    out_rows = [rows // 2] * 2 if halves else [rows]
    return elementwise(body, "chosen", [receives], [value, arrived], out_rows)


def down_product(section, kept, came, weight, part, parts, before, group, arrived, kinds):
    counts = [k.shape[0] for k in kept]
    count, half = sum(counts), kept[0].shape[1]
    width = weight.shape[0]
    tile = tile_of(width, 1024)
    n = len(kept)
    extra = [] if before is None else [before]
    others = list(arrived)

    def kernel(section_ref, *refs):
        weight_ref = refs[2 * n]
        added = refs[2 * n + 1 : 2 * n + 1 + len(extra)]
        arrived_refs = refs[2 * n + 1 + len(extra) : 2 * n + 1 + len(extra) + len(others)]
        results = refs[2 * n + 1 + len(extra) + len(others) : -1]
        held = refs[-1]

        @pl.when(pl.program_id(0) == 0)
        def _():
            mine = pl.ds(pl.multiple_of(section_ref[0] * half, half), half)
            theirs = pl.ds(pl.multiple_of((1 - section_ref[0]) * half, half), half)
            at = 0
            for i, rows in enumerate(counts):
                held[mine, at : at + rows] = refs[i][...].T
                held[theirs, at : at + rows] = refs[n + i][...].T
                at += rows

        product = dot_f32(weight_ref[...], held[...], (1, 0))
        for ref in added:
            product = product + ref[...]
        if kinds:
            product = product.T
            piece = count // len(kinds)
            for i, result in enumerate(results):
                value = product[i * piece : (i + 1) * piece]
                if others:
                    value = value + arrived_refs[i][...].astype(jnp.float32)
                result[...] = value.astype(result.dtype)
        else:
            results[0][...] = product

    whole = [fixed((rows, half), (0, 0)) for rows in counts]
    if kinds:
        out_specs = [pl.BlockSpec((count // len(kinds), tile), lambda i, s: (0, i))] * len(kinds)
        out_shape = [jax.ShapeDtypeStruct((count // len(kinds), width), kind) for kind in kinds]
    else:
        out_specs = [pl.BlockSpec((tile, count), lambda i, s: (i, 0))]
        out_shape = [jax.ShapeDtypeStruct((width, count), jnp.float32)]
    return call(
        kernel,
        "down_product",
        (width // tile,),
        [section],
        [*kept, *came, weight, *extra, *others],
        whole
        + whole
        + [pl.BlockSpec((tile, 2 * half), lambda i, s: (i, part))]
        + [pl.BlockSpec((tile, count), lambda i, s: (i, group))] * len(extra)
        + [pl.BlockSpec((count // max(len(kinds), 1), tile), lambda i, s: (0, i))] * len(others),
        out_specs,
        out_shape,
        [pltpu.VMEM((2 * half, count), jnp.bfloat16)],
    )


def weight_gradient(section, turned, kept, came, part, parts, into):
    width, count = turned.shape
    counts = [k.shape[0] for k in kept]
    half = kept[0].shape[1]
    tile = tile_of(width, 1024)
    step = half
    n = len(kept)

    def kernel(section_ref, turned_ref, *refs):
        out, held = refs[-2:]

        @pl.when(pl.program_id(0) == 0)
        def _():
            mine = pl.ds(pl.multiple_of(section_ref[0] * half, half), half)
            theirs = pl.ds(pl.multiple_of((1 - section_ref[0]) * half, half), half)
            at = 0
            for i, rows in enumerate(counts):
                held[at : at + rows, mine] = refs[i][...]
                held[at : at + rows, theirs] = refs[n + i][...]
                at += rows

        for at in range(0, 2 * half, step):
            own = slice(at, at + step)
            out[:, own] = dot_f32(turned_ref[...], held[:, own], (1, 0)).astype(jnp.bfloat16)

    whole = [fixed((rows, half), (0, 0)) for rows in counts]
    extra = [] if into is None else [into]
    return call(
        kernel,
        "weight_gradient",
        (width // tile,),
        [section],
        [turned, *kept, *came, *extra],
        [pl.BlockSpec((tile, count), lambda i, s: (i, 0))]
        + whole
        + whole
        + [pl.BlockSpec(memory_space=pl.ANY)] * len(extra),
        pl.BlockSpec((tile, 2 * half), lambda i, s: (i, part)),
        jax.ShapeDtypeStruct((width, 2 * half * parts), jnp.bfloat16),
        [pltpu.VMEM((count, 2 * half), jnp.bfloat16)],
        {2 + 2 * n: 0} if extra else {},
    )


def transposed(value):
    count, width = value.shape
    tile = tile_of(width, 512)

    def kernel(value_ref, out):
        out[...] = value_ref[...].T

    return call(
        kernel,
        "transposed",
        (width // tile,),
        [],
        [value],
        [pl.BlockSpec((count, tile), lambda i: (0, i))],
        pl.BlockSpec((tile, count), lambda i: (i, 0)),
        jax.ShapeDtypeStruct((width, count), value.dtype),
        vmem=SMALL_VMEM,
    )


def from_peer(value, by):
    peers = lax.axis_size("mp")
    return lax.ppermute(value, "mp", [(i, i ^ by) for i in range(peers)])


def across_sections(value):
    return lax.ppermute(value, "section", [(0, 1), (1, 0)])


def local(tokens, weights, gain, cotangent):
    section = lax.axis_index("section").astype(jnp.int32).reshape(1)
    first = 1 - section
    weight = weights[0]
    peers = lax.axis_size("mp")
    line = lax.axis_size("dp")
    half = line // 2
    place = lax.axis_index("dp")
    rows = tokens.shape[0]
    each = peers // 4
    parts = 4 if weight.shape[1] % 1024 == 0 else 3

    last = []

    def run(work, anchor, *others):
        if last:
            held = last[-1]
            anchor, held["value"] = lax.optimization_barrier((anchor, held["value"]))
        held = {"value": work(anchor, *others)}
        last.append(held)
        return held

    receives = {
        hop: jnp.logical_or(place == hop, place == line - 1 - hop).astype(jnp.int32).reshape(1)
        for hop in range(half - 1)
    }
    tokens, section, first, receives = lax.optimization_barrier((tokens, section, first, receives))

    raw = run(lambda a, b: jnp.where(first[0] == 1, a, b), tokens, cotangent)["value"]
    across = peers // 2
    near = list(range(each, 2 * each)) + list(range(each))
    far = [by ^ across for by in near]
    gathered = {by: from_peer(raw, by) if by else raw for by in near}

    values = tokens.astype(jnp.float32)
    row_total, row_squares = lax.psum((jnp.sum(values, 1), jnp.sum(values * values, 1)), "dp")
    average = row_total / D
    inverse_std = lax.rsqrt(row_squares / D - average * average + epsilon)
    own_scale = jnp.stack([average, inverse_std], 1)
    near_scale = jnp.concatenate([from_peer(own_scale, by) if by else own_scale for by in near], 0)
    gathered[across] = from_peer(raw, across)
    gathered, near_scale = lax.optimization_barrier((gathered, near_scale))
    gathered.update({by: from_peer(gathered[by ^ across], across) for by in far if by != across})
    far_scale = from_peer(near_scale, across)

    def prepare(members, scale, group, into):
        blocks = [gathered[by] for by in members]
        return run(lambda g: normalize(first, blocks, scale, g, group, into), gain)["value"]

    chunks = {}

    def multiply(value, part, groups):
        products = run(lambda s: up_product(s, value, weight, part, parts, groups), section)
        for i, group in enumerate(groups):
            chunks[part, group] = {"products": products, "mine": i, "theirs": len(groups) + i}

    def stack(chunk):
        products = chunk["products"]
        arrived = across_sections(products["value"][chunk["theirs"]])
        chunk["sum"] = run(stacked, products["value"][chunk["mine"]], arrived)

    def inward(chunk):
        for hop in range(half - 1):
            value = chunk["sum"]["value"]
            arrived = lax.ppermute(value, "dp", [(hop, hop + 1), (line - 1 - hop, line - 2 - hop)])
            chunk["sum"] = run(added, value, arrived)

    def middle(chunk):
        value = chunk["sum"]["value"]
        arrived = lax.ppermute(value, "dp", [(half - 1, half), (half, half - 1)])
        chunk["result"] = run(lambda a, b: activated(first, a, b), value, arrived)

    def outward(chunk):
        for hop in reversed(range(half - 1)):
            value = chunk["result"]["value"]
            arrived = lax.ppermute(value, "dp", [(hop + 1, hop), (line - 2 - hop, line - 1 - hop)])
            if hop:
                chunk["result"] = run(lambda a, b: chosen(receives[hop], a, b, False)[0], value, arrived)
            else:
                chunk["halves"] = run(lambda a, b: chosen(receives[hop], a, b, True), value, arrived)

    def hidden(part, groups):
        kept = [chunks[part, g]["halves"]["value"][0] for g in groups]
        for g in groups:
            if "came" not in chunks[part, g]:
                chunks[part, g]["came"] = across_sections(chunks[part, g]["halves"]["value"][1])
        return kept, [chunks[part, g]["came"] for g in groups]

    both = (FAR, NEAR)
    order = [(0, NEAR)] + [(part, FAR) for part in range(parts)] + [(part, NEAR) for part in range(1, parts)]
    count = len(order)
    held = {"gradient": None}

    def need(c):
        if c < count and order[c] not in chunks:
            part, group = order[c]
            multiply(x_all, part, [group] if part < 2 else both)

    def tick(t):
        if 0 <= t - 1 < count:
            middle(chunks[order[t - 1]])
        if 0 <= t - 2 < count:
            outward(chunks[order[t - 2]])
        if 2 <= t + 2 < count:
            stack(chunks[order[t + 2]])

    def go_down(part, groups, before, column, kinds=(), arrived=()):
        kept, came = hidden(part, groups)
        before = None if before is None else before["value"][0]
        return run(
            lambda k: down_product(section, [k] + kept[1:], came, weight, part, parts, before, column, arrived, kinds),
            kept[0],
        )

    def go_gradient(part):
        kept, came = hidden(part, both)
        into = None if held["gradient"] is None else held["gradient"]["value"]
        held["gradient"] = run(
            lambda k: weight_gradient(section, turned, [k] + kept[1:], came, part, parts, into), kept[0]
        )

    x_near = prepare(near, near_scale, NEAR, None)
    multiply(x_near, 0, [NEAR])
    stack(chunks[order[0]])
    multiply(x_near, 1, [NEAR])
    x_all = prepare(far, far_scale, FAR, x_near)
    multiply(x_all, 0, [FAR])
    inward(chunks[order[0]])
    stack(chunks[order[1]])
    need(2)
    for t in range(count + 2):
        if 0 < t < count:
            inward(chunks[order[t]])
        tick(t)
        need(t + 3)
        far_part, near_part = t - 3, t - 2 - parts
        if t == 1:
            turned = run(transposed, x_all)["value"]
        if far_part == 0:
            near_sum = far_sum = go_down(0, both, None, 0)
        elif 0 < far_part < parts - 1:
            far_sum = go_down(far_part, [FAR], far_sum, FAR if far_part == 1 else 0)
        elif far_part == parts - 1:
            sent_far = go_down(far_part, [FAR], far_sum, 0, [jnp.bfloat16] * 2)
            arrived = [from_peer(value, across) for value in sent_far["value"]]
        elif 0 < near_part < parts - 1:
            near_sum = go_down(near_part, [NEAR], near_sum, NEAR if near_part == 1 else 0)
        if t >= count - 1 and t <= count:
            go_gradient(t - count + 1)
        if t >= count - 1 and t <= count:
            k = t - count + 1
            last[-1]["value"], arrived[k] = lax.optimization_barrier((last[-1]["value"], arrived[k]))
    sent_near = go_down(parts - 1, [NEAR], near_sum, 0, [jnp.bfloat16, jnp.float32], arrived)
    for part in range(2, parts):
        go_gradient(part)

    own = sent_near["value"][1]
    blocks = {0: own.astype(jnp.bfloat16), 1: sent_near["value"][0]}
    result = own[:rows]
    for by in range(1, across):
        at = (by % each) * rows
        result = result + from_peer(blocks[by // each][at : at + rows], by).astype(jnp.float32)
    return (result.astype(jnp.bfloat16)[None], held["gradient"]["value"][None])


def solution(mesh):
    placed = (P("mp", "dp"), P("section", "dp", "mp"), P("dp"), P("mp", "dp"))
    return jax.shard_map(
        local,
        mesh=mesh,
        in_specs=placed,
        out_specs=(P("section", "mp", "dp"), P("section", "dp", "mp")),
        check_vma=False,
    )
```

```python
import jax
import jax.numpy as jnp
from jax import lax
from jax.experimental import pallas as pl
from jax.experimental.pallas import tpu as pltpu
from jax.sharding import PartitionSpec as P

D = 12288
MATMUL_VMEM = 22 * 1024 * 1024
SMALL_VMEM = 8 * 1024 * 1024
FAR, NEAR = 0, 1


epsilon = 1e-05


def dot_f32(left, right, contract):
    return lax.dot_general(
        left, right, ((contract[:1], contract[1:]), ((), ())), preferred_element_type=jnp.float32
    )


def tile_of(extent, limit):
    return max(t for t in range(128, limit + 1, 128) if extent % t == 0)


def fixed(shape, index):
    return pl.BlockSpec(shape, lambda *_: index, pipeline_mode=pl.Buffered(1))


def call(kernel, name, grid, scalars, operands, in_specs, out_specs, out_shape, scratch=(), aliases={}, vmem=MATMUL_VMEM):
    return pl.pallas_call(
        kernel,
        grid_spec=pltpu.PrefetchScalarGridSpec(
            num_scalar_prefetch=len(scalars),
            grid=grid,
            in_specs=in_specs,
            out_specs=out_specs,
            scratch_shapes=list(scratch),
        ),
        out_shape=out_shape,
        input_output_aliases=aliases,
        compiler_params=pltpu.CompilerParams(vmem_limit_bytes=vmem),
        name=name,
    )(*scalars, *operands)


def normalize(first, blocks, scale, gain, group, into):
    rows, width = blocks[0].shape
    count = rows * len(blocks)
    tile = tile_of(width, 768)

    def kernel(first_ref, gain_ref, scale_ref, *refs):
        out = refs[-1]
        for i in range(len(blocks)):
            own = slice(i * rows, (i + 1) * rows)
            value = refs[i][...].astype(jnp.float32)
            centred = (value - scale_ref[own, 0:1]) * scale_ref[own, 1:2]
            normed = (centred * gain_ref[...]).astype(jnp.bfloat16)
            out[own, :] = jnp.where(first_ref[0] == 1, normed, refs[i][...])

    column = lambda i, _: (0, i)
    extra = [] if into is None else [into]
    return call(
        kernel,
        "normalize",
        (width // tile,),
        [first],
        [gain.reshape(1, width), scale, *blocks, *extra],
        [pl.BlockSpec((1, tile), column), fixed((count, 2), (0, 0))]
        + [pl.BlockSpec((rows, tile), column)] * len(blocks)
        + [pl.BlockSpec(memory_space=pl.ANY)] * len(extra),
        pl.BlockSpec((count, tile), lambda i, _: (group, i)),
        jax.ShapeDtypeStruct((2 * count, width), jnp.bfloat16),
        aliases={3 + len(blocks): 0} if extra else {},
        vmem=SMALL_VMEM,
    )


def up_product(section, rows, weight, part, parts, groups):
    pieces = len(groups)
    count, width = rows.shape[0] // 2 * pieces, rows.shape[1]
    at = groups[0]
    columns = weight.shape[1] // parts
    tile = tile_of(columns // 2, 768)
    steps = columns // tile
    mine = steps // 2
    piece = count // pieces

    def kernel(section_ref, rows_ref, weight_ref, *results):
        product = dot_f32(rows_ref[...], weight_ref[...], (1, 0)).astype(jnp.bfloat16)

        def store(refs):
            for i, result in enumerate(refs):
                result[...] = product[i * piece : (i + 1) * piece]

        pl.when(pl.program_id(0) < mine)(lambda: store(results[:pieces]))
        pl.when(pl.program_id(0) >= mine)(lambda: store(results[pieces:]))

    return call(
        kernel,
        "up_product",
        (steps,),
        [section],
        [rows, weight],
        [
            fixed((count, width), (at, 0)),
            pl.BlockSpec((width, tile), lambda i, s: (0, part * steps + lax.rem(i + s[0] * mine, steps))),
        ],
        [pl.BlockSpec((piece, tile), lambda i, s: (0, jnp.minimum(i, mine - 1)))] * pieces
        + [pl.BlockSpec((piece, tile), lambda i, s: (0, jnp.maximum(i - mine, 0)))] * pieces,
        [jax.ShapeDtypeStruct((piece, columns // 2), jnp.bfloat16)] * (2 * pieces),
    )


def elementwise(body, name, scalars, operands, out_rows):
    columns = operands[0].shape[1]
    tile = tile_of(columns, 256)
    column = lambda i, *_: (0, i)

    def kernel(*refs):
        scalar_refs = refs[: len(scalars)]
        ins = refs[len(scalars) : len(scalars) + len(operands)]
        outs = refs[len(scalars) + len(operands) :]
        for out, value in zip(outs, body(scalar_refs, ins)):
            out[...] = value

    return call(
        kernel,
        name,
        (columns // tile,),
        scalars,
        operands,
        [pl.BlockSpec((o.shape[0], tile), column) for o in operands],
        [pl.BlockSpec((r, tile), column) for r in out_rows],
        [jax.ShapeDtypeStruct((r, columns), jnp.bfloat16) for r in out_rows],
        vmem=SMALL_VMEM,
    )


def stacked(mine, arrived):
    rows = mine.shape[0]
    body = lambda _, ins: (jnp.concatenate([ins[0][...], ins[1][...]], 0),)
    return elementwise(body, "stacked", [], [mine, arrived], [2 * rows])[0]


def added(value, arrived):
    def body(_, ins):
        total = ins[0][...].astype(jnp.float32) + ins[1][...].astype(jnp.float32)
        return (total.astype(jnp.bfloat16),)

    return elementwise(body, "added", [], [value, arrived], [value.shape[0]])[0]


def activated(first, value, arrived):
    rows = value.shape[0] // 2

    def body(scalars, ins):
        is_first = scalars[0][0] == 1
        total = ins[0][...].astype(jnp.float32) + ins[1][...].astype(jnp.float32)
        above, below = total[:rows], total[rows:]
        v = jnp.where(is_first, above, below)
        grad = jnp.where(is_first, below, above)
        c = 0.7978845608028654
        t = jnp.tanh(c * (v + 0.044715 * (v * v * v)))
        hidden = (0.5 * v * (1.0 + t)).astype(jnp.bfloat16)
        slope = 0.5 * (1.0 + t) + 0.5 * v * (1.0 - t * t) * (c * (1.0 + 3.0 * 0.044715 * (v * v)))
        grad_preact = (grad * slope).astype(jnp.bfloat16)
        kept = jnp.where(is_first, grad_preact, hidden)
        sent = jnp.where(is_first, hidden, grad_preact)
        return (jnp.concatenate([kept, sent], 0),)

    return elementwise(body, "activated", [first], [value, arrived], [2 * rows])[0]


def chosen(receives, value, arrived, halves):
    rows = value.shape[0]

    def body(scalars, ins):
        result = jnp.where(scalars[0][0] == 1, ins[1][...], ins[0][...])
        return (result[: rows // 2], result[rows // 2 :]) if halves else (result,)

    out_rows = [rows // 2] * 2 if halves else [rows]
    return elementwise(body, "chosen", [receives], [value, arrived], out_rows)


def down_product(section, kept, came, weight, part, parts, before, group, arrived, kinds):
    counts = [k.shape[0] for k in kept]
    count, half = sum(counts), kept[0].shape[1]
    width = weight.shape[0]
    tile = tile_of(width, 1024)
    n = len(kept)
    extra = [] if before is None else [before]
    others = list(arrived)

    def kernel(section_ref, *refs):
        weight_ref = refs[2 * n]
        added = refs[2 * n + 1 : 2 * n + 1 + len(extra)]
        arrived_refs = refs[2 * n + 1 + len(extra) : 2 * n + 1 + len(extra) + len(others)]
        results = refs[2 * n + 1 + len(extra) + len(others) : -1]
        held = refs[-1]

        @pl.when(pl.program_id(0) == 0)
        def _():
            mine = pl.ds(pl.multiple_of(section_ref[0] * half, half), half)
            theirs = pl.ds(pl.multiple_of((1 - section_ref[0]) * half, half), half)
            at = 0
            for i, rows in enumerate(counts):
                held[mine, at : at + rows] = refs[i][...].T
                held[theirs, at : at + rows] = refs[n + i][...].T
                at += rows

        product = dot_f32(weight_ref[...], held[...], (1, 0))
        for ref in added:
            product = product + ref[...]
        if kinds:
            product = product.T
            piece = count // len(kinds)
            for i, result in enumerate(results):
                value = product[i * piece : (i + 1) * piece]
                if others:
                    value = value + arrived_refs[i][...].astype(jnp.float32)
                result[...] = value.astype(result.dtype)
        else:
            results[0][...] = product

    whole = [fixed((rows, half), (0, 0)) for rows in counts]
    if kinds:
        out_specs = [pl.BlockSpec((count // len(kinds), tile), lambda i, s: (0, i))] * len(kinds)
        out_shape = [jax.ShapeDtypeStruct((count // len(kinds), width), kind) for kind in kinds]
    else:
        out_specs = [pl.BlockSpec((tile, count), lambda i, s: (i, 0))]
        out_shape = [jax.ShapeDtypeStruct((width, count), jnp.float32)]
    return call(
        kernel,
        "down_product",
        (width // tile,),
        [section],
        [*kept, *came, weight, *extra, *others],
        whole
        + whole
        + [pl.BlockSpec((tile, 2 * half), lambda i, s: (i, part))]
        + [pl.BlockSpec((tile, count), lambda i, s: (i, group))] * len(extra)
        + [pl.BlockSpec((count // max(len(kinds), 1), tile), lambda i, s: (0, i))] * len(others),
        out_specs,
        out_shape,
        [pltpu.VMEM((2 * half, count), jnp.bfloat16)],
    )


def weight_gradient(section, turned, kept, came, part, parts, into):
    width, count = turned.shape
    counts = [k.shape[0] for k in kept]
    half = kept[0].shape[1]
    tile = tile_of(width, 1024)
    step = half
    n = len(kept)

    def kernel(section_ref, turned_ref, *refs):
        out, held = refs[-2:]

        @pl.when(pl.program_id(0) == 0)
        def _():
            mine = pl.ds(pl.multiple_of(section_ref[0] * half, half), half)
            theirs = pl.ds(pl.multiple_of((1 - section_ref[0]) * half, half), half)
            at = 0
            for i, rows in enumerate(counts):
                held[at : at + rows, mine] = refs[i][...]
                held[at : at + rows, theirs] = refs[n + i][...]
                at += rows

        for at in range(0, 2 * half, step):
            own = slice(at, at + step)
            out[:, own] = dot_f32(turned_ref[...], held[:, own], (1, 0)).astype(jnp.bfloat16)

    whole = [fixed((rows, half), (0, 0)) for rows in counts]
    extra = [] if into is None else [into]
    return call(
        kernel,
        "weight_gradient",
        (width // tile,),
        [section],
        [turned, *kept, *came, *extra],
        [pl.BlockSpec((tile, count), lambda i, s: (i, 0))]
        + whole
        + whole
        + [pl.BlockSpec(memory_space=pl.ANY)] * len(extra),
        pl.BlockSpec((tile, 2 * half), lambda i, s: (i, part)),
        jax.ShapeDtypeStruct((width, 2 * half * parts), jnp.bfloat16),
        [pltpu.VMEM((count, 2 * half), jnp.bfloat16)],
        {2 + 2 * n: 0} if extra else {},
    )


def transposed(value):
    count, width = value.shape
    tile = tile_of(width, 512)

    def kernel(value_ref, out):
        out[...] = value_ref[...].T

    return call(
        kernel,
        "transposed",
        (width // tile,),
        [],
        [value],
        [pl.BlockSpec((count, tile), lambda i: (0, i))],
        pl.BlockSpec((tile, count), lambda i: (i, 0)),
        jax.ShapeDtypeStruct((width, count), value.dtype),
        vmem=SMALL_VMEM,
    )


def from_peer(value, by):
    peers = lax.axis_size("mp")
    return lax.ppermute(value, "mp", [(i, i ^ by) for i in range(peers)])


def across_sections(value):
    return lax.ppermute(value, "section", [(0, 1), (1, 0)])


def local(tokens, weights, gain, cotangent):
    section = lax.axis_index("section").astype(jnp.int32).reshape(1)
    first = 1 - section
    weight = weights[0]
    peers = lax.axis_size("mp")
    line = lax.axis_size("dp")
    half = line // 2
    place = lax.axis_index("dp")
    rows = tokens.shape[0]
    each = peers // 4
    parts = 4 if weight.shape[1] % 1024 == 0 else 3

    last = []

    def run(work, anchor, *others):
        if last:
            held = last[-1]
            anchor, held["value"] = lax.optimization_barrier((anchor, held["value"]))
        held = {"value": work(anchor, *others)}
        last.append(held)
        return held

    receives = {
        hop: jnp.logical_or(place == hop, place == line - 1 - hop).astype(jnp.int32).reshape(1)
        for hop in range(half - 1)
    }
    tokens, section, first, receives = lax.optimization_barrier((tokens, section, first, receives))

    raw = run(lambda a, b: jnp.where(first[0] == 1, a, b), tokens, cotangent)["value"]
    across = peers // 2
    near = list(range(each, 2 * each)) + list(range(each))
    far = [by ^ across for by in near]
    gathered = {by: from_peer(raw, by) if by else raw for by in near}

    values = tokens.astype(jnp.float32)
    row_total, row_squares = lax.psum((jnp.sum(values, 1), jnp.sum(values * values, 1)), "dp")
    average = row_total / D
    inverse_std = lax.rsqrt(row_squares / D - average * average + epsilon)
    own_scale = jnp.stack([average, inverse_std], 1)
    near_scale = jnp.concatenate([from_peer(own_scale, by) if by else own_scale for by in near], 0)
    gathered[across] = from_peer(raw, across)
    gathered, near_scale = lax.optimization_barrier((gathered, near_scale))
    gathered.update({by: from_peer(gathered[by ^ across], across) for by in far if by != across})
    far_scale = from_peer(near_scale, across)

    def prepare(members, scale, group, into):
        blocks = [gathered[by] for by in members]
        return run(lambda g: normalize(first, blocks, scale, g, group, into), gain)["value"]

    chunks = {}

    def multiply(value, part, groups):
        products = run(lambda s: up_product(s, value, weight, part, parts, groups), section)
        for i, group in enumerate(groups):
            chunks[part, group] = {"products": products, "mine": i, "theirs": len(groups) + i}

    def stack(chunk):
        products = chunk["products"]
        arrived = across_sections(products["value"][chunk["theirs"]])
        chunk["sum"] = run(stacked, products["value"][chunk["mine"]], arrived)

    def inward(chunk):
        for hop in range(half - 1):
            value = chunk["sum"]["value"]
            arrived = lax.ppermute(value, "dp", [(hop, hop + 1), (line - 1 - hop, line - 2 - hop)])
            chunk["sum"] = run(added, value, arrived)

    def middle(chunk):
        value = chunk["sum"]["value"]
        arrived = lax.ppermute(value, "dp", [(half - 1, half), (half, half - 1)])
        chunk["result"] = run(lambda a, b: activated(first, a, b), value, arrived)

    def outward(chunk):
        for hop in reversed(range(half - 1)):
            value = chunk["result"]["value"]
            arrived = lax.ppermute(value, "dp", [(hop + 1, hop), (line - 2 - hop, line - 1 - hop)])
            if hop:
                chunk["result"] = run(lambda a, b: chosen(receives[hop], a, b, False)[0], value, arrived)
            else:
                chunk["halves"] = run(lambda a, b: chosen(receives[hop], a, b, True), value, arrived)

    def hidden(part, groups):
        kept = [chunks[part, g]["halves"]["value"][0] for g in groups]
        for g in groups:
            if "came" not in chunks[part, g]:
                chunks[part, g]["came"] = across_sections(chunks[part, g]["halves"]["value"][1])
        return kept, [chunks[part, g]["came"] for g in groups]

    both = (FAR, NEAR)
    order = [(0, NEAR)] + [(part, FAR) for part in range(parts)] + [(part, NEAR) for part in range(1, parts)]
    count = len(order)
    held = {"gradient": None}

    def need(c):
        if c < count and order[c] not in chunks:
            part, group = order[c]
            multiply(x_all, part, [group] if part < 2 else both)

    def tick(t):
        if 0 <= t - 1 < count:
            middle(chunks[order[t - 1]])
        if 0 <= t - 2 < count:
            outward(chunks[order[t - 2]])
        if 2 <= t + 2 < count:
            stack(chunks[order[t + 2]])

    def go_down(part, groups, before, column, kinds=(), arrived=()):
        kept, came = hidden(part, groups)
        before = None if before is None else before["value"][0]
        return run(
            lambda k: down_product(section, [k] + kept[1:], came, weight, part, parts, before, column, arrived, kinds),
            kept[0],
        )

    def go_gradient(part):
        kept, came = hidden(part, both)
        into = None if held["gradient"] is None else held["gradient"]["value"]
        held["gradient"] = run(
            lambda k: weight_gradient(section, turned, [k] + kept[1:], came, part, parts, into), kept[0]
        )

    x_near = prepare(near, near_scale, NEAR, None)
    multiply(x_near, 0, [NEAR])
    stack(chunks[order[0]])
    multiply(x_near, 1, [NEAR])
    x_all = prepare(far, far_scale, FAR, x_near)
    multiply(x_all, 0, [FAR])
    inward(chunks[order[0]])
    stack(chunks[order[1]])
    need(2)
    for t in range(count + 2):
        if 0 < t < count:
            inward(chunks[order[t]])
        if t == 3:
            turned = run(transposed, x_all)["value"]
        tick(t)
        need(t + 3)
        far_part, near_part = t - 3, t - 2 - parts
        if far_part == 0:
            near_sum = far_sum = go_down(0, both, None, 0)
        elif 0 < far_part < parts - 1:
            far_sum = go_down(far_part, [FAR], far_sum, FAR if far_part == 1 else 0)
        elif far_part == parts - 1:
            sent_far = go_down(far_part, [FAR], far_sum, 0, [jnp.bfloat16] * 2)
            arrived = [from_peer(value, across) for value in sent_far["value"]]
        elif 0 < near_part < parts - 1:
            near_sum = go_down(near_part, [NEAR], near_sum, NEAR if near_part == 1 else 0)
        if t == count:
            go_gradient(0)
        if t >= count - 1 and t <= count:
            k = t - count + 1
            last[-1]["value"], arrived[k] = lax.optimization_barrier((last[-1]["value"], arrived[k]))
    sent_near = go_down(parts - 1, [NEAR], near_sum, 0, [jnp.bfloat16, jnp.float32], arrived)
    for part in range(1, parts):
        go_gradient(part)

    own = sent_near["value"][1]
    blocks = {0: own.astype(jnp.bfloat16), 1: sent_near["value"][0]}
    result = own[:rows]
    for by in range(1, across):
        at = (by % each) * rows
        result = result + from_peer(blocks[by // each][at : at + rows], by).astype(jnp.float32)
    return (result.astype(jnp.bfloat16)[None], held["gradient"]["value"][None])


def solution(mesh):
    placed = (P("mp", "dp"), P("section", "dp", "mp"), P("dp"), P("mp", "dp"))
    return jax.shard_map(
        local,
        mesh=mesh,
        in_specs=placed,
        out_specs=(P("section", "mp", "dp"), P("section", "dp", "mp")),
        check_vma=False,
    )
```
